256 devices in a mesh: view: 4 (over x_lo, core), tx: 2 (over x_hi), ty: 32 (over z, y).
Axes of the slice: x: 4 (x_hi: 2, x_lo: 2; x = x_hi * 2 + x_lo), y: 4, z: 8, core: 2. Of those that a mesh axis runs over, the one named last changes fastest.
Arguments:
- raw_views: float32 [4, 48, 1024, 256], P('view', None, 'ty', 'tx'), may hold values from 0.2 to 5
- psf_taps: float32 [4, 3, 31], replicated, may hold values from 0.05 to 1
- offsets: int32 [4, 2], replicated, may hold values from -8 to 8, as said below
- estimate: float32 [48, 1024, 256], P(None, 'ty', 'tx'), may hold values from 0.5 to 2
Outputs:
- deconvolved: float32 [48, 1024, 256], P(None, 'ty', 'tx')
The draws below stay inside these ranges and needn't reach their ends.
Inputs may be any that keep to these rules, and one draw needn't show every extreme that they name: `offsets`: integer registration shifts; some entry equals 8 and some equals -8.
All inputs are finite; a program needn't handle non-finite values.
Results may differ from the reference program's by a relative error of at most 0.00011.
Values sent between devices are 32-bit elements; how exact they have to be, the bound alone decides.
No kernel may reach another device: no remote copies, remote signals or barrier semaphores. Data moves between devices by JAX's collectives and lax.ppermute only.
A program may use at most 128 MiB of HBM per device.

```python
import math
import jax
import jax.numpy as jnp
from jax import lax

DEPTH = 48
TAPS = 31
HALF = 15
OMAX = 8
ITERS = 2
VIEWS = 4
NX = 1024
NY = 256


def draw_offsets(key, part):
    subkeys = jax.random.split(jax.random.fold_in(key, 7), 3)
    values = jax.random.randint(subkeys[0], (VIEWS * 2,), -OMAX, OMAX + 1)
    first_slot = jax.random.randint(subkeys[1], (), 0, VIEWS * 2)
    second_slot = (first_slot + 1 + jax.random.randint(subkeys[2], (), 0, VIEWS * 2 - 1)) % (VIEWS * 2)
    values = values.at[first_slot].set(OMAX).at[second_slot].set(-OMAX)
    return values.reshape(VIEWS, 2).astype(jnp.int32)


def level_of(own_key, dims, shards, low, largest):
    def one(axis_at, blocks):
        steps = jax.random.uniform(jax.random.fold_in(jax.random.fold_in(own_key, 6), axis_at), (blocks,), jnp.float32, low / len(shards), largest / len(shards))
        return jnp.repeat(jnp.exp(steps), dims[axis_at] // blocks).reshape((-1,) + (1,) * (len(dims) - axis_at - 1))

    factor_of = one(*shards[0])
    for cut in shards[1:]:
        factor_of = factor_of * one(*cut)
    return factor_of


def setup_inputs(seed: int = 0) -> dict:
    splits = jax.random.split(jax.random.key(seed), 5)
    raw_views = jnp.clip(jnp.exp(math.log(5.0) - 3.218876 * jax.random.uniform(splits[0], (VIEWS, DEPTH, NX, NY), jnp.float32) ** level_of(splits[0], (VIEWS, DEPTH, NX, NY), ((0, 4), (2, 32), (3, 2)), -0.2, 0.2)), 0.2, 5.0)
    psf_taps = jnp.clip(jnp.exp(jax.random.uniform(splits[1], (VIEWS, 3, TAPS), jnp.float32, math.log(0.05), math.log(1.0))), 0.05, 1.0)
    offsets = draw_offsets(jax.random.fold_in(splits[4], 71), 0)
    estimate = jnp.clip(jnp.exp(math.log(2.0) - 1.3862944 * jax.random.uniform(splits[3], (DEPTH, NX, NY), jnp.float32) ** level_of(splits[3], (DEPTH, NX, NY), ((1, 32), (2, 2)), -0.2, 0.2)), 0.5, 2.0)
    return dict(raw_views=raw_views, psf_taps=psf_taps, offsets=offsets, estimate=estimate)


highest = lax.Precision.HIGHEST


def line_blur(volume, kernel, axis_number):
    moved_axis = jnp.moveaxis(volume, axis_number, -1)
    full_shape = moved_axis.shape
    flattened = moved_axis.reshape(-1, 1, full_shape[-1])
    result = lax.conv_general_dilated(flattened, kernel.reshape(1, 1, -1), (1,), [(HALF, HALF)], precision=highest)
    return jnp.moveaxis(result.reshape(full_shape), -1, axis_number)


def apply_blur(volume, kernels, mirror):
    for axis_number in range(3):
        kernel = kernels[axis_number]
        if mirror:
            kernel = kernel[::-1]
        volume = line_blur(volume, kernel, axis_number)
    return volume


def reference(raw_views, psf_taps, offsets, estimate):
    kernels_all = psf_taps / jnp.sum(psf_taps, axis=-1, keepdims=True)
    padded = jnp.pad(raw_views, ((0, 0), (0, 0), (OMAX, OMAX), (OMAX, OMAX)))
    positions_x = jnp.arange(NX, dtype=jnp.int32)
    positions_y = jnp.arange(NY, dtype=jnp.int32)
    registered_list = []
    weight_norm = jnp.zeros((DEPTH, NX, NY), jnp.float32)
    for view_number in range(VIEWS):
        shift_x = offsets[view_number, 0].astype(jnp.int32)
        shift_y = offsets[view_number, 1].astype(jnp.int32)
        registered = lax.dynamic_slice(padded[view_number], (jnp.int32(0), (OMAX + shift_x).astype(jnp.int32), (OMAX + shift_y).astype(jnp.int32)), (DEPTH, NX, NY))
        registered_list.append(registered)
        inside_x = ((positions_x + shift_x >= 0) & (positions_x + shift_x < NX)).astype(jnp.float32)
        inside_y = ((positions_y + shift_y >= 0) & (positions_y + shift_y < NY)).astype(jnp.float32)
        valid_mask = jnp.broadcast_to(inside_x[None, :, None] * inside_y[None, None, :], (DEPTH, NX, NY))
        weight_norm = weight_norm + apply_blur(valid_mask, kernels_all[view_number], True)
    current = estimate
    for iteration in range(ITERS):
        correction = jnp.zeros((DEPTH, NX, NY), jnp.float32)
        for view_number in range(VIEWS):
            blurred = apply_blur(current, kernels_all[view_number], False)
            ratio_field = registered_list[view_number] / blurred
            correction = correction + apply_blur(ratio_field, kernels_all[view_number], True)
        current = current * correction / weight_norm
    return current
```

```python
import jax
import jax.numpy as jnp
import numpy as np
from jax import lax
from jax.experimental import pallas as pl
from jax.experimental.pallas import tpu as pltpu
from jax.sharding import PartitionSpec as P

OMAX = 8
ITERS = 2
TAPS = 31
HALF = 15
EDGE = 16
F32 = jnp.float32
BF16 = jnp.bfloat16
highest = lax.Precision.HIGHEST

NN = (((1,), (0,)), ((), ()))
NT = (((1,), (1,)), ((), ()))


def split(value):
    high = value.astype(BF16)
    low = (value - high.astype(F32)).astype(BF16)
    return high, low


def dot3(a, b, dims):
    def one(p, q):
        return lax.dot_general(p, q, dims, preferred_element_type=F32)

    return one(a[0], b[0]) + (one(a[0], b[1]) + one(a[1], b[0]))


def call(body, outs, args, scratch=(), flops=0, name=None):
    specs = [
        pl.BlockSpec(memory_space=pltpu.SMEM) if a.dtype == jnp.int32 else pl.BlockSpec(memory_space=pltpu.VMEM)
        for a in args
    ]
    outs = [jax.ShapeDtypeStruct(*o) for o in outs]
    moved = sum(int(np.prod(a.shape)) * a.dtype.itemsize for a in list(args) + outs)
    return pl.pallas_call(
        body,
        out_shape=outs,
        in_specs=specs,
        out_specs=[pl.BlockSpec(memory_space=pltpu.VMEM)] * len(outs),
        scratch_shapes=list(scratch),
        compiler_params=pltpu.CompilerParams(vmem_limit_bytes=24 << 20),
        cost_estimate=pl.CostEstimate(flops=flops, bytes_accessed=moved, transcendentals=0),
        name=name,
    )(*args)


def toeplitz(row, rows, width, shift):
    wide = jnp.broadcast_to(row[:, :width], (rows, width))
    return pltpu.roll(wide, shift % width, 1, stride=1, stride_axis=0)


def bands_body(taps, kz_h, kz_l, bx_h, bx_l, bt_h, bt_l, yf_h, yf_l, ym_h, ym_l):
    nz = kz_h.shape[1]
    for m in range(2):
        kz_h[m], kz_l[m] = split(toeplitz(taps[m : m + 1], nz, 512, 0)[:, :nz])
    lane = lax.broadcasted_iota(jnp.int32, (64, 256), 1)
    for v in range(2):
        for p in range(4):
            h, l = split(toeplitz(taps[2 + v : 3 + v], 32, 256, 64 * p + 1))
            bx_h[v, 32 * p : 32 * p + 32], bx_l[v, 32 * p : 32 * p + 32] = h, l
        h, l = split(toeplitz(taps[6 + v : 7 + v], 128, 256, -HALF))
        yf_h[128 * v : 128 * v + 128], yf_l[128 * v : 128 * v + 128] = h, l
        ym_h[v], ym_l[v] = split(toeplitz(taps[8 + v : 9 + v], 128, 256, -HALF))
    for p in range(4):
        both = jnp.zeros((64, 256), F32)
        for v in range(2):
            at = 128 * v + 32 * p
            band = toeplitz(taps[4 + v : 5 + v], 64, 256, at - 2 * HALF - 1)
            both = jnp.where((lane >= at) & (lane < at + 32), band, both)
        bt_h[64 * p : 64 * p + 64], bt_l[64 * p : 64 * p + 64] = split(both)


def placing(width, step, start):
    place = np.zeros((TAPS, width), np.float32)
    for k in range(TAPS):
        place[k, (step * (k - start)) % width] = 1
    return place


def bands(own, other, planes):
    nz = 8 * planes
    z_rows = jnp.dot(jnp.stack([own[0], own[0, ::-1]]), placing(512, 8, HALF), precision=highest)
    rows = jnp.stack([own[1], other[1], own[1, ::-1], other[1, ::-1], own[2], other[2], own[2, ::-1], other[2, ::-1]])
    taps = jnp.concatenate([z_rows, jnp.pad(rows, ((0, 6), (0, 512 - TAPS)))])
    shapes = [(2, nz, nz), (2, 128, 256), (256, 256), (256, 256), (2, 128, 256)]
    return call(bands_body, [(s, BF16) for s in shapes for _ in range(2)], [taps], name="bands")


def pack_columns(value, at, width, scratch):
    flat = value.reshape(value.shape[0] * value.shape[1], 128)
    scratch[...] = flat.T
    return scratch[pl.ds(pl.multiple_of(at, 8), width), :]


def spread_columns(pack, at, width, scratch):
    for t, part in enumerate(pack):
        scratch[pl.ds(pl.multiple_of(at, 8), width), 128 * t : 128 * t + 128] = part
    return scratch[...].T


def begin_body(info, est, raw, cur_out, pack_out, turned):
    core, tx = info[0], info[1]
    cur_out[...] = est[pl.ds(24 * core, 24)]
    for xh in range(2):
        cols = pack_columns(cur_out[:, 16 * xh : 16 * xh + 16, :], 112 * (1 - tx), 16, turned)
        for t in range(3):
            pack_out[3 * xh + t] = cols[:, 128 * t : 128 * t + 128]
    for xb in range(4):
        cols = pack_columns(raw[:, 8 * xb : 8 * xb + 8, :], 120 * (1 - tx), 8, turned)
        for t in range(3):
            pack_out[6 + 3 * (xb // 2) + t, 8 * (xb % 2) : 8 * (xb % 2) + 8, :] = cols[:, 128 * t : 128 * t + 128]


def rims_body(cur, raw, pack, ext_out, up_out, dn_out, rup_out, rdn_out):
    ext_out[...] = pack[0:6]
    up_out[0:24] = cur[:, 0:16, :]
    up_out[24:27] = pack[0:3]
    dn_out[0:24] = cur[:, 16:32, :]
    dn_out[24:27] = pack[3:6]
    rup_out[0:48] = raw[:, 0:8, :]
    rup_out[48:51] = pack[6:9, 0:8, :]
    rdn_out[0:48] = raw[:, 24:32, :]
    rdn_out[48:51] = pack[9:12, 8:16, :]


def register_body(info, raw, pack, above, below, out, wide, turned):
    tx, sx, sy = info[1], info[2], info[3]
    wide[:, 0:8, 0:128] = above[0:48]
    wide[:, 8:40, 0:128] = raw[...]
    wide[:, 40:48, 0:128] = below[0:48]
    turned[...] = jnp.zeros_like(turned)
    for b in range(6):
        if b == 0:
            parts = [above[48 + t] for t in range(3)]
        elif b == 5:
            parts = [below[48 + t] for t in range(3)]
        else:
            xb = b - 1
            parts = [pack[6 + 3 * (xb // 2) + t, 8 * (xb % 2) : 8 * (xb % 2) + 8, :] for t in range(3)]
        wide[:, 8 * b : 8 * b + 8, 128:256] = spread_columns(parts, 120 * tx, 8, turned).reshape(48, 8, 128)
    for z in range(0, 48, 4):
        rows = pltpu.roll(wide[z : z + 4], lax.rem(40 - sx, 48), 1)[:, 0:32, :]
        out[z : z + 4] = pltpu.roll(rows, lax.rem(256 - sy, 256), 2)[:, :, 0:128]


def forward_body(info, cur, ext, above, below, yf_h, yf_l, bx_h, bx_l, own, other, x_h, x_l, turned):
    tx = info[1]
    turned[...] = jnp.zeros_like(turned)
    for b in range(4):
        main = (above[0:24], cur[:, 0:16, :], cur[:, 16:32, :], below[0:24])[b]
        rim = ([above[24 + t] for t in range(3)], [ext[t] for t in range(3)],
               [ext[3 + t] for t in range(3)], [below[24 + t] for t in range(3)])[b]
        at = slice(16 * b, 16 * b + 16)
        x_h[:, at, 0:128], x_l[:, at, 0:128] = split(main)
        side = spread_columns(rim, 112 * tx, 16, turned).reshape(24, 16, 128)
        x_h[:, at, 128:256], x_l[:, at, 128:256] = split(side)
    yf = (yf_h[...], yf_l[...])
    for g in range(6):
        z = slice(4 * g, 4 * g + 4)
        rows = (x_h[z].reshape(256, 256), x_l[z].reshape(256, 256))
        along_y = split(dot3(rows, yf, NT))
        for v, out in ((0, own), (1, other)):
            cols = slice(128 * v, 128 * v + 128)
            part = (along_y[0][:, cols], along_y[1][:, cols])
            out[z] = dot3((bx_h[v], bx_l[v]), part, NN).reshape(4, 32, 128)


def ratio_body(info, mine, theirs, seen, kz_h, kz_l, keep, send, side_keep, side_send, full, turned):
    core, tx = info[0], info[1]
    full[pl.ds(24 * core, 24)] = mine[...]
    full[pl.ds(24 * (1 - core), 24)] = theirs[...]
    for xp in range(2):
        def pair(ref):
            return jnp.concatenate(
                [ref[:, 16 * xp + 8 * i : 16 * xp + 8 * i + 8, :].reshape(384, 128) for i in range(2)], axis=1
            )
        blurred = dot3((kz_h[0], kz_l[0]), split(pair(full)), NN)
        ratio = pair(seen) / blurred
        turned_back = dot3((kz_h[1], kz_l[1]), split(ratio), NN)
        for i in range(2):
            at = slice(16 * xp + 8 * i, 16 * xp + 8 * i + 8)
            full[:, at, :] = turned_back[:, 128 * i : 128 * i + 128].reshape(48, 8, 128)
    for half, out, side in ((core, keep, side_keep), (1 - core, send, side_send)):
        out[...] = full[pl.ds(24 * half, 24)]
        for xh in range(2):
            cols = pack_columns(out[:, 16 * xh : 16 * xh + 16, :], 112 * (1 - tx), 16, turned)
            for t in range(3):
                side[3 * xh + t] = cols[:, 128 * t : 128 * t + 128]


def mirror_body(info, own, other, side_own, side_other, ym_h, ym_l, bt_h, bt_l, up, mid, dn, x_h, x_l, turned):
    tx = info[1]
    turned[...] = jnp.zeros_like(turned)
    for v, main, side in ((0, own, side_own), (1, other, side_other)):
        x_h[v, :, :, 0:128], x_l[v, :, :, 0:128] = split(main[...])
        for xh in range(2):
            at = slice(16 * xh, 16 * xh + 16)
            cols = spread_columns([side[3 * xh + t] for t in range(3)], 112 * tx, 16, turned).reshape(24, 16, 128)
            x_h[v, :, at, 128:256], x_l[v, :, at, 128:256] = split(cols)
    for g in range(6):
        z = slice(4 * g, 4 * g + 4)
        along_y = [
            split(dot3((x_h[v, z].reshape(128, 256), x_l[v, z].reshape(128, 256)), (ym_h[v], ym_l[v]), NT))
            for v in range(2)
        ]
        both = tuple(jnp.concatenate([along_y[0][i], along_y[1][i]], axis=0) for i in range(2))
        wide = dot3((bt_h[...], bt_l[...]), both, NN).reshape(4, 64, 128)
        up[z] = wide[:, 0:16, :]
        mid[z] = wide[:, 16:48, :]
        dn[z] = wide[:, 48:64, :]


def gather_body(info, mid, above, below, out, side, turned):
    tx = info[1]
    out[:, 0:16, :] = mid[:, 0:16, :] + above[...]
    out[:, 16:32, :] = mid[:, 16:32, :] + below[...]
    for xh in range(2):
        cols = pack_columns(out[:, 16 * xh : 16 * xh + 16, :], 112 * (1 - tx), 16, turned)
        for t in range(3):
            side[3 * xh + t] = cols[:, 128 * t : 128 * t + 128]


def update_body(mine, theirs, cur, norm, ext, side_a, side_b, norm_ext, cur_out, ext_out, up_out, dn_out):
    cur_out[...] = cur[...] * (mine[...] + theirs[...]) / norm[...]
    ext_out[...] = ext[...] * (side_a[...] + side_b[...]) / norm_ext[...]
    up_out[0:24] = cur_out[:, 0:16, :]
    up_out[24:27] = ext_out[0:3]
    dn_out[0:24] = cur_out[:, 16:32, :]
    dn_out[24:27] = ext_out[3:6]


def last_body(mine, theirs, cur, norm, cur_out):
    cur_out[...] = cur[...] * (mine[...] + theirs[...]) / norm[...]


def whole_body(info, mine, theirs, out):
    core = info[0]
    out[pl.ds(24 * core, 24)] = mine[...]
    out[pl.ds(24 * (1 - core), 24)] = theirs[...]


def window_sums(taps, first, count, shift, extent):
    place = first + lax.broadcasted_iota(jnp.int32, (1, count, TAPS), 1) + lax.broadcasted_iota(jnp.int32, (1, count, TAPS), 2) - HALF
    moved = place + shift[:, None, None]
    inside = (place >= 0) & (place < extent) & (moved >= 0) & (moved < extent)
    return jnp.sum(jnp.where(inside, taps[:, None, :], 0.0), axis=-1)


def norms(kernels, offsets, core, tx, ty, depth, tile_x, tile_y, nx, ny):
    mirrored = kernels[:, :, ::-1]
    zero = jnp.zeros_like(offsets[:, 0])
    part_z = window_sums(mirrored[:, 0], core * (depth // 2), depth // 2, zero, depth)
    part_x = window_sums(mirrored[:, 1], ty * tile_x, tile_x, offsets[:, 0], nx)
    part_y = window_sums(mirrored[:, 2], tx * tile_y, tile_y, offsets[:, 1], ny)
    part_e = window_sums(mirrored[:, 2], tile_y - EDGE * tx, EDGE, offsets[:, 1], ny)
    zx = part_z[:, :, None] * part_x[:, None, :]
    views = kernels.shape[0]
    norm = sum(zx[v][:, :, None] * part_y[v][None, None, :] for v in range(views))
    flat = jnp.stack([zx[:, :, :EDGE].reshape(views, 3, 128), zx[:, :, EDGE:].reshape(views, 3, 128)], axis=1)
    flat = flat.reshape(views, 6, 128)
    norm_ext = sum(flat[v][:, None, :] * part_e[v][None, :, None] for v in range(views))
    return norm, norm_ext


def swap(value, axis, by, sizes):
    count = int(np.prod(sizes))
    return lax.ppermute(value, axis, [(i, i ^ by) for i in range(count)])


def shards(raw_views, psf_taps, offsets, estimate):
    depth, tile_x, tile_y = estimate.shape
    half = depth // 2
    view, tx, ty = (lax.axis_index(a) for a in ("view", "tx", "ty"))
    core = view % 2
    rows = lax.axis_size("ty")
    lower = [(i, i + 1) for i in range(rows - 1)]
    upper = [(i + 1, i) for i in range(rows - 1)]
    raw = raw_views[0]

    shifts = lax.dynamic_index_in_dim(offsets, view, 0, keepdims=False)
    info = jnp.stack([core, tx, shifts[0], shifts[1]]).astype(jnp.int32)

    tile_half = (half, tile_x, tile_y)
    pack = (6, EDGE, 128)
    turned = pltpu.VMEM((128, 384), F32)

    cur, sides = call(begin_body, [(tile_half, F32), ((12, EDGE, 128), F32)], [info, estimate, raw], [turned], name="begin")
    sides = swap(sides, "tx", 1, (2,))

    kernels = psf_taps / jnp.sum(psf_taps, axis=-1, keepdims=True)
    own = lax.dynamic_index_in_dim(kernels, view, 0, keepdims=False)
    other = lax.dynamic_index_in_dim(kernels, view ^ 1, 0, keepdims=False)
    kz_h, kz_l, bx_h, bx_l, bt_h, bt_l, yf_h, yf_l, ym_h, ym_l = bands(own, other, depth)
    norm, norm_ext = norms(
        kernels, offsets, core, tx, ty, depth, tile_x, tile_y, tile_x * rows, tile_y * lax.axis_size("tx")
    )

    rim = (half + 3, EDGE, 128)
    raw_rim = (depth + 3, OMAX, 128)
    ext, up, dn, raw_up, raw_dn = call(
        rims_body, [(pack, F32), (rim, F32), (rim, F32), (raw_rim, F32), (raw_rim, F32)], [cur, raw, sides], name="rims"
    )
    above = lax.ppermute(dn, "ty", lower)
    below = lax.ppermute(up, "ty", upper)
    raw_above = lax.ppermute(raw_dn, "ty", lower)
    raw_below = lax.ppermute(raw_up, "ty", upper)
    seen = None

    for iteration in range(ITERS):
        mine, theirs = call(
            forward_body,
            [(tile_half, F32), (tile_half, F32)],
            [info, cur, ext, above, below, yf_h, yf_l, bx_h, bx_l],
            [pltpu.VMEM((half, 64, 256), BF16), pltpu.VMEM((half, 64, 256), BF16), turned],
            flops=3 * 2 * (1536 * 256 * 256 + 12 * 128 * 256 * 128),
            name="forward",
        )
        theirs = swap(theirs, "view", 1, (4,))
        if seen is None:
            (seen,) = call(
                register_body,
                [((depth, tile_x, tile_y), F32)],
                [info, raw, sides, raw_above, raw_below],
                [pltpu.VMEM((depth, tile_x + 2 * OMAX, 256), F32), turned],
                name="register",
            )
        keep, send, side_keep, side_send = call(
            ratio_body,
            [(tile_half, F32), (tile_half, F32), (pack, F32), (pack, F32)],
            [info, mine, theirs, seen, kz_h, kz_l],
            [pltpu.VMEM((depth, tile_x, tile_y), F32), turned],
            flops=3 * 2 * 2 * 384 * 384 * 512,
            name="ratio",
        )
        send = swap(send, "view", 1, (4,))
        side_keep = swap(side_keep, "tx", 1, (2,))
        side_send = swap(side_send, ("view", "tx"), 3, (4, 2))
        up_part, mid, dn_part = call(
            mirror_body,
            [((half, EDGE, tile_y), F32), (tile_half, F32), ((half, EDGE, tile_y), F32)],
            [info, keep, send, side_keep, side_send, ym_h, ym_l, bt_h, bt_l],
            [pltpu.VMEM((2, half, 32, 256), BF16), pltpu.VMEM((2, half, 32, 256), BF16), turned],
            flops=3 * 2 * (1536 * 256 * 128 + 6 * 256 * 256 * 128),
            name="mirror",
        )
        from_above = lax.ppermute(dn_part, "ty", lower)
        from_below = lax.ppermute(up_part, "ty", upper)
        summed, side = call(
            gather_body, [(tile_half, F32), (pack, F32)], [info, mid, from_above, from_below], [turned], name="gather"
        )
        partner = swap(summed, "view", 2, (4,))
        if iteration == ITERS - 1:
            (cur,) = call(last_body, [(tile_half, F32)], [summed, partner, cur, norm], name="last")
        else:
            side_a = swap(side, "tx", 1, (2,))
            side_b = swap(side, ("view", "tx"), 5, (4, 2))
            cur, ext, up, dn = call(
                update_body,
                [(tile_half, F32), (pack, F32), (rim, F32), (rim, F32)],
                [summed, partner, cur, norm, ext, side_a, side_b, norm_ext],
                name="update",
            )
            above = lax.ppermute(dn, "ty", lower)
            below = lax.ppermute(up, "ty", upper)
    far = swap(cur, "view", 1, (4,))
    (out,) = call(whole_body, [((depth, tile_x, tile_y), F32)], [info, cur, far], name="whole")
    return out


def solution(mesh):
    placed = (P("view", None, "ty", "tx"), P(), P(), P(None, "ty", "tx"))
    return jax.shard_map(
        shards, mesh=mesh, in_specs=placed, out_specs=P(None, "ty", "tx"), check_vma=False
    )
```

```python
import functools

import jax
import jax.numpy as jnp
import numpy as np
from jax import lax
from jax.experimental import pallas as pl
from jax.experimental.pallas import tpu as pltpu
from jax.sharding import PartitionSpec as P

OMAX = 8
ITERS = 2
TAPS = 31
HALF = 15
EDGE = 16
F32 = jnp.float32
BF16 = jnp.bfloat16
highest = lax.Precision.HIGHEST

NN = (((1,), (0,)), ((), ()))
NT = (((1,), (1,)), ((), ()))


def split(value):
    high = value.astype(BF16)
    low = (value - high.astype(F32)).astype(BF16)
    return high, low


def dot3(a, b, dims):
    def one(p, q):
        return lax.dot_general(p, q, dims, preferred_element_type=F32)

    return one(a[0], b[0]) + (one(a[0], b[1]) + one(a[1], b[0]))


def call(body, outs, args, scratch=(), flops=0, name=None, place=pltpu.VMEM):
    specs = [
        pl.BlockSpec(memory_space=pltpu.SMEM if a.ndim == 1 or a.dtype == jnp.int32 else place) for a in args
    ]
    outs = [jax.ShapeDtypeStruct(*o) for o in outs]
    moved = sum(int(np.prod(a.shape)) * a.dtype.itemsize for a in list(args) + outs)
    return pl.pallas_call(
        body,
        out_shape=outs,
        in_specs=specs,
        out_specs=[pl.BlockSpec(memory_space=pltpu.VMEM)] * len(outs),
        scratch_shapes=list(scratch),
        compiler_params=pltpu.CompilerParams(vmem_limit_bytes=10 << 20),
        cost_estimate=pl.CostEstimate(flops=flops, bytes_accessed=moved, transcendentals=0),
        name=name,
    )(*args)


def toeplitz(row, rows, width, shift):
    wide = jnp.broadcast_to(row[:, :width], (rows, width))
    return pltpu.roll(wide, shift % width, 1, stride=1, stride_axis=0)


BX, BT, YF = 0, 2, 4


def bands_body(taps, kz, mats):
    nz = kz.shape[1]
    for m in range(2):
        kz[2 * m], kz[2 * m + 1] = split(toeplitz(taps[m : m + 1], nz, 512, 0)[:, :nz])
    lane = lax.broadcasted_iota(jnp.int32, (64, 256), 1)

    def put(m, at, band):
        rows = slice(at, at + band.shape[0])
        mats[m, rows], mats[m + 1, rows] = split(band)

    for v in range(2):
        for p in range(4):
            put(BX, 128 * v + 32 * p, toeplitz(taps[2 + v : 3 + v], 32, 256, 64 * p + 1))
        put(YF, 128 * v, toeplitz(taps[6 + v : 7 + v], 128, 256, -HALF))
    for p in range(4):
        both = jnp.zeros((64, 256), F32)
        for v in range(2):
            at = 128 * v + 32 * p
            band = toeplitz(taps[4 + v : 5 + v], 64, 256, at - 2 * HALF - 1)
            both = jnp.where((lane >= at) & (lane < at + 32), band, both)
        put(BT, 64 * p, both)


def placing(width, step, start):
    place = np.zeros((TAPS, width), np.float32)
    for k in range(TAPS):
        place[k, (step * (k - start)) % width] = 1
    return place


def bands(own, other, planes):
    nz = 8 * planes
    z_rows = jnp.dot(jnp.stack([own[0], own[0, ::-1]]), placing(512, 8, HALF), precision=highest)
    rows = jnp.stack([own[1], other[1], own[1, ::-1], other[1, ::-1], own[2], other[2]])
    taps = jnp.concatenate([z_rows, jnp.pad(rows, ((0, 0), (0, 512 - TAPS)))])
    return call(bands_body, [((4, nz, nz), BF16), ((6, 256, 256), BF16)], [taps], name="bands")


def pack_columns(value, at, width, scratch):
    flat = value.reshape(value.shape[0] * value.shape[1], 128)
    scratch[...] = flat.T
    return scratch[pl.ds(pl.multiple_of(at, 8), width), :]


def spread_columns(pack, at, width, scratch):
    for t, part in enumerate(pack):
        scratch[pl.ds(pl.multiple_of(at, 8), width), 128 * t : 128 * t + 128] = part
    return scratch[...].T


def norm_body(shape, psf, offsets, norm, norm_ext):
    nx, ny = shape
    views = offsets.shape[0]
    core = lax.axis_index("view") % 2
    x_first = 32 * lax.axis_index("ty")
    tx = lax.axis_index("tx")

    def window(view, dim, place, shift, extent):
        total = jnp.zeros(place.shape, F32)
        weight = 0.0
        for i in range(TAPS):
            tap = psf[(view * 3 + dim) * TAPS + TAPS - 1 - i]
            at = place + (i - HALF)
            moved = at + shift
            inside = (at >= 0) & (at < extent) & (moved >= 0) & (moved < extent)
            total = total + jnp.where(inside, tap, 0.0)
            weight = weight + tap
        return total / weight

    def iota(shape, dim):
        return lax.broadcasted_iota(jnp.int32, shape, dim)

    lane = iota((8, 128), 1)
    tile = jnp.minimum(iota((8, 128), 0), 2)
    flat_z = 24 * core + (128 * tile + lane) // EDGE
    flat_x = x_first + EDGE * (iota((8, 128), 0) % 2) + lane % EDGE
    acc = [jnp.zeros((32, 128), F32) for _ in range(24)]
    ext = [jnp.zeros((EDGE, 128), F32) for _ in range(6)]
    for v in range(views):
        sx, sy = offsets[v, 0], offsets[v, 1]
        in_z = window(v, 0, 24 * core + iota((24, 128), 0), 0, 48)
        in_x = window(v, 1, x_first + iota((32, 128), 0), sx, nx)
        in_y = window(v, 2, 128 * tx + lane, sy, ny)[0:1]
        in_e = window(v, 2, 128 - EDGE * tx + iota((EDGE, 128), 0), sy, ny)
        z_row = window(v, 0, flat_z, 0, 48)
        x_row = window(v, 1, flat_x, sx, nx)
        xy = in_x * in_y
        acc = [acc[z] + in_z[z : z + 1] * xy for z in range(24)]
        for k in range(6):
            ext[k] = ext[k] + in_e * (z_row[k % 3 : k % 3 + 1] * x_row[k // 3 : k // 3 + 1])
    for z in range(24):
        norm[z] = acc[z]
    for k in range(6):
        norm_ext[k] = ext[k]


def mesh_core():
    return lax.axis_index("view") % 2


def parity():
    return lax.axis_index("ty") % 2 == 1


def put_packs(value, at, width, turned, out, first):
    cols = pack_columns(value, at, width, turned)
    for t in range(3):
        out[first + t] = cols[:, 128 * t : 128 * t + 128]


def begin_body(est, raw, cur_out, pack_out, raw_here, turned, sems):
    tx = lax.axis_index("tx")
    half = est.at[pl.ds(24 * mesh_core(), 24)]
    copies = [pltpu.make_async_copy(half, cur_out, sems.at[0]), pltpu.make_async_copy(raw, raw_here, sems.at[1])]
    for copy in copies:
        copy.start()
    copies[0].wait()
    for xh in range(2):
        put_packs(cur_out[:, 16 * xh : 16 * xh + 16, :], 112 * (1 - tx), 16, turned, pack_out, 3 * xh)
    copies[1].wait()
    for xb in range(4):
        cols = pack_columns(raw_here[:, 8 * xb : 8 * xb + 8, :], 120 * (1 - tx), 8, turned)
        for t in range(3):
            pack_out[6 + 3 * (xb // 2) + t, 8 * (xb % 2) : 8 * (xb % 2) + 8, :] = cols[:, 128 * t : 128 * t + 128]


def raw_part(pack, xb, t):
    at = 8 * (xb % 2)
    return pack[6 + 3 * (xb // 2) + t, at : at + 8, :]


def put_rims(top, bottom, even_out, odd_out, planes):
    odd = parity()
    even_out[planes] = jnp.where(odd, top, bottom)
    odd_out[planes] = jnp.where(odd, bottom, top)


def rims_body(cur, raw, pack, ext_out, even_out, odd_out):
    ext_out[...] = pack[0:6]
    put_rims(cur[:, 0:16, :], cur[:, 16:32, :], even_out, odd_out, slice(0, 24))
    put_rims(pack[0:3], pack[3:6], even_out, odd_out, slice(24, 27))
    top = raw[:, 0:8, :].reshape(24, 16, 128)
    bottom = raw[:, 24:32, :].reshape(24, 16, 128)
    put_rims(top, bottom, even_out, odd_out, slice(27, 51))
    for p in range(2):
        tops, bottoms = (
            jnp.concatenate([raw_part(pack, xb, 2 * p), raw_part(pack, xb, min(2 * p + 1, 2))])[None] for xb in (0, 3)
        )
        put_rims(tops, bottoms, even_out, odd_out, slice(51 + p, 52 + p))


def register_body(offsets, raw, pack, from_even, from_odd, out, wide, turned):
    view, tx = lax.axis_index("view"), lax.axis_index("tx")
    sx, sy = offsets[view, 0], offsets[view, 1]
    odd = parity()
    above = jnp.where(odd, from_even[27:53], from_odd[27:53])
    below = jnp.where(odd, from_odd[27:53], from_even[27:53])
    wide[:, 0:8, 0:128] = above[0:24].reshape(48, 8, 128)
    wide[:, 8:40, 0:128] = raw[...]
    wide[:, 40:48, 0:128] = below[0:24].reshape(48, 8, 128)
    turned[...] = jnp.zeros_like(turned)
    for b in range(6):
        if b in (0, 5):
            rim = above if b == 0 else below
            parts = [rim[24, 0:8], rim[24, 8:16], rim[25, 0:8]]
        else:
            parts = [raw_part(pack, b - 1, t) for t in range(3)]
        wide[:, 8 * b : 8 * b + 8, 128:256] = spread_columns(parts, 120 * tx, 8, turned).reshape(48, 8, 128)
    for z in range(0, 48, 4):
        rows = pltpu.roll(wide[z : z + 4], lax.rem(40 - sx, 48), 1)[:, 0:32, :]
        out[z : z + 4] = pltpu.roll(rows, lax.rem(256 - sy, 256), 2)[:, :, 0:128]


def forward_body(cur, ext, from_even, from_odd, mats, own, other, x_h, x_l, turned):
    tx = lax.axis_index("tx")
    odd = parity()
    above = jnp.where(odd, from_even[0:27], from_odd[0:27])
    below = jnp.where(odd, from_odd[0:27], from_even[0:27])
    turned[...] = jnp.zeros_like(turned)
    for b in range(4):
        main = (above[0:24], cur[:, 0:16, :], cur[:, 16:32, :], below[0:24])[b]
        rim = ([above[24 + t] for t in range(3)], [ext[t] for t in range(3)],
               [ext[3 + t] for t in range(3)], [below[24 + t] for t in range(3)])[b]
        at = slice(16 * b, 16 * b + 16)
        x_h[:, at, 0:128], x_l[:, at, 0:128] = split(main)
        side = spread_columns(rim, 112 * tx, 16, turned).reshape(24, 16, 128)
        x_h[:, at, 128:256], x_l[:, at, 128:256] = split(side)
    yf = (mats[YF], mats[YF + 1])
    for g in range(6):
        z = slice(4 * g, 4 * g + 4)
        rows = (x_h[z].reshape(256, 256), x_l[z].reshape(256, 256))
        along_y = split(dot3(rows, yf, NT))
        for v, out in ((0, own), (1, other)):
            cols = slice(128 * v, 128 * v + 128)
            part = (along_y[0][:, cols], along_y[1][:, cols])
            out[z] = dot3((mats[BX, cols], mats[BX + 1, cols]), part, NN).reshape(4, 32, 128)


def ratio_body(mine, theirs, seen, kz, keep, send, full):
    core = mesh_core()
    full[pl.ds(24 * core, 24)] = mine[...]
    full[pl.ds(24 * (1 - core), 24)] = theirs[...]
    for xp in range(2):
        def pair(ref):
            return jnp.concatenate(
                [ref[:, 16 * xp + 8 * i : 16 * xp + 8 * i + 8, :].reshape(384, 128) for i in range(2)], axis=1
            )
        blurred = dot3((kz[0], kz[1]), split(pair(full)), NN)
        ratio = pair(seen) / blurred
        back = dot3((kz[2], kz[3]), split(ratio), NN)
        for i in range(2):
            at = slice(16 * xp + 8 * i, 16 * xp + 8 * i + 8)
            full[:, at, :] = back[:, 128 * i : 128 * i + 128].reshape(48, 8, 128)
    keep[...] = full[pl.ds(24 * core, 24)]
    send[...] = full[pl.ds(24 * (1 - core), 24)]


def mirror_body(own, other, mats, even_out, odd_out, mid, mid_ext, sides, turned):
    tx = lax.axis_index("tx")
    for g in range(6):
        z = slice(4 * g, 4 * g + 4)
        along_y = [
            split(dot3(split(ref[z].reshape(128, 128)), (mats[YF, at : at + 128], mats[YF + 1, at : at + 128]), NN))
            for ref, at in ((own, 0), (other, 128))
        ]
        both = tuple(jnp.concatenate([along_y[0][i], along_y[1][i]], axis=0) for i in range(2))
        wide = dot3((mats[BT], mats[BT + 1]), both, NN).reshape(4, 64, 256)
        put_rims(wide[:, 0:16, 0:128], wide[:, 48:64, 0:128], even_out, odd_out, z)
        mid[z] = wide[:, 16:48, 0:128]
        sides[z] = wide[:, :, 128:256]
    cols = []
    for b in range(4):
        cols.append(pack_columns(sides[:, 16 * b : 16 * b + 16, :], 112 * tx, 16, turned))
    parts = [[c[:, 128 * t : 128 * t + 128] for t in range(3)] for c in cols]
    for t in range(3):
        put_rims(parts[0][t][None], parts[3][t][None], even_out, odd_out, slice(24 + t, 25 + t))
        mid_ext[t] = parts[1][t]
        mid_ext[3 + t] = parts[2][t]


def gather_body(mid, mid_ext, from_even, from_odd, low_out, high_out, sides_out, turned):
    tx = lax.axis_index("tx")
    odd = parity()
    above = jnp.where(odd, from_even[...], from_odd[...])
    below = jnp.where(odd, from_odd[...], from_even[...])
    for out, z in ((low_out, slice(0, 12)), (high_out, slice(12, 24))):
        out[0:12, 0:16, :] = mid[z, 0:16, :] + above[z]
        out[0:12, 16:32, :] = mid[z, 16:32, :] + below[z]
    sides_out[0:3] = mid_ext[0:3] + above[24:27]
    sides_out[3:6] = mid_ext[3:6] + below[24:27]
    low_out[12:13] = sides_out[0:2].reshape(1, 32, 128)
    high_out[12:14] = sides_out[2:6].reshape(2, 32, 128)
    for xh in range(2):
        at = slice(16 * xh, 16 * xh + 16)
        both = jnp.concatenate([low_out[0:12, at, :], high_out[0:12, at, :]])
        put_packs(both, 112 * (1 - tx), 16, turned, sides_out, 6 + 3 * xh)


def new_estimate(low, high, p_low, p_high, side_a, side_b, cur, norm, cur_out, turned):
    tx = lax.axis_index("tx")
    turned[...] = jnp.zeros_like(turned)
    for xh in range(2):
        at = slice(16 * xh, 16 * xh + 16)
        parts = [side_a[3 * xh + t] + side_b[3 * xh + t] for t in range(3)]
        edge = spread_columns(parts, 112 * (1 - tx), 16, turned).reshape(24, 16, 128)
        for mine, theirs, z in ((low, p_low, slice(0, 12)), (high, p_high, slice(12, 24))):
            total = mine[0:12, at, :] + theirs[0:12, at, :] + edge[z]
            cur_out[z, at, :] = cur[z, at, :] * total / norm[z, at, :]


def update_body(
    low, high, p_low, p_high, side_a, side_b, cur, norm, ext, norm_ext, cur_out, ext_out, even_out, odd_out, turned
):
    new_estimate(low, high, p_low, p_high, side_a, side_b, cur, norm, cur_out, turned)
    total = side_a[6:12] + side_b[6:12]
    total_low = total[0:2] + low[12:13].reshape(2, 16, 128) + p_low[12:13].reshape(2, 16, 128)
    total_high = total[2:6] + high[12:14].reshape(4, 16, 128) + p_high[12:14].reshape(4, 16, 128)
    ext_out[0:2] = ext[0:2] * total_low / norm_ext[0:2]
    ext_out[2:6] = ext[2:6] * total_high / norm_ext[2:6]
    put_rims(cur_out[:, 0:16, :], cur_out[:, 16:32, :], even_out, odd_out, slice(0, 24))
    put_rims(ext_out[0:3], ext_out[3:6], even_out, odd_out, slice(24, 27))


def whole_body(mine, theirs, out):
    core = mesh_core()
    out[pl.ds(24 * core, 24)] = mine[...]
    out[pl.ds(24 * (1 - core), 24)] = theirs[...]


def swap(value, axis, by, sizes):
    count = int(np.prod(sizes))
    return lax.ppermute(value, axis, [(i, i ^ by) for i in range(count)])


def rim_swap(even, odd):
    rows = lax.axis_size("ty")
    odd_pairs = [(i, i + 1) for i in range(1, rows - 1, 2)]
    odd_pairs += [(b, a) for a, b in odd_pairs]
    from_odd = lax.ppermute(odd, "ty", odd_pairs)
    from_even = lax.ppermute(even, "ty", [(i, i ^ 1) for i in range(rows)])
    return from_even, from_odd


def shards(raw_views, psf_taps, offsets, estimate):
    depth, tile_x, tile_y = estimate.shape
    half = depth // 2
    view = lax.axis_index("view")
    raw = raw_views[0]

    tile_half = ((half, tile_x, tile_y), F32)
    pack = ((6, EDGE, 128), F32)
    rim = ((half + 3, EDGE, 128), F32)
    turned = pltpu.VMEM((128, 384), F32)

    cur, sides = call(
        begin_body,
        [tile_half, ((12, EDGE, 128), F32)],
        [estimate, raw],
        [pltpu.VMEM(raw.shape, F32), turned, pltpu.SemaphoreType.DMA((2,))],
        name="begin",
        place=pl.ANY,
    )
    sides = swap(sides, "tx", 1, (2,))

    kernels = psf_taps / jnp.sum(psf_taps, axis=-1, keepdims=True)
    own = lax.dynamic_index_in_dim(kernels, view, 0, keepdims=False)
    other = lax.dynamic_index_in_dim(kernels, view ^ 1, 0, keepdims=False)
    kz, mats = bands(own, other, depth)
    extents = (tile_x * lax.axis_size("ty"), tile_y * lax.axis_size("tx"))
    norm, norm_ext = call(
        functools.partial(norm_body, extents), [tile_half, pack], [psf_taps.reshape(-1), offsets], name="norm"
    )

    first_rim = ((half + 3 + half + 2, EDGE, 128), F32)
    ext, even, odd = call(rims_body, [pack, first_rim, first_rim], [cur, raw, sides], name="rims")
    from_even, from_odd = rim_swap(even, odd)
    seen = None

    for iteration in range(ITERS):
        mine, theirs = call(
            forward_body,
            [tile_half, tile_half],
            [cur, ext, from_even, from_odd, mats],
            [pltpu.VMEM((half, 64, 256), BF16), pltpu.VMEM((half, 64, 256), BF16), turned],
            flops=3 * 2 * (1536 * 256 * 256 + 12 * 128 * 256 * 128),
            name="forward",
        )
        theirs = swap(theirs, "view", 1, (4,))
        if seen is None:
            (seen,) = call(
                register_body,
                [((depth, tile_x, tile_y), F32)],
                [offsets, raw, sides, from_even, from_odd],
                [pltpu.VMEM((depth, tile_x + 2 * OMAX, 256), F32), turned],
                name="register",
            )
        keep, send = call(
            ratio_body,
            [tile_half, tile_half],
            [mine, theirs, seen, kz],
            [pltpu.VMEM((depth, tile_x, tile_y), F32)],
            flops=3 * 2 * 2 * 384 * 384 * 512,
            name="ratio",
        )
        send = swap(send, "view", 1, (4,))
        even, odd, mid, mid_ext = call(
            mirror_body,
            [rim, rim, tile_half, pack],
            [keep, send, mats],
            [pltpu.VMEM((half, 64, 128), F32), turned],
            flops=3 * 2 * (1536 * 128 * 256 + 6 * 256 * 256 * 256),
            name="mirror",
        )
        from_even, from_odd = rim_swap(even, odd)
        low, high, sides_now = call(
            gather_body,
            [((13, tile_x, tile_y), F32), ((14, tile_x, tile_y), F32), ((12, EDGE, 128), F32)],
            [mid, mid_ext, from_even, from_odd],
            [turned],
            name="gather",
        )
        last = iteration == ITERS - 1
        if last:
            low, high, sides_now = low[0:12], high[0:12], sides_now[0:6]
        p_low = swap(low, "view", 2, (4,))
        p_high = swap(high, "view", 2, (4,))
        side_a = swap(sides_now, "tx", 1, (2,))
        side_b = swap(sides_now, ("view", "tx"), 5, (4, 2))
        parts = [low, high, p_low, p_high, side_a, side_b, cur, norm]
        if last:
            (cur,) = call(new_estimate, [tile_half], parts, [turned], name="last")
        else:
            cur, ext, even, odd = call(
                update_body, [tile_half, pack, rim, rim], parts + [ext, norm_ext], [turned], name="update"
            )
            from_even, from_odd = rim_swap(even, odd)
    far = swap(cur, "view", 1, (4,))
    (out,) = call(whole_body, [((depth, tile_x, tile_y), F32)], [cur, far], name="whole")
    return out


def solution(mesh):
    placed = (P("view", None, "ty", "tx"), P(), P(), P(None, "ty", "tx"))
    return jax.shard_map(
        shards, mesh=mesh, in_specs=placed, out_specs=P(None, "ty", "tx"), check_vma=False
    )
```

```python
import functools

import jax
import jax.numpy as jnp
import numpy as np
from jax import lax
from jax.experimental import pallas as pl
from jax.experimental.pallas import tpu as pltpu
from jax.sharding import PartitionSpec as P

OMAX = 8
ITERS = 2
TAPS = 31
HALF = 15
EDGE = 16
F32 = jnp.float32
BUSY = 6000000000
BF16 = jnp.bfloat16
highest = lax.Precision.HIGHEST

NN = (((1,), (0,)), ((), ()))


def split(value):
    high = value.astype(BF16)
    low = (value - high.astype(F32)).astype(BF16)
    return high, low


def dot(a, b, dims):
    return lax.dot_general(a, b, dims, preferred_element_type=F32)


def rows3(a, b):
    n = a.shape[0] // 2
    both = dot(a, b[0], NN)
    return both[:n] + (dot(a[:n], b[1], NN) + both[n:])


def call(body, outs, args, scratch=(), flops=0, name=None, hbm=(), limit=8, aliases=None, out_place=pltpu.VMEM):
    def place(i, a):
        if i in hbm:
            return pltpu.HBM
        return pltpu.SMEM if a.ndim == 1 or a.dtype == jnp.int32 else pltpu.VMEM

    specs = [pl.BlockSpec(memory_space=place(i, a)) for i, a in enumerate(args)]
    outs = [jax.ShapeDtypeStruct(*o) for o in outs]
    moved = sum(int(np.prod(a.shape)) * a.dtype.itemsize for a in list(args) + outs)
    return pl.pallas_call(
        body,
        out_shape=outs,
        in_specs=specs,
        out_specs=[pl.BlockSpec(memory_space=out_place)] * len(outs),
        scratch_shapes=list(scratch),
        input_output_aliases=aliases or {},
        compiler_params=pltpu.CompilerParams(vmem_limit_bytes=limit << 20),
        cost_estimate=pl.CostEstimate(flops=flops, bytes_accessed=moved, transcendentals=0),
        name=name,
    )(*args)


def toeplitz(row, rows, width, shift):
    wide = jnp.broadcast_to(row[:, :width], (rows, width))
    return pltpu.roll(wide, shift % width, 1, stride=1, stride_axis=0)


MATS = 10
YF, IN, OUT, BT, YT = 0, 2, 4, 6, 8


def bands_body(taps, psf, offsets, kz, mats):
    for m in range(2):
        high, low = split(toeplitz(taps[m : m + 1], 384, 512, 0)[:, :384])
        for third in range(3):
            rows = slice(128 * third, 128 * third + 128)
            kz[m, 256 * third : 256 * third + 128] = high[rows]
            kz[m, 256 * third + 128 : 256 * third + 256] = low[rows]
    lane = lax.broadcasted_iota(jnp.int32, (64, 256), 1)

    def between(band, first, count, rest):
        at = lane[: band.shape[0]]
        return jnp.where((at >= first) & (at < first + count), band, rest)

    for v in range(2):
        row = taps[2 + v : 3 + v]
        for p in range(4):
            at = 32 * p
            none = jnp.zeros((32, 256), F32)
            inner = between(toeplitz(row, 32, 256, at - HALF), at, 32, none)
            outer = between(toeplitz(row, 32, 256, at + 1), at, 16, none)
            outer = between(toeplitz(row, 32, 256, at - 2 * HALF - 1), at + 16, 16, outer)
            for m, band in ((IN + v, inner), (OUT + v, outer)):
                mats[m, at : at + 32], mats[m, 128 + at : 160 + at] = split(band)
        rows = slice(128 * v, 128 * v + 128)
        mats[0, rows], mats[1, rows] = split(toeplitz(taps[6 + v : 7 + v], 128, 256, -HALF))
        mats[YT, :, rows], mats[YT + 1, :, rows] = split(toeplitz(taps[8 + v : 9 + v], 256, 256, -HALF)[:, :128])
    for p in range(4):
        both = jnp.zeros((64, 256), F32)
        for v in range(2):
            at = 128 * v + 32 * p
            both = between(toeplitz(taps[4 + v : 5 + v], 64, 256, at - 2 * HALF - 1), at, 32, both)
        rows = slice(64 * p, 64 * p + 64)
        mats[BT, rows], mats[BT + 1, rows] = split(both)


def placing(width, step, start):
    place = np.zeros((TAPS, width), np.float32)
    for k in range(TAPS):
        place[k, (step * (k - start)) % width] = 1
    return place


def bands(own, other, planes, psf, offsets):
    nz = 8 * planes
    z_rows = jnp.dot(jnp.stack([own[0], own[0, ::-1]]), placing(512, 8, HALF), precision=highest)
    rows = jnp.stack([own[1], other[1], own[1, ::-1], other[1, ::-1], own[2], other[2], own[2, ::-1], other[2, ::-1]])
    taps = jnp.concatenate([z_rows, jnp.pad(rows, ((0, 0), (0, 512 - TAPS)))])
    return call(bands_body, [((2, 2 * nz, nz), BF16), ((MATS, 256, 256), BF16)], [taps, psf, offsets], name="bands")


def pack_columns(value, at, width, scratch):
    flat = value.reshape(value.shape[0] * value.shape[1], 128)
    scratch[...] = flat.T
    return scratch[pl.ds(pl.multiple_of(at, 8), width), :]


def spread_columns(pack, at, width, scratch):
    for t, part in enumerate(pack):
        scratch[pl.ds(pl.multiple_of(at, 8), width), 128 * t : 128 * t + 128] = part
    return scratch[...].T


def norm_body(shape, psf, offsets, norm, norm_ext):
    nx, ny = shape
    views = offsets.shape[0]
    core = lax.axis_index("view") % 2
    x_first = 32 * lax.axis_index("ty")
    tx = lax.axis_index("tx")

    def window(view, dim, place, shift, extent):
        total = jnp.zeros(place.shape, F32)
        weight = 0.0
        for i in range(TAPS):
            tap = psf[(view * 3 + dim) * TAPS + TAPS - 1 - i]
            at = place + (i - HALF)
            moved = at + shift
            inside = (at >= 0) & (at < extent) & (moved >= 0) & (moved < extent)
            total = total + jnp.where(inside, tap, 0.0)
            weight = weight + tap
        return total / weight

    def iota(shape, dim):
        return lax.broadcasted_iota(jnp.int32, shape, dim)

    lane = iota((8, 128), 1)
    tile = jnp.minimum(iota((8, 128), 0), 2)
    flat_z = 24 * core + (128 * tile + lane) // EDGE
    flat_x = x_first + EDGE * (iota((8, 128), 0) % 2) + lane % EDGE
    acc = [jnp.zeros((32, 128), F32) for _ in range(24)]
    ext = [jnp.zeros((EDGE, 128), F32) for _ in range(6)]
    for v in range(views):
        sx, sy = offsets[v, 0], offsets[v, 1]
        in_z = window(v, 0, 24 * core + iota((24, 128), 0), 0, 48)
        in_x = window(v, 1, x_first + iota((32, 128), 0), sx, nx)
        in_y = window(v, 2, 128 * tx + lane, sy, ny)[0:1]
        in_e = window(v, 2, 128 - EDGE * tx + iota((EDGE, 128), 0), sy, ny)
        z_row = window(v, 0, flat_z, 0, 48)
        x_row = window(v, 1, flat_x, sx, nx)
        xy = in_x * in_y
        acc = [acc[z] + in_z[z : z + 1] * xy for z in range(24)]
        for k in range(6):
            ext[k] = ext[k] + in_e * (z_row[k % 3 : k % 3 + 1] * x_row[k // 3 : k // 3 + 1])
    for z in range(24):
        norm[z] = acc[z]
    for k in range(6):
        norm_ext[k] = ext[k]


def mesh_core():
    return lax.axis_index("view") % 2


def parity():
    return lax.axis_index("ty") % 2 == 1


def put_packs(value, at, width, turned, out, first):
    cols = pack_columns(value, at, width, turned)
    for t in range(3):
        out[first + t] = cols[:, 128 * t : 128 * t + 128]


def begin_body(est, pack_out, cur, turned, sem):
    tx = lax.axis_index("tx")
    copy = pltpu.make_async_copy(est.at[pl.ds(24 * mesh_core(), 24)], cur, sem)
    copy.start()
    copy.wait()
    for xh in range(2):
        put_packs(cur[:, 16 * xh : 16 * xh + 16, :], 112 * (1 - tx), 16, turned, pack_out, 3 * xh)


def raw_sides_body(raw, pack_out, turned):
    tx = lax.axis_index("tx")
    for xb in range(4):
        put_packs(raw[:, 8 * xb : 8 * xb + 8, :], 120 * (1 - tx), 8, turned, pack_out, 3 * xb)


def put_rims(top, bottom, even_out, odd_out, planes):
    odd = parity()
    even_out[planes] = jnp.where(odd, top, bottom)
    odd_out[planes] = jnp.where(odd, bottom, top)


def rims_body(est, cur_out, odd_out, even_out):
    cur_out[...] = est[pl.ds(24 * mesh_core(), 24)]
    put_rims(cur_out[:, 0:16, :], cur_out[:, 16:32, :], even_out, odd_out, slice(0, 24))
    odd_out[24:27] = jnp.zeros((3, 16, 128), F32)
    even_out[24:27] = jnp.zeros((3, 16, 128), F32)


def corners_body(pack, odd_in, even_in, odd_out, even_out):
    put_rims(pack[0:3], pack[3:6], even_out, odd_out, slice(24, 27))


def raw_rims_body(raw, pack, odd_out, even_out):
    put_rims(raw[:, 0:8, :], raw[:, 24:32, :], even_out, odd_out, slice(0, 48))
    for t in range(3):
        put_rims(pack[t][None], pack[9 + t][None], even_out, odd_out, slice(48 + t, 49 + t))


def register_body(offsets, raw, pack, from_odd, from_even, out, wide, turned):
    view, tx = lax.axis_index("view"), lax.axis_index("tx")
    sx, sy = offsets[view, 0], offsets[view, 1]
    odd = parity()
    above = jnp.where(odd, from_even[...], from_odd[...])
    below = jnp.where(odd, from_odd[...], from_even[...])
    wide[:, 0:8, 0:128] = above[0:48]
    wide[:, 8:40, 0:128] = raw[...]
    wide[:, 40:48, 0:128] = below[0:48]
    turned[...] = jnp.zeros_like(turned)
    for b in range(6):
        if b in (0, 5):
            parts = [(above if b == 0 else below)[48 + t] for t in range(3)]
        else:
            parts = [pack[3 * (b - 1) + t] for t in range(3)]
        wide[:, 8 * b : 8 * b + 8, 128:256] = spread_columns(parts, 120 * tx, 8, turned).reshape(48, 8, 128)
    for z in range(0, 48, 4):
        rows = pltpu.roll(wide[z : z + 4], lax.rem(40 - sx, 48), 1)[:, 0:32, :]
        out[z : z + 4] = pltpu.roll(rows, lax.rem(256 - sy, 256), 2)[:, :, 0:128]


def put_columns(rows, main, rim, tx, x_h, x_l, turned):
    x_h[:, rows, 0:128], x_l[:, rows, 0:128] = split(main)
    side = spread_columns(rim, 112 * tx, 16, turned).reshape(24, 16, 128)
    x_h[:, rows, 128:256], x_l[:, rows, 128:256] = split(side)


def blur_rows(x_h, x_l, yf, bx, g):
    z = slice(4 * g, 4 * g + 4)
    high, low = x_h[z].reshape(128, 256), x_l[z].reshape(128, 256)
    along_y = split(dot(high, yf[0], NN) + (dot(high, yf[1], NN) + dot(low, yf[0], NN)))
    for v in range(2):
        cols = slice(128 * v, 128 * v + 128)
        yield v, z, rows3(bx[v][:, 0:128], (along_y[0][:, cols], along_y[1][:, cols])).reshape(4, 32, 128)


def inner_body(cur, ext, mats, own, other, x_h, x_l, turned):
    tx = lax.axis_index("tx")
    turned[...] = jnp.zeros_like(turned)
    for xh in range(2):
        rows = slice(16 * xh, 16 * xh + 16)
        put_columns(rows, cur[:, rows, :], [ext[3 * xh + t] for t in range(3)], tx, x_h, x_l, turned)
    for g in range(6):
        for v, z, part in blur_rows(x_h, x_l, (mats[YT], mats[YT + 1]), (mats[IN], mats[IN + 1]), g):
            (own, other)[v][z] = part


def outer_body(from_odd, from_even, mats, in_own, in_other, own, other, x_h, x_l, turned):
    tx = lax.axis_index("tx")
    odd = parity()
    above = jnp.where(odd, from_even[...], from_odd[...])
    below = jnp.where(odd, from_odd[...], from_even[...])
    turned[...] = jnp.zeros_like(turned)
    for xh, rim in ((0, above), (1, below)):
        rows = slice(16 * xh, 16 * xh + 16)
        put_columns(rows, rim[0:24], [rim[24 + t] for t in range(3)], tx, x_h, x_l, turned)
    for g in range(6):
        for v, z, part in blur_rows(x_h, x_l, (mats[YT], mats[YT + 1]), (mats[OUT], mats[OUT + 1]), g):
            (own, other)[v][z] = (in_own, in_other)[v][z] + part


def along_z(kz, m, high, low):
    parts = []
    for third, reach in ((0, slice(0, 256)), (1, slice(0, 384)), (2, slice(128, 384))):
        parts.append(rows3(kz[m, 256 * third : 256 * third + 256, reach], (high[reach], low[reach])))
    return jnp.concatenate(parts)


def ratio_body(mine, theirs, seen, kz, keep, send, full):
    core = mesh_core()
    full[pl.ds(24 * core, 24)] = mine[...]
    full[pl.ds(24 * (1 - core), 24)] = theirs[...]
    for xp in range(2):
        def pair(ref):
            return jnp.concatenate(
                [ref[:, 16 * xp + 8 * i : 16 * xp + 8 * i + 8, :].reshape(384, 128) for i in range(2)], axis=1
            )
        blurred = along_z(kz, 0, *split(pair(full)))
        ratio = pair(seen) / blurred
        back = along_z(kz, 1, *split(ratio))
        for i in range(2):
            at = slice(16 * xp + 8 * i, 16 * xp + 8 * i + 8)
            full[:, at, :] = back[:, 128 * i : 128 * i + 128].reshape(48, 8, 128)
    keep[...] = full[pl.ds(24 * core, 24)]
    send[...] = full[pl.ds(24 * (1 - core), 24)]


def mirror_body(own, other, mats, odd_out, even_out, mid, mid_ext, sides, turned):
    tx = lax.axis_index("tx")
    parts = [split(ref[...].reshape(768, 128)) for ref in (own, other)]
    along_y = []
    for v in range(2):
        rows = slice(128 * v, 128 * v + 128)
        high = mats[YF, rows]
        along_y.append(
            split(
                dot(jnp.concatenate(parts[v], axis=1), jnp.concatenate([high, high]), NN)
                + dot(parts[v][0], mats[YF + 1, rows], NN)
            )
        )
    both_rows = mats[BT : BT + 2].reshape(512, 256)
    for g in range(6):
        z = slice(4 * g, 4 * g + 4)
        rows = slice(128 * g, 128 * g + 128)
        both = tuple(jnp.concatenate([along_y[0][i][rows], along_y[1][i][rows]], axis=0) for i in range(2))
        wide = rows3(both_rows, both).reshape(4, 64, 256)
        put_rims(wide[:, 0:16, 0:128], wide[:, 48:64, 0:128], even_out, odd_out, z)
        mid[z] = wide[:, 16:48, 0:128]
        sides[z] = wide[:, :, 128:256]
    cols = []
    for b in range(4):
        cols.append(pack_columns(sides[:, 16 * b : 16 * b + 16, :], 112 * tx, 16, turned))
    parts = [[c[:, 128 * t : 128 * t + 128] for t in range(3)] for c in cols]
    for t in range(3):
        put_rims(parts[0][t][None], parts[3][t][None], even_out, odd_out, slice(24 + t, 25 + t))
        mid_ext[t] = parts[1][t]
        mid_ext[3 + t] = parts[2][t]


def gather_body(mid, mid_ext, from_odd, from_even, sides_out, low_out, high_out, turned):
    tx = lax.axis_index("tx")
    odd = parity()
    above = jnp.where(odd, from_even[...], from_odd[...])
    below = jnp.where(odd, from_odd[...], from_even[...])
    for out, z in ((low_out, slice(0, 12)), (high_out, slice(12, 24))):
        out[:, 0:16, :] = mid[z, 0:16, :] + above[z]
        out[:, 16:32, :] = mid[z, 16:32, :] + below[z]
    sides_out[0:3] = mid_ext[0:3] + above[24:27]
    sides_out[3:6] = mid_ext[3:6] + below[24:27]
    if sides_out.shape[0] == 12:
        for xh in range(2):
            at = slice(16 * xh, 16 * xh + 16)
            both = jnp.concatenate([low_out[:, at, :], high_out[:, at, :]])
            put_packs(both, 112 * (1 - tx), 16, turned, sides_out, 6 + 3 * xh)


def join_body(mine, theirs, out):
    out[...] = mine[...] + theirs[...]


def new_estimate(side, low, high, p_low, p_high, cur, norm, cur_out, turned):
    tx = lax.axis_index("tx")
    turned[...] = jnp.zeros_like(turned)
    for xh in range(2):
        at = slice(16 * xh, 16 * xh + 16)
        parts = [side[3 * xh + t] for t in range(3)]
        edge = spread_columns(parts, 112 * (1 - tx), 16, turned).reshape(24, 16, 128)
        for mine, theirs, z in ((low, p_low, slice(0, 12)), (high, p_high, slice(12, 24))):
            total = mine[:, at, :] + theirs[:, at, :] + edge[z]
            cur_out[z, at, :] = cur[z, at, :] * total / norm[z, at, :]


def update_body(
    side, low, high, p_low, p_high, cur, norm, joined, ext, norm_ext, cur_out, ext_out, odd_out, even_out, turned
):
    new_estimate(side, low, high, p_low, p_high, cur, norm, cur_out, turned)
    ext_out[...] = ext[0:6] * (side[6:12] + joined[0:6]) / norm_ext[...]
    put_rims(cur_out[:, 0:16, :], cur_out[:, 16:32, :], even_out, odd_out, slice(0, 24))
    put_rims(ext_out[0:3], ext_out[3:6], even_out, odd_out, slice(24, 27))


def whole_body(mine, theirs, out, sems):
    core = mesh_core()
    copies = [
        pltpu.make_async_copy(part, out.at[pl.ds(24 * half, 24)], sems.at[i])
        for i, (part, half) in enumerate(((mine, core), (theirs, 1 - core)))
    ]
    for copy in copies:
        copy.start()
    for copy in copies:
        copy.wait()


def swap(value, axis, by, sizes):
    count = int(np.prod(sizes))
    return lax.ppermute(value, axis, [(i, i ^ by) for i in range(count)])


def rim_swap(odd, even):
    rows = lax.axis_size("ty")
    odd_pairs = [(i, i + 1) for i in range(1, rows - 1, 2)]
    odd_pairs += [(b, a) for a, b in odd_pairs]
    from_odd = lax.ppermute(odd, "ty", odd_pairs)
    from_even = lax.ppermute(even, "ty", [(i, i ^ 1) for i in range(rows)])
    return from_odd, from_even


def shards(raw_views, psf_taps, offsets, estimate):
    depth, tile_x, tile_y = estimate.shape
    half = depth // 2
    view = lax.axis_index("view")
    raw = raw_views[0]

    tile_half = ((half, tile_x, tile_y), F32)
    tile_quarter = ((half // 2, tile_x, tile_y), F32)
    pack = ((6, EDGE, 128), F32)
    rim = ((half + 3, EDGE, 128), F32)
    turned = pltpu.VMEM((128, 384), F32)
    two_sems = pltpu.SemaphoreType.DMA((2,))

    (ext,) = call(
        begin_body,
        [pack],
        [estimate],
        [pltpu.VMEM((half, tile_x, tile_y), F32), turned, pltpu.SemaphoreType.DMA],
        name="begin",
        hbm=(0,),
        limit=62,
    )
    ext = swap(ext, ("view", "tx"), 5, (4, 2))
    (sides,) = call(raw_sides_body, [((12, OMAX, 128), F32)], [raw], [turned], flops=BUSY, name="raw_sides")
    sides = swap(sides, "tx", 1, (2,))
    cur, odd, even = call(rims_body, [tile_half, rim, rim], [estimate], name="rims")

    kernels = psf_taps / jnp.sum(psf_taps, axis=-1, keepdims=True)
    own = lax.dynamic_index_in_dim(kernels, view, 0, keepdims=False)
    other = lax.dynamic_index_in_dim(kernels, view ^ 1, 0, keepdims=False)
    flat_psf = psf_taps.reshape(-1)
    kz, mats = bands(own, other, depth, flat_psf, offsets)
    extents = (tile_x * lax.axis_size("ty"), tile_y * lax.axis_size("tx"))
    norm, norm_ext = call(
        functools.partial(norm_body, extents), [tile_half, pack], [flat_psf, offsets], name="norm"
    )

    odd, even = call(corners_body, [rim, rim], [ext, odd, even], name="corners", aliases={1: 0, 2: 1})
    from_odd, from_even = rim_swap(odd, even)
    raw_rim = ((depth + 3, OMAX, 128), F32)
    raw_odd, raw_even = call(raw_rims_body, [raw_rim, raw_rim], [raw, sides], name="raw_rims")
    raw_from = rim_swap(raw_odd, raw_even)
    columns = [pltpu.VMEM((half, 32, 256), BF16), pltpu.VMEM((half, 32, 256), BF16), turned]
    seen = None

    for iteration in range(ITERS):
        inner = call(
            inner_body, [tile_half, tile_half], [cur, ext, mats], columns, flops=BUSY, name="inner"
        )
        mine, theirs = call(
            outer_body,
            [tile_half, tile_half],
            [from_odd, from_even, mats, *inner],
            columns,
            flops=BUSY,
            name="outer",
        )
        theirs = swap(theirs, "view", 1, (4,))
        if seen is None:
            (seen,) = call(
                register_body,
                [((depth, tile_x, tile_y), F32)],
                [offsets, raw, sides, *raw_from],
                [pltpu.VMEM((depth, tile_x + 2 * OMAX, 256), F32), turned],
                flops=BUSY,
                name="register",
            )
        keep, send = call(
            ratio_body,
            [tile_half, tile_half],
            [mine, theirs, seen, kz],
            [pltpu.VMEM((depth, tile_x, tile_y), F32)],
            flops=3 * 2 * 2 * 384 * 384 * 512,
            name="ratio",
        )
        send = swap(send, "view", 1, (4,))
        odd, even, mid, mid_ext = call(
            mirror_body,
            [rim, rim, tile_half, pack],
            [keep, send, mats],
            [pltpu.VMEM((half, 64, 128), F32), turned],
            flops=3 * 2 * (1536 * 128 * 256 + 6 * 256 * 256 * 256),
            name="mirror",
        )
        from_odd, from_even = rim_swap(odd, even)
        last = iteration == ITERS - 1
        sides, low, high = call(
            gather_body,
            [pack if last else ((12, EDGE, 128), F32), tile_quarter, tile_quarter],
            [mid, mid_ext, from_odd, from_even],
            [turned],
            name="gather",
        )
        theirs = swap(sides, "view", 2, (4,))
        p_low = swap(low, "view", 2, (4,))
        p_high = swap(high, "view", 2, (4,))
        (joined,) = call(join_body, [(sides.shape, F32)], [sides, theirs], flops=BUSY, name="join")
        side = swap(joined, ("view", "tx"), 5, (4, 2))
        if last:
            (cur,) = call(new_estimate, [tile_half], [side, low, high, p_low, p_high, cur, norm], [turned], name="last")
            break
        cur, ext, odd, even = call(
            update_body,
            [tile_half, pack, rim, rim],
            [side, low, high, p_low, p_high, cur, norm, joined, ext, norm_ext],
            [turned],
            name="update",
        )
        from_odd, from_even = rim_swap(odd, even)
    far = swap(cur, "view", 1, (4,))
    (out,) = call(whole_body, [((depth, tile_x, tile_y), F32)], [cur, far], [two_sems], name="whole", out_place=pl.ANY)
    return out


def solution(mesh):
    placed = (P("view", None, "ty", "tx"), P(), P(), P(None, "ty", "tx"))
    return jax.shard_map(
        shards, mesh=mesh, in_specs=placed, out_specs=P(None, "ty", "tx"), check_vma=False
    )
```

```python
import functools

import jax
import jax.numpy as jnp
import numpy as np
from jax import lax
from jax.experimental import pallas as pl
from jax.experimental.pallas import tpu as pltpu
from jax.sharding import PartitionSpec as P

OMAX = 8
ITERS = 2
TAPS = 31
HALF = 15
EDGE = 16
F32 = jnp.float32
BUSY = 6000000000
BF16 = jnp.bfloat16
highest = lax.Precision.HIGHEST

NN = (((1,), (0,)), ((), ()))


def split(value):
    high = value.astype(BF16)
    low = (value - high.astype(F32)).astype(BF16)
    return high, low


def dot(a, b, dims):
    return lax.dot_general(a, b, dims, preferred_element_type=F32)


def rows3(a, b):
    n = a.shape[0] // 2
    both = dot(a, b[0], NN)
    return both[:n] + (dot(a[:n], b[1], NN) + both[n:])


def call(body, outs, args, scratch=(), flops=0, name=None, hbm=(), limit=8, aliases=None, out_place=pltpu.VMEM):
    def place(i, a):
        if i in hbm:
            return pltpu.HBM
        return pltpu.SMEM if a.ndim == 1 or a.dtype == jnp.int32 else pltpu.VMEM

    specs = [pl.BlockSpec(memory_space=place(i, a)) for i, a in enumerate(args)]
    outs = [jax.ShapeDtypeStruct(*o) for o in outs]
    moved = sum(int(np.prod(a.shape)) * a.dtype.itemsize for a in list(args) + outs)
    return pl.pallas_call(
        body,
        out_shape=outs,
        in_specs=specs,
        out_specs=[pl.BlockSpec(memory_space=out_place)] * len(outs),
        scratch_shapes=list(scratch),
        input_output_aliases=aliases or {},
        compiler_params=pltpu.CompilerParams(vmem_limit_bytes=limit << 20),
        cost_estimate=pl.CostEstimate(flops=flops, bytes_accessed=moved, transcendentals=0),
        name=name,
    )(*args)


def toeplitz(row, rows, width, shift):
    wide = jnp.broadcast_to(row[:, :width], (rows, width))
    return pltpu.roll(wide, shift % width, 1, stride=1, stride_axis=0)


MATS = 10
YF, IN, OUT, BT, YT = 0, 2, 4, 6, 8


def bands_body(taps, psf, offsets, kz, mats):
    for m in range(2):
        high, low = split(toeplitz(taps[m : m + 1], 384, 512, 0)[:, :384])
        for third in range(3):
            rows = slice(128 * third, 128 * third + 128)
            kz[m, 256 * third : 256 * third + 128] = high[rows]
            kz[m, 256 * third + 128 : 256 * third + 256] = low[rows]
    lane = lax.broadcasted_iota(jnp.int32, (64, 256), 1)

    def between(band, first, count, rest):
        at = lane[: band.shape[0]]
        return jnp.where((at >= first) & (at < first + count), band, rest)

    for v in range(2):
        row = taps[2 + v : 3 + v]
        for p in range(4):
            at = 32 * p
            none = jnp.zeros((32, 256), F32)
            inner = between(toeplitz(row, 32, 256, at - HALF), at, 32, none)
            outer = between(toeplitz(row, 32, 256, at + 1), at, 16, none)
            outer = between(toeplitz(row, 32, 256, at - 2 * HALF - 1), at + 16, 16, outer)
            for m, band in ((IN + v, inner), (OUT + v, outer)):
                mats[m, at : at + 32], mats[m, 128 + at : 160 + at] = split(band)
        rows = slice(128 * v, 128 * v + 128)
        mats[0, rows], mats[1, rows] = split(toeplitz(taps[6 + v : 7 + v], 128, 256, -HALF))
        mats[YT, :, rows], mats[YT + 1, :, rows] = split(toeplitz(taps[8 + v : 9 + v], 256, 256, -HALF)[:, :128])
    for p in range(4):
        both = jnp.zeros((64, 256), F32)
        for v in range(2):
            at = 128 * v + 32 * p
            both = between(toeplitz(taps[4 + v : 5 + v], 64, 256, at - 2 * HALF - 1), at, 32, both)
        rims, at = jnp.concatenate([both[0:16], both[48:64]]), 32 * p
        mats[BT, at : at + 32], mats[BT, 128 + at : 160 + at] = split(rims)
        mats[BT + 1, at : at + 32], mats[BT + 1, 128 + at : 160 + at] = split(both[16:48])


def placing(width, step, start):
    place = np.zeros((TAPS, width), np.float32)
    for k in range(TAPS):
        place[k, (step * (k - start)) % width] = 1
    return place


def bands(own, other, planes, psf, offsets):
    nz = 8 * planes
    z_rows = jnp.dot(jnp.stack([own[0], own[0, ::-1]]), placing(512, 8, HALF), precision=highest)
    rows = jnp.stack([own[1], other[1], own[1, ::-1], other[1, ::-1], own[2], other[2], own[2, ::-1], other[2, ::-1]])
    taps = jnp.concatenate([z_rows, jnp.pad(rows, ((0, 0), (0, 512 - TAPS)))])
    return call(bands_body, [((2, 2 * nz, nz), BF16), ((MATS, 256, 256), BF16)], [taps, psf, offsets], name="bands")


def pack_columns(value, at, width, scratch):
    flat = value.reshape(value.shape[0] * value.shape[1], 128)
    scratch[...] = flat.T
    return scratch[pl.ds(pl.multiple_of(at, 8), width), :]


def spread_columns(pack, at, width, scratch):
    for t, part in enumerate(pack):
        scratch[pl.ds(pl.multiple_of(at, 8), width), 128 * t : 128 * t + 128] = part
    return scratch[...].T


def norm_body(shape, psf, offsets, norm, norm_ext):
    nx, ny = shape
    views = offsets.shape[0]
    core = lax.axis_index("view") % 2
    x_first = 32 * lax.axis_index("ty")
    tx = lax.axis_index("tx")

    def iota(shape, dim):
        return lax.broadcasted_iota(jnp.int32, shape, dim)

    lane = iota((8, 128), 1)
    tile = jnp.minimum(iota((8, 128), 0), 2)
    places = (
        (0, 24 * core + iota((24, 128), 0)),
        (0, 24 * core + (128 * tile + lane) // EDGE),
        (1, x_first + iota((32, 128), 0)),
        (1, x_first + EDGE * (iota((8, 128), 0) % 2) + lane % EDGE),
        (2, 128 * tx + lane),
        (2, 128 - EDGE * tx + iota((EDGE, 128), 0)),
    )
    extents = (48, nx, ny)
    norm[...] = jnp.zeros_like(norm)
    norm_ext[...] = jnp.zeros_like(norm_ext)

    def one_view(v, _):
        shifts = (0, offsets[v, 0], offsets[v, 1])

        def one_tap(i, carry):
            totals, weights = carry
            taps = [psf[(v * 3 + dim) * TAPS + TAPS - 1 - i] for dim in range(3)]
            new = []
            for (dim, place), total in zip(places, totals):
                at = place + (i - HALF)
                moved = at + shifts[dim]
                inside = (at >= 0) & (at < extents[dim]) & (moved >= 0) & (moved < extents[dim])
                new.append(total + jnp.where(inside, taps[dim], 0.0))
            return tuple(new), tuple(w + t for w, t in zip(weights, taps))

        none = tuple(jnp.zeros(place.shape, F32) for _, place in places)
        totals, weights = lax.fori_loop(0, TAPS, one_tap, (none, (0.0, 0.0, 0.0)))
        in_z, z_row, in_x, x_row, in_y, in_e = (t / weights[dim] for t, (dim, _) in zip(totals, places))
        xy = in_x * in_y[0:1]
        for z in range(24):
            norm[z] += in_z[z : z + 1] * xy
        for k in range(6):
            norm_ext[k] += in_e * (z_row[k % 3 : k % 3 + 1] * x_row[k // 3 : k // 3 + 1])
        return 0

    lax.fori_loop(0, offsets.shape[0], one_view, 0)


def mesh_core():
    return lax.axis_index("view") % 2


def parity():
    return lax.axis_index("ty") % 2 == 1


def put_packs(value, at, width, turned, out, first):
    cols = pack_columns(value, at, width, turned)
    for t in range(3):
        out[first + t] = cols[:, 128 * t : 128 * t + 128]


def begin_body(est, pack_out, cur, turned, sem):
    tx = lax.axis_index("tx")
    copy = pltpu.make_async_copy(est.at[pl.ds(24 * mesh_core(), 24)], cur, sem)
    copy.start()
    copy.wait()
    for xh in range(2):
        put_packs(cur[:, 16 * xh : 16 * xh + 16, :], 112 * (1 - tx), 16, turned, pack_out, 3 * xh)


def raw_sides_body(raw, pack_out, turned):
    tx = lax.axis_index("tx")
    for xb in range(4):
        put_packs(raw[:, 8 * xb : 8 * xb + 8, :], 120 * (1 - tx), 8, turned, pack_out, 3 * xb)


def put_rims(top, bottom, even_out, odd_out, planes):
    odd = parity()
    even_out[planes] = jnp.where(odd, top, bottom)
    odd_out[planes] = jnp.where(odd, bottom, top)


def rims_body(est, cur_out, odd_out, even_out):
    cur_out[...] = est[pl.ds(24 * mesh_core(), 24)]
    put_rims(cur_out[:, 0:16, :], cur_out[:, 16:32, :], even_out, odd_out, slice(0, 24))
    odd_out[24:27] = jnp.zeros((3, 16, 128), F32)
    even_out[24:27] = jnp.zeros((3, 16, 128), F32)


def corners_body(pack, odd_in, even_in, odd_out, even_out):
    put_rims(pack[0:3], pack[3:6], even_out, odd_out, slice(24, 27))


def raw_rims_body(raw, pack, odd_out, even_out):
    put_rims(raw[:, 0:8, :], raw[:, 24:32, :], even_out, odd_out, slice(0, 48))
    for t in range(3):
        put_rims(pack[t][None], pack[9 + t][None], even_out, odd_out, slice(48 + t, 49 + t))


def register_columns_body(offsets, raw, pack, after, out, wide, turned):
    view, tx = lax.axis_index("view"), lax.axis_index("tx")
    sy = offsets[view, 1]
    wide[:, :, 0:128] = raw[...]
    turned[...] = jnp.zeros_like(turned)
    for b in range(4):
        parts = [pack[3 * b + t] for t in range(3)]
        wide[:, 8 * b : 8 * b + 8, 128:256] = spread_columns(parts, 120 * tx, 8, turned).reshape(48, 8, 128)
    for z in range(0, 48, 4):
        out[z : z + 4] = pltpu.roll(wide[z : z + 4], lax.rem(256 - sy, 256), 2)[:, :, 0:128]


def register_body(offsets, moved, from_odd, from_even, out, wide, turned):
    view, tx = lax.axis_index("view"), lax.axis_index("tx")
    sx, sy = offsets[view, 0], offsets[view, 1]
    odd = parity()
    above = jnp.where(odd, from_even[...], from_odd[...])
    below = jnp.where(odd, from_odd[...], from_even[...])
    turned[...] = jnp.zeros_like(turned)
    wide[:, 8:40, :] = moved[...]
    for rim, rows in ((above, slice(0, 8)), (below, slice(40, 48))):
        side = spread_columns([rim[48 + t] for t in range(3)], 120 * tx, 8, turned).reshape(48, 8, 128)
        both = jnp.concatenate([rim[0:48], side], axis=2)
        wide[:, rows, :] = pltpu.roll(both, lax.rem(256 - sy, 256), 2)[:, :, 0:128]
    for z in range(0, 48, 8):
        out[z : z + 8] = pltpu.roll(wide[z : z + 8], lax.rem(40 - sx, 48), 1)[:, 0:32, :]


def put_columns(rows, main, rim, tx, x_h, x_l, turned):
    x_h[:, rows, 0:128], x_l[:, rows, 0:128] = split(main)
    side = spread_columns(rim, 112 * tx, 16, turned).reshape(24, 16, 128)
    x_h[:, rows, 128:256], x_l[:, rows, 128:256] = split(side)


def blur_rows(x_h, x_l, yf, bx, g):
    z = slice(4 * g, 4 * g + 4)
    high, low = x_h[z].reshape(128, 256), x_l[z].reshape(128, 256)
    along_y = split(dot(high, yf[0], NN) + (dot(high, yf[1], NN) + dot(low, yf[0], NN)))
    for v in range(2):
        cols = slice(128 * v, 128 * v + 128)
        yield v, z, rows3(bx[v][:, 0:128], (along_y[0][:, cols], along_y[1][:, cols])).reshape(4, 32, 128)


def inner_body(cur, ext, mats, own, other, x_h, x_l, turned):
    tx = lax.axis_index("tx")
    turned[...] = jnp.zeros_like(turned)
    for xh in range(2):
        rows = slice(16 * xh, 16 * xh + 16)
        put_columns(rows, cur[:, rows, :], [ext[3 * xh + t] for t in range(3)], tx, x_h, x_l, turned)
    for g in range(6):
        for v, z, part in blur_rows(x_h, x_l, (mats[YT], mats[YT + 1]), (mats[IN], mats[IN + 1]), g):
            (own, other)[v][z] = part


def outer_body(from_odd, from_even, mats, in_own, in_other, own, other, x_h, x_l, turned):
    tx = lax.axis_index("tx")
    odd = parity()
    above = jnp.where(odd, from_even[...], from_odd[...])
    below = jnp.where(odd, from_odd[...], from_even[...])
    turned[...] = jnp.zeros_like(turned)
    for xh, rim in ((0, above), (1, below)):
        rows = slice(16 * xh, 16 * xh + 16)
        put_columns(rows, rim[0:24], [rim[24 + t] for t in range(3)], tx, x_h, x_l, turned)
    for g in range(6):
        for v, z, part in blur_rows(x_h, x_l, (mats[YT], mats[YT + 1]), (mats[OUT], mats[OUT + 1]), g):
            (own, other)[v][z] = (in_own, in_other)[v][z] + part


def along_z(kz, m, high, low):
    parts = []
    for third, reach in ((0, slice(0, 256)), (1, slice(0, 384)), (2, slice(128, 384))):
        parts.append(rows3(kz[m, 256 * third : 256 * third + 256, reach], (high[reach], low[reach])))
    return jnp.concatenate(parts)


def ratio_body(mine, theirs, seen, kz, keep, send, full):
    core = mesh_core()
    full[pl.ds(24 * core, 24)] = mine[...]
    full[pl.ds(24 * (1 - core), 24)] = theirs[...]
    for xp in range(2):
        def pair(ref):
            return jnp.concatenate(
                [ref[:, 16 * xp + 8 * i : 16 * xp + 8 * i + 8, :].reshape(384, 128) for i in range(2)], axis=1
            )
        blurred = along_z(kz, 0, *split(pair(full)))
        ratio = pair(seen) / blurred
        back = along_z(kz, 1, *split(ratio))
        for i in range(2):
            at = slice(16 * xp + 8 * i, 16 * xp + 8 * i + 8)
            full[:, at, :] = back[:, 128 * i : 128 * i + 128].reshape(48, 8, 128)
    keep[...] = full[pl.ds(24 * core, 24)]
    send[...] = full[pl.ds(24 * (1 - core), 24)]


def put_sides(sides, tx, turned, put):
    for xh in range(2):
        cols = pack_columns(sides[:, 16 * xh : 16 * xh + 16, :], 112 * tx, 16, turned)
        for t in range(3):
            put(xh, t, cols[:, 128 * t : 128 * t + 128])


def spread_rows(band, y_h, y_l, g):
    rows = slice(128 * g, 128 * g + 128)
    both = tuple(jnp.concatenate([y[0, rows], y[1, rows]], axis=0) for y in (y_h, y_l))
    return rows3(band, both).reshape(4, 32, 256)


def mirror_rims_body(own, other, mats, odd_out, even_out, y_h, y_l, sides, turned):
    tx = lax.axis_index("tx")
    for v, ref in ((0, own), (1, other)):
        high, low = split(ref[...].reshape(768, 128))
        rows = slice(128 * v, 128 * v + 128)
        band = mats[YF, rows]
        y_h[v], y_l[v] = split(
            dot(jnp.concatenate([high, low], axis=1), jnp.concatenate([band, band]), NN)
            + dot(high, mats[YF + 1, rows], NN)
        )
    for g in range(6):
        z = slice(4 * g, 4 * g + 4)
        wide = spread_rows(mats[BT], y_h, y_l, g)
        put_rims(wide[:, 0:16, 0:128], wide[:, 16:32, 0:128], even_out, odd_out, z)
        sides[z] = wide[:, :, 128:256]
    parts = {}
    put_sides(sides, tx, turned, lambda xh, t, cols: parts.update({(xh, t): cols}))
    for t in range(3):
        put_rims(parts[0, t][None], parts[1, t][None], even_out, odd_out, slice(24 + t, 25 + t))


def mirror_body(y_h, y_l, mats, mid, mid_ext, sides, turned):
    for g in range(6):
        z = slice(4 * g, 4 * g + 4)
        wide = spread_rows(mats[BT + 1], y_h, y_l, g)
        mid[z] = wide[:, :, 0:128]
        sides[z] = wide[:, :, 128:256]

    def put(xh, t, cols):
        mid_ext[3 * xh + t] = cols

    put_sides(sides, lax.axis_index("tx"), turned, put)


def gather_body(mid, mid_ext, from_odd, from_even, sides_out, low_out, high_out, turned):
    tx = lax.axis_index("tx")
    odd = parity()
    above = jnp.where(odd, from_even[...], from_odd[...])
    below = jnp.where(odd, from_odd[...], from_even[...])
    for out, z in ((low_out, slice(0, 12)), (high_out, slice(12, 24))):
        out[:, 0:16, :] = mid[z, 0:16, :] + above[z]
        out[:, 16:32, :] = mid[z, 16:32, :] + below[z]
    sides_out[0:3] = mid_ext[0:3] + above[24:27]
    sides_out[3:6] = mid_ext[3:6] + below[24:27]
    if sides_out.shape[0] == 12:
        for xh in range(2):
            at = slice(16 * xh, 16 * xh + 16)
            both = jnp.concatenate([low_out[:, at, :], high_out[:, at, :]])
            put_packs(both, 112 * (1 - tx), 16, turned, sides_out, 6 + 3 * xh)


def join_body(mine, theirs, out):
    out[...] = mine[...] + theirs[...]


def new_estimate(side, low, high, p_low, p_high, cur, norm, cur_out, turned):
    tx = lax.axis_index("tx")
    turned[...] = jnp.zeros_like(turned)
    for xh in range(2):
        at = slice(16 * xh, 16 * xh + 16)
        parts = [side[3 * xh + t] for t in range(3)]
        edge = spread_columns(parts, 112 * (1 - tx), 16, turned).reshape(24, 16, 128)
        for mine, theirs, z in ((low, p_low, slice(0, 12)), (high, p_high, slice(12, 24))):
            total = mine[:, at, :] + theirs[:, at, :] + edge[z]
            cur_out[z, at, :] = cur[z, at, :] * total / norm[z, at, :]


def update_body(
    side, low, high, p_low, p_high, cur, norm, joined, ext, norm_ext, cur_out, ext_out, odd_out, even_out, turned
):
    new_estimate(side, low, high, p_low, p_high, cur, norm, cur_out, turned)
    ext_out[...] = ext[0:6] * (side[6:12] + joined[0:6]) / norm_ext[...]
    put_rims(cur_out[:, 0:16, :], cur_out[:, 16:32, :], even_out, odd_out, slice(0, 24))
    put_rims(ext_out[0:3], ext_out[3:6], even_out, odd_out, slice(24, 27))


def whole_body(mine, theirs, out, sems):
    core = mesh_core()
    copies = [
        pltpu.make_async_copy(part, out.at[pl.ds(24 * half, 24)], sems.at[i])
        for i, (part, half) in enumerate(((mine, core), (theirs, 1 - core)))
    ]
    for copy in copies:
        copy.start()
    for copy in copies:
        copy.wait()


def swap(value, axis, by, sizes):
    count = int(np.prod(sizes))
    return lax.ppermute(value, axis, [(i, i ^ by) for i in range(count)])


def rim_swap(odd, even):
    rows = lax.axis_size("ty")
    odd_pairs = [(i, i + 1) for i in range(1, rows - 1, 2)]
    odd_pairs += [(b, a) for a, b in odd_pairs]
    from_odd = lax.ppermute(odd, "ty", odd_pairs)
    from_even = lax.ppermute(even, "ty", [(i, i ^ 1) for i in range(rows)])
    return from_odd, from_even


def shards(raw_views, psf_taps, offsets, estimate):
    depth, tile_x, tile_y = estimate.shape
    half = depth // 2
    view = lax.axis_index("view")
    raw = raw_views[0]

    tile_half = ((half, tile_x, tile_y), F32)
    tile_quarter = ((half // 2, tile_x, tile_y), F32)
    pack = ((6, EDGE, 128), F32)
    rim = ((half + 3, EDGE, 128), F32)
    turned = pltpu.VMEM((128, 384), F32)
    two_sems = pltpu.SemaphoreType.DMA((2,))

    (ext,) = call(
        begin_body,
        [pack],
        [estimate],
        [pltpu.VMEM((half, tile_x, tile_y), F32), turned, pltpu.SemaphoreType.DMA],
        name="begin",
        hbm=(0,),
        limit=62,
    )
    ext = swap(ext, ("view", "tx"), 5, (4, 2))
    (sides,) = call(raw_sides_body, [((12, OMAX, 128), F32)], [raw], [turned], flops=BUSY, name="raw_sides")
    sides = swap(sides, "tx", 1, (2,))
    cur, odd, even = call(rims_body, [tile_half, rim, rim], [estimate], name="rims")

    odd, even = call(corners_body, [rim, rim], [ext, odd, even], name="corners", aliases={1: 0, 2: 1})
    late_taps, late_offsets, _ = lax.optimization_barrier((psf_taps, offsets, odd))
    kernels = late_taps / jnp.sum(late_taps, axis=-1, keepdims=True)
    own = lax.dynamic_index_in_dim(kernels, view, 0, keepdims=False)
    other = lax.dynamic_index_in_dim(kernels, view ^ 1, 0, keepdims=False)
    flat_psf = late_taps.reshape(-1)
    kz, mats = bands(own, other, depth, flat_psf, late_offsets)
    extents = (tile_x * lax.axis_size("ty"), tile_y * lax.axis_size("tx"))
    norm, norm_ext = call(
        functools.partial(norm_body, extents), [tile_half, pack], [flat_psf, late_offsets], name="norm"
    )

    from_odd, from_even = rim_swap(odd, even)
    raw_rim = ((depth + 3, OMAX, 128), F32)
    raw_odd, raw_even = call(raw_rims_body, [raw_rim, raw_rim], [raw, sides], name="raw_rims")
    raw_from = rim_swap(raw_odd, raw_even)
    columns = [pltpu.VMEM((half, 32, 256), BF16), pltpu.VMEM((half, 32, 256), BF16), turned]
    seen = None

    for iteration in range(ITERS):
        inner = call(
            inner_body, [tile_half, tile_half], [cur, ext, mats], columns, flops=BUSY, name="inner"
        )
        mine, theirs = call(
            outer_body,
            [tile_half, tile_half],
            [from_odd, from_even, mats, *inner],
            columns,
            flops=BUSY,
            name="outer",
        )
        theirs = swap(theirs, "view", 1, (4,))
        if seen is None:
            whole = ((depth, tile_x, tile_y), F32)
            (moved,) = call(
                register_columns_body,
                [whole],
                [late_offsets, raw, sides, mine],
                [pltpu.VMEM((depth, tile_x, 256), F32), turned],
                flops=BUSY,
                name="register_columns",
            )
            (seen,) = call(
                register_body,
                [whole],
                [late_offsets, moved, *raw_from],
                [pltpu.VMEM((depth, tile_x + 2 * OMAX, 128), F32), turned],
                flops=BUSY,
                name="register",
            )
        keep, send = call(
            ratio_body,
            [tile_half, tile_half],
            [mine, theirs, seen, kz],
            [pltpu.VMEM((depth, tile_x, tile_y), F32)],
            flops=3 * 2 * 2 * 384 * 384 * 512,
            name="ratio",
        )
        send = swap(send, "view", 1, (4,))
        along_y = ((2, 768, 256), BF16)
        odd, even, y_h, y_l = call(
            mirror_rims_body,
            [rim, rim, along_y, along_y],
            [keep, send, mats],
            [pltpu.VMEM((half, 32, 128), F32), turned],
            name="mirror_rims",
        )
        mid, mid_ext = call(
            mirror_body,
            [tile_half, pack],
            [y_h, y_l, mats],
            [pltpu.VMEM((half, 32, 128), F32), turned],
            flops=BUSY,
            name="mirror",
        )
        from_odd, from_even = rim_swap(odd, even)
        last = iteration == ITERS - 1
        sides, low, high = call(
            gather_body,
            [pack if last else ((12, EDGE, 128), F32), tile_quarter, tile_quarter],
            [mid, mid_ext, from_odd, from_even],
            [turned],
            name="gather",
        )
        theirs = swap(sides, "view", 2, (4,))
        p_low = swap(low, "view", 2, (4,))
        p_high = swap(high, "view", 2, (4,))
        (joined,) = call(join_body, [(sides.shape, F32)], [sides, theirs], flops=BUSY, name="join")
        side = swap(joined, ("view", "tx"), 5, (4, 2))
        if last:
            (cur,) = call(new_estimate, [tile_half], [side, low, high, p_low, p_high, cur, norm], [turned], name="last")
            break
        cur, ext, odd, even = call(
            update_body,
            [tile_half, pack, rim, rim],
            [side, low, high, p_low, p_high, cur, norm, joined, ext, norm_ext],
            [turned],
            name="update",
        )
        from_odd, from_even = rim_swap(odd, even)
    far = swap(cur, "view", 1, (4,))
    (out,) = call(whole_body, [((depth, tile_x, tile_y), F32)], [cur, far], [two_sems], name="whole", out_place=pl.ANY)
    return out


def solution(mesh):
    placed = (P("view", None, "ty", "tx"), P(), P(), P(None, "ty", "tx"))
    return jax.shard_map(
        shards, mesh=mesh, in_specs=placed, out_specs=P(None, "ty", "tx"), check_vma=False
    )
```

```python
import functools

import jax
import jax.numpy as jnp
import numpy as np
from jax import lax
from jax.experimental import pallas as pl
from jax.experimental.pallas import tpu as pltpu
from jax.sharding import PartitionSpec as P

OMAX = 8
ITERS = 2
TAPS = 31
HALF = 15
EDGE = 16
F32 = jnp.float32
BUSY = 6000000000
BF16 = jnp.bfloat16
highest = lax.Precision.HIGHEST

NN = (((1,), (0,)), ((), ()))


def split(value):
    high = value.astype(BF16)
    low = (value - high.astype(F32)).astype(BF16)
    return high, low


def dot(a, b, dims):
    return lax.dot_general(a, b, dims, preferred_element_type=F32)


def rows3(a, b):
    n = a.shape[0] // 2
    both = dot(a, b[0], NN)
    return both[:n] + (dot(a[:n], b[1], NN) + both[n:])


def call(body, outs, args, scratch=(), flops=0, name=None, hbm=(), limit=8, aliases=None, out_place=pltpu.VMEM):
    def place(i, a):
        if i in hbm:
            return pltpu.HBM
        return pltpu.SMEM if a.ndim == 1 or a.dtype == jnp.int32 else pltpu.VMEM

    specs = [pl.BlockSpec(memory_space=place(i, a)) for i, a in enumerate(args)]
    outs = [jax.ShapeDtypeStruct(*o) for o in outs]
    moved = sum(int(np.prod(a.shape)) * a.dtype.itemsize for a in list(args) + outs)
    return pl.pallas_call(
        body,
        out_shape=outs,
        in_specs=specs,
        out_specs=[pl.BlockSpec(memory_space=out_place)] * len(outs),
        scratch_shapes=list(scratch),
        input_output_aliases=aliases or {},
        compiler_params=pltpu.CompilerParams(vmem_limit_bytes=limit << 20),
        cost_estimate=pl.CostEstimate(flops=flops, bytes_accessed=moved, transcendentals=0),
        name=name,
    )(*args)


def toeplitz(row, rows, width, shift):
    wide = jnp.broadcast_to(row[:, :width], (rows, width))
    return pltpu.roll(wide, shift % width, 1, stride=1, stride_axis=0)


MATS = 10
YF, IN, OUT, BT, YT = 0, 2, 4, 6, 8


def bands_body(taps, place, psf, offsets, kz, mats, placed):
    view = lax.axis_index("view")
    views = (view, view + 1 - 2 * (view % 2))
    total = jnp.sum(taps[...], axis=1, keepdims=True)
    rest = taps[...] / jnp.where(total > 0, total, 1.0)
    placed[...] = jnp.zeros_like(placed)
    for _ in range(3):
        part = rest.astype(BF16)
        placed[...] += dot(part, place[...], NN)
        rest = rest - part.astype(F32)

    def row(v, dim, kind):
        return placed[pl.ds(3 * views[v] + dim, 1), 512 * kind : 512 * kind + 512]

    for m in range(2):
        high, low = split(toeplitz(row(0, 0, m), 384, 512, 0)[:, :384])
        for third in range(3):
            rows = slice(128 * third, 128 * third + 128)
            kz[m, 256 * third : 256 * third + 128] = high[rows]
            kz[m, 256 * third + 128 : 256 * third + 256] = low[rows]
    lane = lax.broadcasted_iota(jnp.int32, (64, 256), 1)

    def between(band, first, count, rest):
        at = lane[: band.shape[0]]
        return jnp.where((at >= first) & (at < first + count), band, rest)

    for v in range(2):
        taps_x = row(v, 1, 2)
        for p in range(4):
            at = 32 * p
            none = jnp.zeros((32, 256), F32)
            inner = between(toeplitz(taps_x, 32, 256, at - HALF), at, 32, none)
            outer = between(toeplitz(taps_x, 32, 256, at + 1), at, 16, none)
            outer = between(toeplitz(taps_x, 32, 256, at - 2 * HALF - 1), at + 16, 16, outer)
            for m, band in ((IN + v, inner), (OUT + v, outer)):
                mats[m, at : at + 32], mats[m, 128 + at : 160 + at] = split(band)
        rows = slice(128 * v, 128 * v + 128)
        mats[0, rows], mats[1, rows] = split(toeplitz(row(v, 2, 2), 128, 256, -HALF))
        mats[YT, :, rows], mats[YT + 1, :, rows] = split(toeplitz(row(v, 2, 3), 256, 256, -HALF)[:, :128])
    for p in range(4):
        both = jnp.zeros((64, 256), F32)
        for v in range(2):
            at = 128 * v + 32 * p
            both = between(toeplitz(row(v, 1, 3), 64, 256, at - 2 * HALF - 1), at, 32, both)
        rims, at = jnp.concatenate([both[0:16], both[48:64]]), 32 * p
        mats[BT, at : at + 32], mats[BT, 128 + at : 160 + at] = split(rims)
        mats[BT + 1, at : at + 32], mats[BT + 1, 128 + at : 160 + at] = split(both[16:48])


def placing():
    place = np.zeros((TAPS + 1, 4, 512), np.float32)
    for k in range(TAPS):
        for kind, at in enumerate((8 * (k - HALF), 8 * (HALF - k), k, TAPS - 1 - k)):
            place[k, kind, at % 512] = 1
    return jnp.asarray(place.reshape(TAPS + 1, 2048), BF16)


def bands(taps, planes, psf, offsets):
    nz = 8 * planes
    return call(
        bands_body,
        [((2, 2 * nz, nz), BF16), ((MATS, 256, 256), BF16)],
        [taps, placing(), psf, offsets],
        [pltpu.VMEM((16, 2048), F32)],
        flops=BUSY,
        name="bands",
    )


def pack_columns(value, at, width, scratch):
    flat = value.reshape(value.shape[0] * value.shape[1], 128)
    scratch[...] = flat.T
    return scratch[pl.ds(pl.multiple_of(at, 8), width), :]


def spread_columns(pack, at, width, scratch):
    for t, part in enumerate(pack):
        scratch[pl.ds(pl.multiple_of(at, 8), width), 128 * t : 128 * t + 128] = part
    return scratch[...].T


def norm_body(shape, psf, offsets, after, norm, norm_ext):
    nx, ny = shape
    views = offsets.shape[0]
    core = lax.axis_index("view") % 2
    x_first = 32 * lax.axis_index("ty")
    tx = lax.axis_index("tx")

    def iota(shape, dim):
        return lax.broadcasted_iota(jnp.int32, shape, dim)

    lane = iota((8, 128), 1)
    tile = jnp.minimum(iota((8, 128), 0), 2)
    places = (
        (0, 24 * core + iota((24, 128), 0)),
        (0, 24 * core + (128 * tile + lane) // EDGE),
        (1, x_first + iota((32, 128), 0)),
        (1, x_first + EDGE * (iota((8, 128), 0) % 2) + lane % EDGE),
        (2, 128 * tx + lane),
        (2, 128 - EDGE * tx + iota((EDGE, 128), 0)),
    )
    extents = (48, nx, ny)
    norm[...] = jnp.zeros_like(norm)
    norm_ext[...] = jnp.zeros_like(norm_ext)

    def one_view(v, _):
        shifts = (0, offsets[v, 0], offsets[v, 1])

        def one_tap(i, carry):
            totals, weights = carry
            taps = [psf[(v * 3 + dim) * TAPS + TAPS - 1 - i] for dim in range(3)]
            new = []
            for (dim, place), total in zip(places, totals):
                at = place + (i - HALF)
                moved = at + shifts[dim]
                inside = (at >= 0) & (at < extents[dim]) & (moved >= 0) & (moved < extents[dim])
                new.append(total + jnp.where(inside, taps[dim], 0.0))
            return tuple(new), tuple(w + t for w, t in zip(weights, taps))

        none = tuple(jnp.zeros(place.shape, F32) for _, place in places)
        totals, weights = lax.fori_loop(0, TAPS, one_tap, (none, (0.0, 0.0, 0.0)))
        in_z, z_row, in_x, x_row, in_y, in_e = (t / weights[dim] for t, (dim, _) in zip(totals, places))
        xy = in_x * in_y[0:1]
        for z in range(24):
            norm[z] += in_z[z : z + 1] * xy
        for k in range(6):
            norm_ext[k] += in_e * (z_row[k % 3 : k % 3 + 1] * x_row[k // 3 : k // 3 + 1])
        return 0

    lax.fori_loop(0, offsets.shape[0], one_view, 0)


def mesh_core():
    return lax.axis_index("view") % 2


def parity():
    return lax.axis_index("ty") % 2 == 1


def put_packs(value, at, width, turned, out, first):
    cols = pack_columns(value, at, width, turned)
    for t in range(3):
        out[first + t] = cols[:, 128 * t : 128 * t + 128]


def begin_body(est, pack_out, turned):
    tx = lax.axis_index("tx")
    half = pl.ds(24 * mesh_core(), 24)
    for xh in range(2):
        put_packs(est[half, 16 * xh : 16 * xh + 16, :], 112 * (1 - tx), 16, turned, pack_out, 3 * xh)


def raw_sides_body(raw, pack_out, turned):
    tx = lax.axis_index("tx")
    for xb in range(4):
        put_packs(raw[:, 8 * xb : 8 * xb + 8, :], 120 * (1 - tx), 8, turned, pack_out, 3 * xb)


def put_rims(top, bottom, even_out, odd_out, planes):
    odd = parity()
    even_out[planes] = jnp.where(odd, top, bottom)
    odd_out[planes] = jnp.where(odd, bottom, top)


def rims_body(est, cur_out, odd_out, even_out):
    cur_out[...] = est[pl.ds(24 * mesh_core(), 24)]
    put_rims(cur_out[:, 0:16, :], cur_out[:, 16:32, :], even_out, odd_out, slice(0, 24))
    odd_out[24:27] = jnp.zeros((3, 16, 128), F32)
    even_out[24:27] = jnp.zeros((3, 16, 128), F32)


def corners_body(pack, odd_in, even_in, odd_out, even_out):
    put_rims(pack[0:3], pack[3:6], even_out, odd_out, slice(24, 27))


def raw_rims_body(raw, pack, after, odd_out, even_out):
    put_rims(raw[:, 0:8, :], raw[:, 24:32, :], even_out, odd_out, slice(0, 48))
    for t in range(3):
        put_rims(pack[t][None], pack[9 + t][None], even_out, odd_out, slice(48 + t, 49 + t))


def register_columns_body(offsets, raw, pack, after, out, wide, turned):
    view, tx = lax.axis_index("view"), lax.axis_index("tx")
    sy = offsets[view, 1]
    wide[:, :, 0:128] = raw[...]
    turned[...] = jnp.zeros_like(turned)
    for b in range(4):
        parts = [pack[3 * b + t] for t in range(3)]
        wide[:, 8 * b : 8 * b + 8, 128:256] = spread_columns(parts, 120 * tx, 8, turned).reshape(48, 8, 128)
    for z in range(0, 48, 4):
        out[z : z + 4] = pltpu.roll(wide[z : z + 4], lax.rem(256 - sy, 256), 2)[:, :, 0:128]


def register_body(offsets, moved, from_odd, from_even, out, wide, turned):
    view, tx = lax.axis_index("view"), lax.axis_index("tx")
    sx, sy = offsets[view, 0], offsets[view, 1]
    odd = parity()
    above = jnp.where(odd, from_even[...], from_odd[...])
    below = jnp.where(odd, from_odd[...], from_even[...])
    turned[...] = jnp.zeros_like(turned)
    wide[:, 8:40, :] = moved[...]
    for rim, rows in ((above, slice(0, 8)), (below, slice(40, 48))):
        side = spread_columns([rim[48 + t] for t in range(3)], 120 * tx, 8, turned).reshape(48, 8, 128)
        both = jnp.concatenate([rim[0:48], side], axis=2)
        wide[:, rows, :] = pltpu.roll(both, lax.rem(256 - sy, 256), 2)[:, :, 0:128]
    out[...] = wide[:, pl.ds(8 + sx, 32), :]


def put_columns(rows, main, rim, tx, x_h, x_l, turned):
    x_h[:, rows, 0:128], x_l[:, rows, 0:128] = split(main)
    side = spread_columns(rim, 112 * tx, 16, turned).reshape(24, 16, 128)
    x_h[:, rows, 128:256], x_l[:, rows, 128:256] = split(side)


def blur_rows(x_h, x_l, yf, bx, g):
    z = slice(4 * g, 4 * g + 4)
    high, low = x_h[z].reshape(128, 256), x_l[z].reshape(128, 256)
    along_y = split(dot(high, yf[0], NN) + (dot(high, yf[1], NN) + dot(low, yf[0], NN)))
    for v in range(2):
        cols = slice(128 * v, 128 * v + 128)
        yield v, z, rows3(bx[v][:, 0:128], (along_y[0][:, cols], along_y[1][:, cols])).reshape(4, 32, 128)


def inner_body(cur, ext, mats, own, other, x_h, x_l, turned):
    tx = lax.axis_index("tx")
    turned[...] = jnp.zeros_like(turned)
    for xh in range(2):
        rows = slice(16 * xh, 16 * xh + 16)
        put_columns(rows, cur[:, rows, :], [ext[3 * xh + t] for t in range(3)], tx, x_h, x_l, turned)
    for g in range(6):
        for v, z, part in blur_rows(x_h, x_l, (mats[YT], mats[YT + 1]), (mats[IN], mats[IN + 1]), g):
            (own, other)[v][z] = part


def outer_body(from_odd, from_even, mats, in_own, in_other, own, other, x_h, x_l, turned):
    tx = lax.axis_index("tx")
    odd = parity()
    above = jnp.where(odd, from_even[...], from_odd[...])
    below = jnp.where(odd, from_odd[...], from_even[...])
    turned[...] = jnp.zeros_like(turned)
    for xh, rim in ((0, above), (1, below)):
        rows = slice(16 * xh, 16 * xh + 16)
        put_columns(rows, rim[0:24], [rim[24 + t] for t in range(3)], tx, x_h, x_l, turned)
    for g in range(6):
        for v, z, part in blur_rows(x_h, x_l, (mats[YT], mats[YT + 1]), (mats[OUT], mats[OUT + 1]), g):
            (own, other)[v][z] = (in_own, in_other)[v][z] + part


def along_z(kz, m, high, low):
    parts = []
    for third, reach in ((0, slice(0, 256)), (1, slice(0, 384)), (2, slice(128, 384))):
        parts.append(rows3(kz[m, 256 * third : 256 * third + 256, reach], (high[reach], low[reach])))
    return jnp.concatenate(parts)


def ratio_body(mine, theirs, seen, kz, keep, send, full):
    core = mesh_core()
    full[pl.ds(24 * core, 24)] = mine[...]
    full[pl.ds(24 * (1 - core), 24)] = theirs[...]
    for xp in range(2):
        def pair(ref):
            return jnp.concatenate(
                [ref[:, 16 * xp + 8 * i : 16 * xp + 8 * i + 8, :].reshape(384, 128) for i in range(2)], axis=1
            )
        blurred = along_z(kz, 0, *split(pair(full)))
        ratio = pair(seen) / blurred
        back = along_z(kz, 1, *split(ratio))
        for i in range(2):
            at = slice(16 * xp + 8 * i, 16 * xp + 8 * i + 8)
            full[:, at, :] = back[:, 128 * i : 128 * i + 128].reshape(48, 8, 128)
    keep[...] = full[pl.ds(24 * core, 24)]
    send[...] = full[pl.ds(24 * (1 - core), 24)]


def put_sides(sides, tx, turned, put):
    for xh in range(2):
        cols = pack_columns(sides[:, 16 * xh : 16 * xh + 16, :], 112 * tx, 16, turned)
        for t in range(3):
            put(xh, t, cols[:, 128 * t : 128 * t + 128])


def spread_rows(band, y_h, y_l, g):
    rows = slice(128 * g, 128 * g + 128)
    both = tuple(jnp.concatenate([y[0, rows], y[1, rows]], axis=0) for y in (y_h, y_l))
    return rows3(band, both).reshape(4, 32, 256)


def mirror_rims_body(own, other, mats, odd_out, even_out, y_h, y_l, sides, turned):
    tx = lax.axis_index("tx")
    for v, ref in ((0, own), (1, other)):
        high, low = split(ref[...].reshape(768, 128))
        rows = slice(128 * v, 128 * v + 128)
        band = mats[YF, rows]
        y_h[v], y_l[v] = split(
            dot(jnp.concatenate([high, low], axis=1), jnp.concatenate([band, band]), NN)
            + dot(high, mats[YF + 1, rows], NN)
        )
    for g in range(6):
        z = slice(4 * g, 4 * g + 4)
        wide = spread_rows(mats[BT], y_h, y_l, g)
        put_rims(wide[:, 0:16, 0:128], wide[:, 16:32, 0:128], even_out, odd_out, z)
        sides[z] = wide[:, :, 128:256]
    parts = {}
    put_sides(sides, tx, turned, lambda xh, t, cols: parts.update({(xh, t): cols}))
    for t in range(3):
        put_rims(parts[0, t][None], parts[1, t][None], even_out, odd_out, slice(24 + t, 25 + t))


def mirror_body(y_h, y_l, mats, mid, mid_ext, sides, turned):
    for g in range(6):
        z = slice(4 * g, 4 * g + 4)
        wide = spread_rows(mats[BT + 1], y_h, y_l, g)
        mid[z] = wide[:, :, 0:128]
        sides[z] = wide[:, :, 128:256]

    def put(xh, t, cols):
        mid_ext[3 * xh + t] = cols

    put_sides(sides, lax.axis_index("tx"), turned, put)


def gather_body(mid, mid_ext, from_odd, from_even, after, sides_out, low_out, high_out, turned):
    tx = lax.axis_index("tx")
    odd = parity()
    above = jnp.where(odd, from_even[...], from_odd[...])
    below = jnp.where(odd, from_odd[...], from_even[...])
    for out, z in ((low_out, slice(0, 12)), (high_out, slice(12, 24))):
        out[:, 0:16, :] = mid[z, 0:16, :] + above[z]
        out[:, 16:32, :] = mid[z, 16:32, :] + below[z]
    sides_out[0:3] = mid_ext[0:3] + above[24:27]
    sides_out[3:6] = mid_ext[3:6] + below[24:27]
    if sides_out.shape[0] == 12:
        for xh in range(2):
            at = slice(16 * xh, 16 * xh + 16)
            both = jnp.concatenate([low_out[:, at, :], high_out[:, at, :]])
            put_packs(both, 112 * (1 - tx), 16, turned, sides_out, 6 + 3 * xh)


def join_body(mine, theirs, out):
    out[...] = mine[...] + theirs[...]


def new_estimate(side, low, high, p_low, p_high, cur, norm, cur_out, turned):
    tx = lax.axis_index("tx")
    turned[...] = jnp.zeros_like(turned)
    for xh in range(2):
        at = slice(16 * xh, 16 * xh + 16)
        parts = [side[3 * xh + t] for t in range(3)]
        edge = spread_columns(parts, 112 * (1 - tx), 16, turned).reshape(24, 16, 128)
        for mine, theirs, z in ((low, p_low, slice(0, 12)), (high, p_high, slice(12, 24))):
            total = mine[:, at, :] + theirs[:, at, :] + edge[z]
            cur_out[z, at, :] = cur[z, at, :] * total / norm[z, at, :]


def update_body(
    side, low, high, p_low, p_high, cur, norm, joined, ext, norm_ext, cur_out, ext_out, odd_out, even_out, turned
):
    new_estimate(side, low, high, p_low, p_high, cur, norm, cur_out, turned)
    ext_out[...] = ext[0:6] * (side[6:12] + joined[0:6]) / norm_ext[...]
    put_rims(cur_out[:, 0:16, :], cur_out[:, 16:32, :], even_out, odd_out, slice(0, 24))
    put_rims(ext_out[0:3], ext_out[3:6], even_out, odd_out, slice(24, 27))


def near_half_body(mine, out, sem):
    copy = pltpu.make_async_copy(mine, out.at[pl.ds(24 * mesh_core(), 24)], sem)
    copy.start()
    copy.wait()


def far_half_body(theirs, near, out, sem):
    copy = pltpu.make_async_copy(theirs, out.at[pl.ds(24 * (1 - mesh_core()), 24)], sem)
    copy.start()
    copy.wait()


def swap(value, axis, by, sizes):
    count = int(np.prod(sizes))
    return lax.ppermute(value, axis, [(i, i ^ by) for i in range(count)])


def rim_swap(odd, even):
    rows = lax.axis_size("ty")
    odd_pairs = [(i, i + 1) for i in range(1, rows - 1, 2)]
    odd_pairs += [(b, a) for a, b in odd_pairs]
    from_odd = lax.ppermute(odd, "ty", odd_pairs)
    from_even = lax.ppermute(even, "ty", [(i, i ^ 1) for i in range(rows)])
    return from_odd, from_even


def shards(raw_views, psf_taps, offsets, estimate):
    depth, tile_x, tile_y = estimate.shape
    half = depth // 2
    raw = raw_views[0]

    tile_half = ((half, tile_x, tile_y), F32)
    tile_quarter = ((half // 2, tile_x, tile_y), F32)
    pack = ((6, EDGE, 128), F32)
    rim = ((half + 3, EDGE, 128), F32)
    turned = pltpu.VMEM((128, 384), F32)
    two_sems = pltpu.SemaphoreType.DMA((2,))

    (ext,) = call(begin_body, [pack], [estimate], [turned], name="begin")
    ext = swap(ext, ("view", "tx"), 5, (4, 2))
    (sides,) = call(raw_sides_body, [((12, OMAX, 128), F32)], [raw], [turned], flops=BUSY, name="raw_sides")
    sides = swap(sides, "tx", 1, (2,))
    cur, odd, even = call(rims_body, [tile_half, rim, rim], [estimate], name="rims")

    odd, even = call(corners_body, [rim, rim], [ext, odd, even], name="corners", aliases={1: 0, 2: 1})
    late_taps, late_offsets, _ = lax.optimization_barrier((psf_taps, offsets, odd))
    taps = jnp.pad(late_taps.reshape(-1, TAPS), ((0, 4), (0, 1)))
    flat_psf = late_taps.reshape(-1)
    kz, mats = bands(taps, depth, flat_psf, late_offsets)
    extents = (tile_x * lax.axis_size("ty"), tile_y * lax.axis_size("tx"))
    from_odd, from_even = rim_swap(odd, even)
    raw_rim = ((depth + 3, OMAX, 128), F32)
    raw_odd, raw_even = call(raw_rims_body, [raw_rim, raw_rim], [raw, sides, taps], name="raw_rims")
    raw_from = rim_swap(raw_odd, raw_even)
    columns = [pltpu.VMEM((half, 32, 256), BF16), pltpu.VMEM((half, 32, 256), BF16), turned]
    seen = None

    for iteration in range(ITERS):
        inner = call(
            inner_body, [tile_half, tile_half], [cur, ext, mats], columns, flops=BUSY, name="inner"
        )
        mine, theirs = call(
            outer_body,
            [tile_half, tile_half],
            [from_odd, from_even, mats, *inner],
            columns,
            flops=BUSY,
            name="outer",
        )
        theirs = swap(theirs, "view", 1, (4,))
        if seen is None:
            whole = ((depth, tile_x, tile_y), F32)
            (moved,) = call(
                register_columns_body,
                [whole],
                [late_offsets, raw, sides, mine],
                [pltpu.VMEM((depth, tile_x, 256), F32), turned],
                flops=BUSY,
                name="register_columns",
            )
            (seen,) = call(
                register_body,
                [whole],
                [late_offsets, moved, *raw_from],
                [pltpu.VMEM((depth, tile_x + 2 * OMAX, 128), F32), turned],
                flops=BUSY,
                name="register",
            )
        keep, send = call(
            ratio_body,
            [tile_half, tile_half],
            [mine, theirs, seen, kz],
            [pltpu.VMEM((depth, tile_x, tile_y), F32)],
            flops=3 * 2 * 2 * 384 * 384 * 512,
            name="ratio",
        )
        send = swap(send, "view", 1, (4,))
        along_y = ((2, 768, 256), BF16)
        odd, even, y_h, y_l = call(
            mirror_rims_body,
            [rim, rim, along_y, along_y],
            [keep, send, mats],
            [pltpu.VMEM((half, 32, 128), F32), turned],
            name="mirror_rims",
        )
        mid, mid_ext = call(
            mirror_body,
            [tile_half, pack],
            [y_h, y_l, mats],
            [pltpu.VMEM((half, 32, 128), F32), turned],
            flops=BUSY,
            name="mirror",
        )
        if iteration == 0:
            norm, norm_ext = call(
                functools.partial(norm_body, extents), [tile_half, pack], [flat_psf, late_offsets, y_h], name="norm"
            )
        from_odd, from_even = rim_swap(odd, even)
        last = iteration == ITERS - 1
        sides, low, high = call(
            gather_body,
            [pack if last else ((12, EDGE, 128), F32), tile_quarter, tile_quarter],
            [mid, mid_ext, from_odd, from_even, norm],
            [turned],
            name="gather",
        )
        theirs = swap(sides, "view", 2, (4,))
        p_low = swap(low, "view", 2, (4,))
        p_high = swap(high, "view", 2, (4,))
        (joined,) = call(join_body, [(sides.shape, F32)], [sides, theirs], flops=BUSY, name="join")
        side = swap(joined, ("view", "tx"), 5, (4, 2))
        if last:
            (cur,) = call(new_estimate, [tile_half], [side, low, high, p_low, p_high, cur, norm], [turned], name="last")
            break
        cur, ext, odd, even = call(
            update_body,
            [tile_half, pack, rim, rim],
            [side, low, high, p_low, p_high, cur, norm, joined, ext, norm_ext],
            [turned],
            name="update",
        )
        from_odd, from_even = rim_swap(odd, even)
    far = swap(cur, "view", 1, (4,))
    outs, sem = [((depth, tile_x, tile_y), F32)], [pltpu.SemaphoreType.DMA]
    (near,) = call(near_half_body, outs, [cur], sem, flops=BUSY, name="near_half", out_place=pl.ANY)
    (out,) = call(far_half_body, outs, [far, near], sem, name="far_half", hbm=(1,), aliases={1: 0}, out_place=pl.ANY)
    return out


def solution(mesh):
    placed = (P("view", None, "ty", "tx"), P(), P(), P(None, "ty", "tx"))
    return jax.shard_map(
        shards, mesh=mesh, in_specs=placed, out_specs=P(None, "ty", "tx"), check_vma=False
    )
```

```python
import functools

import jax
import jax.numpy as jnp
import numpy as np
from jax import lax
from jax.experimental import pallas as pl
from jax.experimental.pallas import tpu as pltpu
from jax.sharding import PartitionSpec as P

OMAX = 8
ITERS = 2
TAPS = 31
HALF = 15
EDGE = 16
F32 = jnp.float32
BUSY = 6000000000
BF16 = jnp.bfloat16
highest = lax.Precision.HIGHEST

NN = (((1,), (0,)), ((), ()))


def split(value):
    high = value.astype(BF16)
    low = (value - high.astype(F32)).astype(BF16)
    return high, low


def dot(a, b, dims):
    return lax.dot_general(a, b, dims, preferred_element_type=F32)


def rows3(a, b):
    n = a.shape[0] // 2
    both = dot(a, b[0], NN)
    return both[:n] + (dot(a[:n], b[1], NN) + both[n:])


def call(body, outs, args, scratch=(), flops=0, name=None, hbm=(), limit=8, aliases=None, out_place=pltpu.VMEM):
    def place(i, a):
        if i in hbm:
            return pltpu.HBM
        return pltpu.SMEM if a.ndim == 1 or a.dtype == jnp.int32 else pltpu.VMEM

    specs = [pl.BlockSpec(memory_space=place(i, a)) for i, a in enumerate(args)]
    outs = [jax.ShapeDtypeStruct(*o) for o in outs]
    moved = sum(int(np.prod(a.shape)) * a.dtype.itemsize for a in list(args) + outs)
    return pl.pallas_call(
        body,
        out_shape=outs,
        in_specs=specs,
        out_specs=[pl.BlockSpec(memory_space=out_place)] * len(outs),
        scratch_shapes=list(scratch),
        input_output_aliases=aliases or {},
        compiler_params=pltpu.CompilerParams(vmem_limit_bytes=limit << 20),
        cost_estimate=pl.CostEstimate(flops=flops, bytes_accessed=moved, transcendentals=0),
        name=name,
    )(*args)


def toeplitz(row, rows, width, shift):
    wide = jnp.broadcast_to(row[:, :width], (rows, width))
    return pltpu.roll(wide, shift % width, 1, stride=1, stride_axis=0)


MATS = 10
YF, IN, OUT, BT, YT = 0, 2, 4, 6, 8


def bands_body(taps, place, psf, offsets, kz, mats, placed):
    view = lax.axis_index("view")
    views = (view, view + 1 - 2 * (view % 2))
    total = jnp.sum(taps[...], axis=1, keepdims=True)
    rest = taps[...] / jnp.where(total > 0, total, 1.0)
    placed[...] = jnp.zeros_like(placed)
    for _ in range(3):
        part = rest.astype(BF16)
        placed[...] += dot(part, place[...], NN)
        rest = rest - part.astype(F32)

    def row(v, dim, kind):
        return placed[pl.ds(3 * views[v] + dim, 1), 512 * kind : 512 * kind + 512]

    for m in range(2):
        high, low = split(toeplitz(row(0, 0, m), 384, 512, 0)[:, :384])
        for third in range(3):
            rows = slice(128 * third, 128 * third + 128)
            kz[m, 256 * third : 256 * third + 128] = high[rows]
            kz[m, 256 * third + 128 : 256 * third + 256] = low[rows]
    lane = lax.broadcasted_iota(jnp.int32, (64, 256), 1)

    def between(band, first, count, rest):
        at = lane[: band.shape[0]]
        return jnp.where((at >= first) & (at < first + count), band, rest)

    for v in range(2):
        taps_x = row(v, 1, 2)
        for p in range(4):
            at = 32 * p
            none = jnp.zeros((32, 256), F32)
            inner = between(toeplitz(taps_x, 32, 256, at - HALF), at, 32, none)
            outer = between(toeplitz(taps_x, 32, 256, at + 1), at, 16, none)
            outer = between(toeplitz(taps_x, 32, 256, at - 2 * HALF - 1), at + 16, 16, outer)
            for m, band in ((IN + v, inner), (OUT + v, outer)):
                mats[m, at : at + 32], mats[m, 128 + at : 160 + at] = split(band)
        rows = slice(128 * v, 128 * v + 128)
        mats[0, rows], mats[1, rows] = split(toeplitz(row(v, 2, 2), 128, 256, -HALF))
        mats[YT, :, rows], mats[YT + 1, :, rows] = split(toeplitz(row(v, 2, 3), 256, 256, -HALF)[:, :128])
    for p in range(4):
        both = jnp.zeros((64, 256), F32)
        for v in range(2):
            at = 128 * v + 32 * p
            both = between(toeplitz(row(v, 1, 3), 64, 256, at - 2 * HALF - 1), at, 32, both)
        rims, at = jnp.concatenate([both[0:16], both[48:64]]), 32 * p
        mats[BT, at : at + 32], mats[BT, 128 + at : 160 + at] = split(rims)
        mats[BT + 1, at : at + 32], mats[BT + 1, 128 + at : 160 + at] = split(both[16:48])


def placing():
    place = np.zeros((TAPS + 1, 4, 512), np.float32)
    for k in range(TAPS):
        for kind, at in enumerate((8 * (k - HALF), 8 * (HALF - k), k, TAPS - 1 - k)):
            place[k, kind, at % 512] = 1
    return jnp.asarray(place.reshape(TAPS + 1, 2048), BF16)


def bands(taps, planes, psf, offsets):
    nz = 8 * planes
    return call(
        bands_body,
        [((2, 2 * nz, nz), BF16), ((MATS, 256, 256), BF16)],
        [taps, placing(), psf, offsets],
        [pltpu.VMEM((16, 2048), F32)],
        flops=BUSY,
        name="bands",
    )


def pack_columns(value, at, width, scratch):
    flat = value.reshape(value.shape[0] * value.shape[1], 128)
    scratch[...] = flat.T
    return scratch[pl.ds(pl.multiple_of(at, 8), width), :]


def spread_columns(pack, at, width, scratch):
    for t, part in enumerate(pack):
        scratch[pl.ds(pl.multiple_of(at, 8), width), 128 * t : 128 * t + 128] = part
    return scratch[...].T


def norm_body(shape, psf, offsets, after, norm, norm_ext):
    nx, ny = shape
    views = offsets.shape[0]
    core = lax.axis_index("view") % 2
    x_first = 32 * lax.axis_index("ty")
    tx = lax.axis_index("tx")

    def iota(shape, dim):
        return lax.broadcasted_iota(jnp.int32, shape, dim)

    lane = iota((8, 128), 1)
    tile = jnp.minimum(iota((8, 128), 0), 2)
    places = (
        (0, 24 * core + iota((24, 128), 0)),
        (0, 24 * core + (128 * tile + lane) // EDGE),
        (1, x_first + iota((32, 128), 0)),
        (1, x_first + EDGE * (iota((8, 128), 0) % 2) + lane % EDGE),
        (2, 128 * tx + lane),
        (2, 128 - EDGE * tx + iota((EDGE, 128), 0)),
    )
    extents = (48, nx, ny)
    norm[...] = jnp.zeros_like(norm)
    norm_ext[...] = jnp.zeros_like(norm_ext)

    def one_view(v, _):
        shifts = (0, offsets[v, 0], offsets[v, 1])

        def one_tap(i, carry):
            totals, weights = carry
            taps = [psf[(v * 3 + dim) * TAPS + TAPS - 1 - i] for dim in range(3)]
            new = []
            for (dim, place), total in zip(places, totals):
                at = place + (i - HALF)
                moved = at + shifts[dim]
                inside = (at >= 0) & (at < extents[dim]) & (moved >= 0) & (moved < extents[dim])
                new.append(total + jnp.where(inside, taps[dim], 0.0))
            return tuple(new), tuple(w + t for w, t in zip(weights, taps))

        none = tuple(jnp.zeros(place.shape, F32) for _, place in places)
        totals, weights = lax.fori_loop(0, TAPS, one_tap, (none, (0.0, 0.0, 0.0)))
        in_z, z_row, in_x, x_row, in_y, in_e = (t / weights[dim] for t, (dim, _) in zip(totals, places))
        xy = in_x * in_y[0:1]
        for z in range(24):
            norm[z] += in_z[z : z + 1] * xy
        for k in range(6):
            norm_ext[k] += in_e * (z_row[k % 3 : k % 3 + 1] * x_row[k // 3 : k // 3 + 1])
        return 0

    lax.fori_loop(0, offsets.shape[0], one_view, 0)


def mesh_core():
    return lax.axis_index("view") % 2


def parity():
    return lax.axis_index("ty") % 2 == 1


def put_packs(value, at, width, turned, out, first):
    cols = pack_columns(value, at, width, turned)
    for t in range(3):
        out[first + t] = cols[:, 128 * t : 128 * t + 128]


def begin_body(est, pack_out, turned):
    tx = lax.axis_index("tx")
    half = pl.ds(24 * mesh_core(), 24)
    for xh in range(2):
        put_packs(est[half, 16 * xh : 16 * xh + 16, :], 112 * (1 - tx), 16, turned, pack_out, 3 * xh)


def raw_sides_body(raw, pack_out, turned):
    tx = lax.axis_index("tx")
    for xb in range(4):
        put_packs(raw[:, 8 * xb : 8 * xb + 8, :], 120 * (1 - tx), 8, turned, pack_out, 3 * xb)


def put_rims(top, bottom, even_out, odd_out, planes):
    odd = parity()
    even_out[planes] = jnp.where(odd, top, bottom)
    odd_out[planes] = jnp.where(odd, bottom, top)


def rims_body(est, cur_out, odd_out, even_out):
    cur_out[...] = est[pl.ds(24 * mesh_core(), 24)]
    put_rims(cur_out[:, 0:16, :], cur_out[:, 16:32, :], even_out, odd_out, slice(0, 24))
    odd_out[24:27] = jnp.zeros((3, 16, 128), F32)
    even_out[24:27] = jnp.zeros((3, 16, 128), F32)


def corners_body(pack, odd_in, even_in, odd_out, even_out):
    put_rims(pack[0:3], pack[3:6], even_out, odd_out, slice(24, 27))


def raw_rims_body(raw, pack, after, odd_out, even_out):
    put_rims(raw[:, 0:8, :], raw[:, 24:32, :], even_out, odd_out, slice(0, 48))
    for t in range(3):
        put_rims(pack[t][None], pack[9 + t][None], even_out, odd_out, slice(48 + t, 49 + t))


def register_columns_body(offsets, raw, pack, after, out, wide, turned):
    view, tx = lax.axis_index("view"), lax.axis_index("tx")
    sy = offsets[view, 1]
    wide[:, :, 0:128] = raw[...]
    turned[...] = jnp.zeros_like(turned)
    for b in range(4):
        parts = [pack[3 * b + t] for t in range(3)]
        wide[:, 8 * b : 8 * b + 8, 128:256] = spread_columns(parts, 120 * tx, 8, turned).reshape(48, 8, 128)
    for z in range(0, 48, 4):
        out[z : z + 4] = pltpu.roll(wide[z : z + 4], lax.rem(256 - sy, 256), 2)[:, :, 0:128]


def register_body(offsets, moved, from_odd, from_even, after, out, wide, turned):
    view, tx = lax.axis_index("view"), lax.axis_index("tx")
    sx, sy = offsets[view, 0], offsets[view, 1]
    odd = parity()
    above = jnp.where(odd, from_even[...], from_odd[...])
    below = jnp.where(odd, from_odd[...], from_even[...])
    turned[...] = jnp.zeros_like(turned)
    wide[:, 8:40, :] = moved[...]
    for rim, rows in ((above, slice(0, 8)), (below, slice(40, 48))):
        side = spread_columns([rim[48 + t] for t in range(3)], 120 * tx, 8, turned).reshape(48, 8, 128)
        both = jnp.concatenate([rim[0:48], side], axis=2)
        wide[:, rows, :] = pltpu.roll(both, lax.rem(256 - sy, 256), 2)[:, :, 0:128]
    out[...] = wide[:, pl.ds(8 + sx, 32), :]


def put_columns(rows, main, rim, tx, x_h, x_l, turned):
    x_h[:, rows, 0:128], x_l[:, rows, 0:128] = split(main)
    side = spread_columns(rim, 112 * tx, 16, turned).reshape(24, 16, 128)
    x_h[:, rows, 128:256], x_l[:, rows, 128:256] = split(side)


def blur_rows(x_h, x_l, yf, bx, g, views=(0, 1)):
    z = slice(4 * g, 4 * g + 4)
    high, low = x_h[z].reshape(128, 256), x_l[z].reshape(128, 256)
    first = 128 * views[0]
    yf = [y[:, first : first + 128 * len(views)] for y in yf]
    along_y = split(dot(high, yf[0], NN) + (dot(high, yf[1], NN) + dot(low, yf[0], NN)))
    for i, v in enumerate(views):
        cols = slice(128 * i, 128 * i + 128)
        yield v, z, rows3(bx[v][:, 0:128], (along_y[0][:, cols], along_y[1][:, cols])).reshape(4, 32, 128)


def inner_body(cur, ext, mats, own, other, x_h, x_l, turned):
    tx = lax.axis_index("tx")
    turned[...] = jnp.zeros_like(turned)
    for xh in range(2):
        rows = slice(16 * xh, 16 * xh + 16)
        put_columns(rows, cur[:, rows, :], [ext[3 * xh + t] for t in range(3)], tx, x_h, x_l, turned)
    for g in range(6):
        for v, z, part in blur_rows(x_h, x_l, (mats[YT], mats[YT + 1]), (mats[IN], mats[IN + 1]), g):
            (own, other)[v][z] = part


def fill_outer(from_odd, from_even, x_h, x_l, turned):
    tx = lax.axis_index("tx")
    odd = parity()
    above = jnp.where(odd, from_even[...], from_odd[...])
    below = jnp.where(odd, from_odd[...], from_even[...])
    turned[...] = jnp.zeros_like(turned)
    for xh, rim in ((0, above), (1, below)):
        rows = slice(16 * xh, 16 * xh + 16)
        put_columns(rows, rim[0:24], [rim[24 + t] for t in range(3)], tx, x_h, x_l, turned)


def outer_one_body(v, from_odd, from_even, mats, inner, out, x_h, x_l, turned):
    fill_outer(from_odd, from_even, x_h, x_l, turned)
    for g in range(6):
        for _, z, part in blur_rows(x_h, x_l, (mats[YT], mats[YT + 1]), (mats[OUT], mats[OUT + 1]), g, (v,)):
            out[z] = inner[z] + part


def outer_body(from_odd, from_even, mats, in_own, in_other, own, other, x_h, x_l, turned):
    fill_outer(from_odd, from_even, x_h, x_l, turned)
    for g in range(6):
        for v, z, part in blur_rows(x_h, x_l, (mats[YT], mats[YT + 1]), (mats[OUT], mats[OUT + 1]), g):
            (own, other)[v][z] = (in_own, in_other)[v][z] + part


def along_z(kz, m, high, low):
    parts = []
    for third, reach in ((0, slice(0, 256)), (1, slice(0, 384)), (2, slice(128, 384))):
        parts.append(rows3(kz[m, 256 * third : 256 * third + 256, reach], (high[reach], low[reach])))
    return jnp.concatenate(parts)


def plane_pair(ref, xp):
    return jnp.concatenate(
        [ref[:, 16 * xp + 8 * i : 16 * xp + 8 * i + 8, :].reshape(384, 128) for i in range(2)], axis=1
    )


def put_pair(ref, xp, value):
    for i in range(2):
        at = slice(16 * xp + 8 * i, 16 * xp + 8 * i + 8)
        ref[:, at, :] = value[:, 128 * i : 128 * i + 128].reshape(48, 8, 128)


def join_planes(mine, theirs, full):
    core = mesh_core()
    full[pl.ds(24 * core, 24)] = mine[...]
    full[pl.ds(24 * (1 - core), 24)] = theirs[...]


def part_planes(keep, send, full):
    core = mesh_core()
    keep[...] = full[pl.ds(24 * core, 24)]
    send[...] = full[pl.ds(24 * (1 - core), 24)]


def ratio_body(mine, theirs, seen, kz, keep, send, full):
    join_planes(mine, theirs, full)
    for xp in range(2):
        blurred = along_z(kz, 0, *split(plane_pair(full, xp)))
        ratio = plane_pair(seen, xp) / blurred
        put_pair(full, xp, along_z(kz, 1, *split(ratio)))
    part_planes(keep, send, full)


def planes_body(mine, theirs, kz, out, full):
    join_planes(mine, theirs, full)
    for xp in range(2):
        put_pair(out, xp, along_z(kz, 0, *split(plane_pair(full, xp))))


def divide_body(blurred, seen, kz, keep, send, full):
    for xp in range(2):
        ratio = plane_pair(seen, xp) / plane_pair(blurred, xp)
        put_pair(full, xp, along_z(kz, 1, *split(ratio)))
    part_planes(keep, send, full)


def put_sides(sides, tx, turned, put):
    for xh in range(2):
        cols = pack_columns(sides[:, 16 * xh : 16 * xh + 16, :], 112 * tx, 16, turned)
        for t in range(3):
            put(xh, t, cols[:, 128 * t : 128 * t + 128])


def spread_rows(band, y_h, y_l, g):
    rows = slice(128 * g, 128 * g + 128)
    both = tuple(jnp.concatenate([y[0, rows], y[1, rows]], axis=0) for y in (y_h, y_l))
    return rows3(band, both).reshape(4, 32, 256)


def mirror_rims_body(own, other, mats, odd_out, even_out, y_h, y_l, sides, turned):
    tx = lax.axis_index("tx")
    for v, ref in ((0, own), (1, other)):
        high, low = split(ref[...].reshape(768, 128))
        rows = slice(128 * v, 128 * v + 128)
        band = mats[YF, rows]
        y_h[v], y_l[v] = split(
            dot(jnp.concatenate([high, low], axis=1), jnp.concatenate([band, band]), NN)
            + dot(high, mats[YF + 1, rows], NN)
        )
    for g in range(6):
        z = slice(4 * g, 4 * g + 4)
        wide = spread_rows(mats[BT], y_h, y_l, g)
        put_rims(wide[:, 0:16, 0:128], wide[:, 16:32, 0:128], even_out, odd_out, z)
        sides[z] = wide[:, :, 128:256]
    parts = {}
    put_sides(sides, tx, turned, lambda xh, t, cols: parts.update({(xh, t): cols}))
    for t in range(3):
        put_rims(parts[0, t][None], parts[1, t][None], even_out, odd_out, slice(24 + t, 25 + t))


def mirror_body(y_h, y_l, mats, mid, mid_ext, sides, turned):
    for g in range(6):
        z = slice(4 * g, 4 * g + 4)
        wide = spread_rows(mats[BT + 1], y_h, y_l, g)
        mid[z] = wide[:, :, 0:128]
        sides[z] = wide[:, :, 128:256]

    def put(xh, t, cols):
        mid_ext[3 * xh + t] = cols

    put_sides(sides, lax.axis_index("tx"), turned, put)


def gather_body(mid, mid_ext, from_odd, from_even, after, sides_out, low_out, high_out, turned):
    tx = lax.axis_index("tx")
    odd = parity()
    above = jnp.where(odd, from_even[...], from_odd[...])
    below = jnp.where(odd, from_odd[...], from_even[...])
    for out, z in ((low_out, slice(0, 12)), (high_out, slice(12, 24))):
        out[:, 0:16, :] = mid[z, 0:16, :] + above[z]
        out[:, 16:32, :] = mid[z, 16:32, :] + below[z]
    sides_out[0:3] = mid_ext[0:3] + above[24:27]
    sides_out[3:6] = mid_ext[3:6] + below[24:27]
    if sides_out.shape[0] == 12:
        for xh in range(2):
            at = slice(16 * xh, 16 * xh + 16)
            both = jnp.concatenate([low_out[:, at, :], high_out[:, at, :]])
            put_packs(both, 112 * (1 - tx), 16, turned, sides_out, 6 + 3 * xh)


def join_body(mine, theirs, out):
    out[...] = mine[...] + theirs[...]


def new_estimate(side, low, high, p_low, p_high, cur, norm, cur_out, turned):
    tx = lax.axis_index("tx")
    turned[...] = jnp.zeros_like(turned)
    for xh in range(2):
        at = slice(16 * xh, 16 * xh + 16)
        parts = [side[3 * xh + t] for t in range(3)]
        edge = spread_columns(parts, 112 * (1 - tx), 16, turned).reshape(24, 16, 128)
        for mine, theirs, z in ((low, p_low, slice(0, 12)), (high, p_high, slice(12, 24))):
            total = mine[:, at, :] + theirs[:, at, :] + edge[z]
            cur_out[z, at, :] = cur[z, at, :] * total / norm[z, at, :]


def update_body(
    side, low, high, p_low, p_high, cur, norm, joined, ext, norm_ext, cur_out, ext_out, odd_out, even_out, turned
):
    new_estimate(side, low, high, p_low, p_high, cur, norm, cur_out, turned)
    ext_out[...] = ext[0:6] * (side[6:12] + joined[0:6]) / norm_ext[...]
    put_rims(cur_out[:, 0:16, :], cur_out[:, 16:32, :], even_out, odd_out, slice(0, 24))
    put_rims(ext_out[0:3], ext_out[3:6], even_out, odd_out, slice(24, 27))


def near_half_body(mine, out, sem):
    copy = pltpu.make_async_copy(mine, out.at[pl.ds(24 * mesh_core(), 24)], sem)
    copy.start()
    copy.wait()


def far_half_body(theirs, near, out, sem):
    copy = pltpu.make_async_copy(theirs, out.at[pl.ds(24 * (1 - mesh_core()), 24)], sem)
    copy.start()
    copy.wait()


def swap(value, axis, by, sizes):
    count = int(np.prod(sizes))
    return lax.ppermute(value, axis, [(i, i ^ by) for i in range(count)])


def rim_swap(odd, even):
    rows = lax.axis_size("ty")
    odd_pairs = [(i, i + 1) for i in range(1, rows - 1, 2)]
    odd_pairs += [(b, a) for a, b in odd_pairs]
    from_odd = lax.ppermute(odd, "ty", odd_pairs)
    from_even = lax.ppermute(even, "ty", [(i, i ^ 1) for i in range(rows)])
    return from_odd, from_even


def shards(raw_views, psf_taps, offsets, estimate):
    depth, tile_x, tile_y = estimate.shape
    half = depth // 2
    raw = raw_views[0]

    tile_half = ((half, tile_x, tile_y), F32)
    tile_quarter = ((half // 2, tile_x, tile_y), F32)
    pack = ((6, EDGE, 128), F32)
    rim = ((half + 3, EDGE, 128), F32)
    turned = pltpu.VMEM((128, 384), F32)
    two_sems = pltpu.SemaphoreType.DMA((2,))

    (ext,) = call(begin_body, [pack], [estimate], [turned], name="begin")
    ext = swap(ext, ("view", "tx"), 5, (4, 2))
    (sides,) = call(raw_sides_body, [((12, OMAX, 128), F32)], [raw], [turned], flops=BUSY, name="raw_sides")
    sides = swap(sides, "tx", 1, (2,))
    cur, odd, even = call(rims_body, [tile_half, rim, rim], [estimate], name="rims")

    odd, even = call(corners_body, [rim, rim], [ext, odd, even], name="corners", aliases={1: 0, 2: 1})
    late_taps, late_offsets, _ = lax.optimization_barrier((psf_taps, offsets, odd))
    taps = jnp.pad(late_taps.reshape(-1, TAPS), ((0, 4), (0, 1)))
    flat_psf = late_taps.reshape(-1)
    kz, mats = bands(taps, depth, flat_psf, late_offsets)
    extents = (tile_x * lax.axis_size("ty"), tile_y * lax.axis_size("tx"))
    from_odd, from_even = rim_swap(odd, even)
    raw_rim = ((depth + 3, OMAX, 128), F32)
    raw_odd, raw_even = call(raw_rims_body, [raw_rim, raw_rim], [raw, sides, taps], name="raw_rims")
    raw_from = rim_swap(raw_odd, raw_even)
    columns = [pltpu.VMEM((half, 32, 256), BF16), pltpu.VMEM((half, 32, 256), BF16), turned]
    seen = None

    for iteration in range(ITERS):
        inner = call(
            inner_body, [tile_half, tile_half], [cur, ext, mats], columns, flops=BUSY, name="inner"
        )
        if iteration == 0:
            mine, theirs = call(
                outer_body,
                [tile_half, tile_half],
                [from_odd, from_even, mats, *inner],
                columns,
                flops=BUSY,
                name="outer",
            )
        else:
            (theirs,), (mine,) = (
                call(
                    functools.partial(outer_one_body, v),
                    [tile_half],
                    [from_odd, from_even, mats, inner[v]],
                    columns,
                    flops=BUSY,
                    name="outer_one",
                )
                for v in (1, 0)
            )
        theirs = swap(theirs, "view", 1, (4,))
        if seen is None:
            whole = ((depth, tile_x, tile_y), F32)
            (blurred,) = call(
                planes_body,
                [whole],
                [mine, theirs, kz],
                [pltpu.VMEM((depth, tile_x, tile_y), F32)],
                flops=BUSY,
                name="planes",
            )
            (moved,) = call(
                register_columns_body,
                [whole],
                [late_offsets, raw, sides, mine],
                [pltpu.VMEM((depth, tile_x, 256), F32), turned],
                flops=BUSY,
                name="register_columns",
            )
            (seen,) = call(
                register_body,
                [whole],
                [late_offsets, moved, *raw_from, blurred],
                [pltpu.VMEM((depth, tile_x + 2 * OMAX, 128), F32), turned],
                flops=BUSY,
                name="register",
            )
        first = iteration == 0
        keep, send = call(
            divide_body if first else ratio_body,
            [tile_half, tile_half],
            [blurred, seen, kz] if first else [mine, theirs, seen, kz],
            [pltpu.VMEM((depth, tile_x, tile_y), F32)],
            flops=3 * 2 * 2 * 384 * 384 * 512,
            name="ratio",
        )
        send = swap(send, "view", 1, (4,))
        along_y = ((2, 768, 256), BF16)
        odd, even, y_h, y_l = call(
            mirror_rims_body,
            [rim, rim, along_y, along_y],
            [keep, send, mats],
            [pltpu.VMEM((half, 32, 128), F32), turned],
            name="mirror_rims",
        )
        mid, mid_ext = call(
            mirror_body,
            [tile_half, pack],
            [y_h, y_l, mats],
            [pltpu.VMEM((half, 32, 128), F32), turned],
            flops=BUSY,
            name="mirror",
        )
        if iteration == 0:
            norm, norm_ext = call(
                functools.partial(norm_body, extents), [tile_half, pack], [flat_psf, late_offsets, y_h], name="norm"
            )
        from_odd, from_even = rim_swap(odd, even)
        last = iteration == ITERS - 1
        sides, low, high = call(
            gather_body,
            [pack if last else ((12, EDGE, 128), F32), tile_quarter, tile_quarter],
            [mid, mid_ext, from_odd, from_even, norm],
            [turned],
            name="gather",
        )
        theirs = swap(sides, "view", 2, (4,))
        p_low = swap(low, "view", 2, (4,))
        p_high = swap(high, "view", 2, (4,))
        (joined,) = call(join_body, [(sides.shape, F32)], [sides, theirs], flops=BUSY, name="join")
        side = swap(joined, ("view", "tx"), 5, (4, 2))
        if last:
            (cur,) = call(new_estimate, [tile_half], [side, low, high, p_low, p_high, cur, norm], [turned], name="last")
            break
        cur, ext, odd, even = call(
            update_body,
            [tile_half, pack, rim, rim],
            [side, low, high, p_low, p_high, cur, norm, joined, ext, norm_ext],
            [turned],
            name="update",
        )
        from_odd, from_even = rim_swap(odd, even)
    far = swap(cur, "view", 1, (4,))
    outs, sem = [((depth, tile_x, tile_y), F32)], [pltpu.SemaphoreType.DMA]
    (near,) = call(near_half_body, outs, [cur], sem, flops=BUSY, name="near_half", out_place=pl.ANY)
    (out,) = call(far_half_body, outs, [far, near], sem, name="far_half", hbm=(1,), aliases={1: 0}, out_place=pl.ANY)
    return out


def solution(mesh):
    placed = (P("view", None, "ty", "tx"), P(), P(), P(None, "ty", "tx"))
    return jax.shard_map(
        shards, mesh=mesh, in_specs=placed, out_specs=P(None, "ty", "tx"), check_vma=False
    )
```

```python
import functools

import jax
import jax.numpy as jnp
import numpy as np
from jax import lax
from jax.experimental import pallas as pl
from jax.experimental.pallas import tpu as pltpu
from jax.sharding import PartitionSpec as P

OMAX = 8
ITERS = 2
TAPS = 31
HALF = 15
EDGE = 16
F32 = jnp.float32
BUSY = 6000000000
BF16 = jnp.bfloat16
highest = lax.Precision.HIGHEST

NN = (((1,), (0,)), ((), ()))


def split(value):
    high = value.astype(BF16)
    low = (value - high.astype(F32)).astype(BF16)
    return high, low


def dot(a, b, dims):
    return lax.dot_general(a, b, dims, preferred_element_type=F32)


def rows3(a, b):
    n = a.shape[0] // 2
    both = dot(a, b[0], NN)
    return both[:n] + (dot(a[:n], b[1], NN) + both[n:])


def call(body, outs, args, scratch=(), flops=0, name=None, hbm=(), limit=8, aliases=None, out_place=pltpu.VMEM):
    def place(i, a):
        if i in hbm:
            return pltpu.HBM
        return pltpu.SMEM if a.ndim == 1 or a.dtype == jnp.int32 else pltpu.VMEM

    specs = [pl.BlockSpec(memory_space=place(i, a)) for i, a in enumerate(args)]
    outs = [jax.ShapeDtypeStruct(*o) for o in outs]
    moved = sum(int(np.prod(a.shape)) * a.dtype.itemsize for a in list(args) + outs)
    return pl.pallas_call(
        body,
        out_shape=outs,
        in_specs=specs,
        out_specs=[pl.BlockSpec(memory_space=out_place)] * len(outs),
        scratch_shapes=list(scratch),
        input_output_aliases=aliases or {},
        compiler_params=pltpu.CompilerParams(vmem_limit_bytes=limit << 20),
        cost_estimate=pl.CostEstimate(flops=flops, bytes_accessed=moved, transcendentals=0),
        name=name,
    )(*args)


def toeplitz(row, rows, width, shift):
    wide = jnp.broadcast_to(row[:, :width], (rows, width))
    return pltpu.roll(wide, shift % width, 1, stride=1, stride_axis=0)


MATS = 10
YF, IN, OUT, BT, YT = 0, 2, 4, 6, 8


def bands_body(taps, place, psf, offsets, kz, mats, placed):
    view = lax.axis_index("view")
    views = (view, view + 1 - 2 * (view % 2))
    total = jnp.sum(taps[...], axis=1, keepdims=True)
    rest = taps[...] / jnp.where(total > 0, total, 1.0)
    placed[...] = jnp.zeros_like(placed)
    for _ in range(3):
        part = rest.astype(BF16)
        placed[...] += dot(part, place[...], NN)
        rest = rest - part.astype(F32)

    def row(v, dim, kind):
        return placed[pl.ds(3 * views[v] + dim, 1), 512 * kind : 512 * kind + 512]

    for m in range(2):
        high, low = split(toeplitz(row(0, 0, m), 384, 512, 0)[:, :384])
        for third in range(3):
            rows = slice(128 * third, 128 * third + 128)
            kz[m, 256 * third : 256 * third + 128] = high[rows]
            kz[m, 256 * third + 128 : 256 * third + 256] = low[rows]
    lane = lax.broadcasted_iota(jnp.int32, (64, 256), 1)

    def between(band, first, count, rest):
        at = lane[: band.shape[0]]
        return jnp.where((at >= first) & (at < first + count), band, rest)

    for v in range(2):
        taps_x = row(v, 1, 2)
        for p in range(4):
            at = 32 * p
            none = jnp.zeros((32, 256), F32)
            inner = between(toeplitz(taps_x, 32, 256, at - HALF), at, 32, none)
            outer = between(toeplitz(taps_x, 32, 256, at + 1), at, 16, none)
            outer = between(toeplitz(taps_x, 32, 256, at - 2 * HALF - 1), at + 16, 16, outer)
            for m, band in ((IN + v, inner), (OUT + v, outer)):
                mats[m, at : at + 32], mats[m, 128 + at : 160 + at] = split(band)
        rows = slice(128 * v, 128 * v + 128)
        mats[0, rows], mats[1, rows] = split(toeplitz(row(v, 2, 2), 128, 256, -HALF))
        mats[YT, :, rows], mats[YT + 1, :, rows] = split(toeplitz(row(v, 2, 3), 256, 256, -HALF)[:, :128])
    for p in range(4):
        both = jnp.zeros((64, 256), F32)
        for v in range(2):
            at = 128 * v + 32 * p
            both = between(toeplitz(row(v, 1, 3), 64, 256, at - 2 * HALF - 1), at, 32, both)
        rims, at = jnp.concatenate([both[0:16], both[48:64]]), 32 * p
        mats[BT, at : at + 32], mats[BT, 128 + at : 160 + at] = split(rims)
        mats[BT + 1, at : at + 32], mats[BT + 1, 128 + at : 160 + at] = split(both[16:48])


def placing():
    place = np.zeros((TAPS + 1, 4, 512), np.float32)
    for k in range(TAPS):
        for kind, at in enumerate((8 * (k - HALF), 8 * (HALF - k), k, TAPS - 1 - k)):
            place[k, kind, at % 512] = 1
    return jnp.asarray(place.reshape(TAPS + 1, 2048), BF16)


def bands(taps, planes, psf, offsets):
    nz = 8 * planes
    return call(
        bands_body,
        [((2, 2 * nz, nz), BF16), ((MATS, 256, 256), BF16)],
        [taps, placing(), psf, offsets],
        [pltpu.VMEM((16, 2048), F32)],
        flops=BUSY,
        name="bands",
    )


def pack_columns(value, at, width, scratch):
    flat = value.reshape(value.shape[0] * value.shape[1], 128)
    scratch[...] = flat.T
    return scratch[pl.ds(pl.multiple_of(at, 8), width), :]


def spread_columns(pack, at, width, scratch):
    for t, part in enumerate(pack):
        scratch[pl.ds(pl.multiple_of(at, 8), width), 128 * t : 128 * t + 128] = part
    return scratch[...].T


def norm_body(shape, psf, offsets, after, norm, norm_ext):
    nx, ny = shape
    views = offsets.shape[0]
    core = lax.axis_index("view") % 2
    x_first = 32 * lax.axis_index("ty")
    tx = lax.axis_index("tx")

    def iota(shape, dim):
        return lax.broadcasted_iota(jnp.int32, shape, dim)

    lane = iota((8, 128), 1)
    tile = jnp.minimum(iota((8, 128), 0), 2)
    places = (
        (0, 24 * core + iota((24, 128), 0)),
        (0, 24 * core + (128 * tile + lane) // EDGE),
        (1, x_first + iota((32, 128), 0)),
        (1, x_first + EDGE * (iota((8, 128), 0) % 2) + lane % EDGE),
        (2, 128 * tx + lane),
        (2, 128 - EDGE * tx + iota((EDGE, 128), 0)),
    )
    extents = (48, nx, ny)
    norm[...] = jnp.zeros_like(norm)
    norm_ext[...] = jnp.zeros_like(norm_ext)

    def one_view(v, _):
        shifts = (0, offsets[v, 0], offsets[v, 1])

        def one_tap(i, carry):
            totals, weights = carry
            taps = [psf[(v * 3 + dim) * TAPS + TAPS - 1 - i] for dim in range(3)]
            new = []
            for (dim, place), total in zip(places, totals):
                at = place + (i - HALF)
                moved = at + shifts[dim]
                inside = (at >= 0) & (at < extents[dim]) & (moved >= 0) & (moved < extents[dim])
                new.append(total + jnp.where(inside, taps[dim], 0.0))
            return tuple(new), tuple(w + t for w, t in zip(weights, taps))

        none = tuple(jnp.zeros(place.shape, F32) for _, place in places)
        totals, weights = lax.fori_loop(0, TAPS, one_tap, (none, (0.0, 0.0, 0.0)))
        in_z, z_row, in_x, x_row, in_y, in_e = (t / weights[dim] for t, (dim, _) in zip(totals, places))
        xy = in_x * in_y[0:1]
        for z in range(24):
            norm[z] += in_z[z : z + 1] * xy
        for k in range(6):
            norm_ext[k] += in_e * (z_row[k % 3 : k % 3 + 1] * x_row[k // 3 : k // 3 + 1])
        return 0

    lax.fori_loop(0, offsets.shape[0], one_view, 0)


def mesh_core():
    return lax.axis_index("view") % 2


def parity():
    return lax.axis_index("ty") % 2 == 1


def put_packs(value, at, width, turned, out, first):
    cols = pack_columns(value, at, width, turned)
    for t in range(3):
        out[first + t] = cols[:, 128 * t : 128 * t + 128]


def begin_body(est, pack_out, turned):
    tx = lax.axis_index("tx")
    half = pl.ds(24 * mesh_core(), 24)
    for xh in range(2):
        put_packs(est[half, 16 * xh : 16 * xh + 16, :], 112 * (1 - tx), 16, turned, pack_out, 3 * xh)


def raw_sides_body(raw, pack_out, turned):
    tx = lax.axis_index("tx")
    for xb in range(4):
        put_packs(raw[:, 8 * xb : 8 * xb + 8, :], 120 * (1 - tx), 8, turned, pack_out, 3 * xb)


def put_rims(top, bottom, even_out, odd_out, planes):
    odd = parity()
    even_out[planes] = jnp.where(odd, top, bottom)
    odd_out[planes] = jnp.where(odd, bottom, top)


def rims_body(est, cur_out, odd_out, even_out):
    cur_out[...] = est[pl.ds(24 * mesh_core(), 24)]
    put_rims(cur_out[:, 0:16, :], cur_out[:, 16:32, :], even_out, odd_out, slice(0, 24))
    odd_out[24:27] = jnp.zeros((3, 16, 128), F32)
    even_out[24:27] = jnp.zeros((3, 16, 128), F32)


def corners_body(pack, odd_in, even_in, odd_out, even_out):
    put_rims(pack[0:3], pack[3:6], even_out, odd_out, slice(24, 27))


def raw_rims_body(raw, pack, after, odd_out, even_out):
    put_rims(raw[:, 0:8, :], raw[:, 24:32, :], even_out, odd_out, slice(0, 48))
    for t in range(3):
        put_rims(pack[t][None], pack[9 + t][None], even_out, odd_out, slice(48 + t, 49 + t))


def shift_columns(tile, side, sy):
    lane = lax.broadcasted_iota(jnp.int32, tile.shape, 2)
    inside = (lane >= sy) & (lane < 128 + sy)
    return pltpu.roll(jnp.where(inside, tile, side), lax.rem(128 - sy, 128), 2)


def register_columns_body(offsets, raw, pack, after, out, turned):
    view, tx = lax.axis_index("view"), lax.axis_index("tx")
    sy = offsets[view, 1]
    turned[...] = jnp.zeros_like(turned)
    for b in range(4):
        parts = [pack[3 * b + t] for t in range(3)]
        side = spread_columns(parts, 120 * tx, 8, turned).reshape(48, 8, 128)
        rows = slice(8 * b, 8 * b + 8)
        out[:, rows, :] = shift_columns(raw[:, rows, :], side, sy)


def register_body(offsets, moved, from_odd, from_even, after, out, wide, turned):
    view, tx = lax.axis_index("view"), lax.axis_index("tx")
    sx, sy = offsets[view, 0], offsets[view, 1]
    odd = parity()
    above = jnp.where(odd, from_even[...], from_odd[...])
    below = jnp.where(odd, from_odd[...], from_even[...])
    turned[...] = jnp.zeros_like(turned)
    wide[:, 8:40, :] = moved[...]
    for rim, rows in ((above, slice(0, 8)), (below, slice(40, 48))):
        side = spread_columns([rim[48 + t] for t in range(3)], 120 * tx, 8, turned).reshape(48, 8, 128)
        wide[:, rows, :] = shift_columns(rim[0:48], side, sy)
    out[...] = wide[:, pl.ds(8 + sx, 32), :]


def put_columns(rows, main, rim, tx, x_h, x_l, turned):
    x_h[:, rows, 0:128], x_l[:, rows, 0:128] = split(main)
    side = spread_columns(rim, 112 * tx, 16, turned).reshape(24, 16, 128)
    x_h[:, rows, 128:256], x_l[:, rows, 128:256] = split(side)


def blur_rows(x_h, x_l, yf, bx, g):
    z = slice(4 * g, 4 * g + 4)
    high, low = x_h[z].reshape(128, 256), x_l[z].reshape(128, 256)
    along_y = split(dot(high, yf[0], NN) + (dot(high, yf[1], NN) + dot(low, yf[0], NN)))
    for v in range(2):
        cols = slice(128 * v, 128 * v + 128)
        yield v, z, rows3(bx[v][:, 0:128], (along_y[0][:, cols], along_y[1][:, cols])).reshape(4, 32, 128)


def inner_body(cur, ext, mats, own, other, x_h, x_l, turned):
    tx = lax.axis_index("tx")
    turned[...] = jnp.zeros_like(turned)
    for xh in range(2):
        rows = slice(16 * xh, 16 * xh + 16)
        put_columns(rows, cur[:, rows, :], [ext[3 * xh + t] for t in range(3)], tx, x_h, x_l, turned)
    for g in range(6):
        for v, z, part in blur_rows(x_h, x_l, (mats[YT], mats[YT + 1]), (mats[IN], mats[IN + 1]), g):
            (own, other)[v][z] = part


def fill_outer(from_odd, from_even, x_h, x_l, turned):
    tx = lax.axis_index("tx")
    odd = parity()
    above = jnp.where(odd, from_even[...], from_odd[...])
    below = jnp.where(odd, from_odd[...], from_even[...])
    turned[...] = jnp.zeros_like(turned)
    for xh, rim in ((0, above), (1, below)):
        rows = slice(16 * xh, 16 * xh + 16)
        put_columns(rows, rim[0:24], [rim[24 + t] for t in range(3)], tx, x_h, x_l, turned)


def outer_body(from_odd, from_even, mats, in_own, in_other, own, other, x_h, x_l, turned):
    fill_outer(from_odd, from_even, x_h, x_l, turned)
    for g in range(6):
        for v, z, part in blur_rows(x_h, x_l, (mats[YT], mats[YT + 1]), (mats[OUT], mats[OUT + 1]), g):
            (own, other)[v][z] = (in_own, in_other)[v][z] + part


def along_z(kz, m, high, low):
    parts = []
    for third, reach in ((0, slice(0, 256)), (1, slice(0, 384)), (2, slice(128, 384))):
        parts.append(rows3(kz[m, 256 * third : 256 * third + 256, reach], (high[reach], low[reach])))
    return jnp.concatenate(parts)


def plane_pair(ref, xp):
    return jnp.concatenate(
        [ref[:, 16 * xp + 8 * i : 16 * xp + 8 * i + 8, :].reshape(384, 128) for i in range(2)], axis=1
    )


def put_pair(ref, xp, value):
    for i in range(2):
        at = slice(16 * xp + 8 * i, 16 * xp + 8 * i + 8)
        ref[:, at, :] = value[:, 128 * i : 128 * i + 128].reshape(48, 8, 128)


def join_planes(mine, theirs, full):
    core = mesh_core()
    full[pl.ds(24 * core, 24)] = mine[...]
    full[pl.ds(24 * (1 - core), 24)] = theirs[...]


def part_planes(keep, send, full):
    core = mesh_core()
    keep[...] = full[pl.ds(24 * core, 24)]
    send[...] = full[pl.ds(24 * (1 - core), 24)]


def ratio_body(mine, theirs, seen, kz, keep, send, full):
    join_planes(mine, theirs, full)
    for xp in range(2):
        blurred = along_z(kz, 0, *split(plane_pair(full, xp)))
        ratio = plane_pair(seen, xp) / blurred
        put_pair(full, xp, along_z(kz, 1, *split(ratio)))
    part_planes(keep, send, full)


def planes_body(mine, theirs, kz, out, full):
    join_planes(mine, theirs, full)
    for xp in range(2):
        put_pair(out, xp, along_z(kz, 0, *split(plane_pair(full, xp))))


def divide_body(blurred, seen, kz, keep, send, full):
    for xp in range(2):
        ratio = plane_pair(seen, xp) / plane_pair(blurred, xp)
        put_pair(full, xp, along_z(kz, 1, *split(ratio)))
    part_planes(keep, send, full)


def put_sides(sides, tx, turned, put):
    for xh in range(2):
        cols = pack_columns(sides[:, 16 * xh : 16 * xh + 16, :], 112 * tx, 16, turned)
        for t in range(3):
            put(xh, t, cols[:, 128 * t : 128 * t + 128])


def spread_rows(band, y_h, y_l, g):
    rows = slice(128 * g, 128 * g + 128)
    both = tuple(jnp.concatenate([y[0, rows], y[1, rows]], axis=0) for y in (y_h, y_l))
    return rows3(band, both).reshape(4, 32, 256)


def mirror_rims_body(own, other, mats, odd_out, even_out, y_h, y_l, sides, turned):
    tx = lax.axis_index("tx")
    for v, ref in ((0, own), (1, other)):
        high, low = split(ref[...].reshape(768, 128))
        rows = slice(128 * v, 128 * v + 128)
        band = mats[YF, rows]
        y_h[v], y_l[v] = split(
            dot(jnp.concatenate([high, low], axis=1), jnp.concatenate([band, band]), NN)
            + dot(high, mats[YF + 1, rows], NN)
        )
    for g in range(6):
        z = slice(4 * g, 4 * g + 4)
        wide = spread_rows(mats[BT], y_h, y_l, g)
        put_rims(wide[:, 0:16, 0:128], wide[:, 16:32, 0:128], even_out, odd_out, z)
        sides[z] = wide[:, :, 128:256]
    parts = {}
    put_sides(sides, tx, turned, lambda xh, t, cols: parts.update({(xh, t): cols}))
    for t in range(3):
        put_rims(parts[0, t][None], parts[1, t][None], even_out, odd_out, slice(24 + t, 25 + t))


def mirror_body(y_h, y_l, mats, mid, mid_ext, sides, turned):
    for g in range(6):
        z = slice(4 * g, 4 * g + 4)
        wide = spread_rows(mats[BT + 1], y_h, y_l, g)
        mid[z] = wide[:, :, 0:128]
        sides[z] = wide[:, :, 128:256]

    def put(xh, t, cols):
        mid_ext[3 * xh + t] = cols

    put_sides(sides, lax.axis_index("tx"), turned, put)


def gather_body(mid, mid_ext, from_odd, from_even, after, sides_out, low_out, high_out, turned):
    tx = lax.axis_index("tx")
    odd = parity()
    above = jnp.where(odd, from_even[...], from_odd[...])
    below = jnp.where(odd, from_odd[...], from_even[...])
    for out, z in ((low_out, slice(0, 12)), (high_out, slice(12, 24))):
        out[:, 0:16, :] = mid[z, 0:16, :] + above[z]
        out[:, 16:32, :] = mid[z, 16:32, :] + below[z]
    sides_out[0:3] = mid_ext[0:3] + above[24:27]
    sides_out[3:6] = mid_ext[3:6] + below[24:27]
    if sides_out.shape[0] == 12:
        for xh in range(2):
            at = slice(16 * xh, 16 * xh + 16)
            both = jnp.concatenate([low_out[:, at, :], high_out[:, at, :]])
            put_packs(both, 112 * (1 - tx), 16, turned, sides_out, 6 + 3 * xh)


def join_body(mine, theirs, out):
    out[...] = mine[...] + theirs[...]


def new_estimate(side, low, high, p_low, p_high, cur, norm, cur_out, turned):
    tx = lax.axis_index("tx")
    turned[...] = jnp.zeros_like(turned)
    for xh in range(2):
        at = slice(16 * xh, 16 * xh + 16)
        parts = [side[3 * xh + t] for t in range(3)]
        edge = spread_columns(parts, 112 * (1 - tx), 16, turned).reshape(24, 16, 128)
        for mine, theirs, z in ((low, p_low, slice(0, 12)), (high, p_high, slice(12, 24))):
            total = mine[:, at, :] + theirs[:, at, :] + edge[z]
            cur_out[z, at, :] = cur[z, at, :] * total / norm[z, at, :]


def update_body(
    side, low, high, p_low, p_high, cur, norm, joined, ext, norm_ext, cur_out, ext_out, odd_out, even_out, turned
):
    new_estimate(side, low, high, p_low, p_high, cur, norm, cur_out, turned)
    ext_out[...] = ext[0:6] * (side[6:12] + joined[0:6]) / norm_ext[...]
    put_rims(cur_out[:, 0:16, :], cur_out[:, 16:32, :], even_out, odd_out, slice(0, 24))
    put_rims(ext_out[0:3], ext_out[3:6], even_out, odd_out, slice(24, 27))


def near_half_body(mine, out, sem):
    copy = pltpu.make_async_copy(mine, out.at[pl.ds(24 * mesh_core(), 24)], sem)
    copy.start()
    copy.wait()


def far_half_body(theirs, near, out, sem):
    copy = pltpu.make_async_copy(theirs, out.at[pl.ds(24 * (1 - mesh_core()), 24)], sem)
    copy.start()
    copy.wait()


def swap(value, axis, by, sizes):
    count = int(np.prod(sizes))
    return lax.ppermute(value, axis, [(i, i ^ by) for i in range(count)])


def rim_swap(odd, even):
    rows = lax.axis_size("ty")
    odd_pairs = [(i, i + 1) for i in range(1, rows - 1, 2)]
    odd_pairs += [(b, a) for a, b in odd_pairs]
    from_odd = lax.ppermute(odd, "ty", odd_pairs)
    from_even = lax.ppermute(even, "ty", [(i, i ^ 1) for i in range(rows)])
    return from_odd, from_even


def shards(raw_views, psf_taps, offsets, estimate):
    depth, tile_x, tile_y = estimate.shape
    half = depth // 2
    raw = raw_views[0]

    tile_half = ((half, tile_x, tile_y), F32)
    tile_quarter = ((half // 2, tile_x, tile_y), F32)
    pack = ((6, EDGE, 128), F32)
    rim = ((half + 3, EDGE, 128), F32)
    turned = pltpu.VMEM((128, 384), F32)
    two_sems = pltpu.SemaphoreType.DMA((2,))

    (ext,) = call(begin_body, [pack], [estimate], [turned], name="begin")
    ext = swap(ext, ("view", "tx"), 5, (4, 2))
    (sides,) = call(raw_sides_body, [((12, OMAX, 128), F32)], [raw], [turned], flops=BUSY, name="raw_sides")
    sides = swap(sides, "tx", 1, (2,))
    cur, odd, even = call(rims_body, [tile_half, rim, rim], [estimate], name="rims")

    odd, even = call(corners_body, [rim, rim], [ext, odd, even], name="corners", aliases={1: 0, 2: 1})
    late_taps, late_offsets, _ = lax.optimization_barrier((psf_taps, offsets, odd))
    taps = jnp.pad(late_taps.reshape(-1, TAPS), ((0, 4), (0, 1)))
    flat_psf = late_taps.reshape(-1)
    kz, mats = bands(taps, depth, flat_psf, late_offsets)
    extents = (tile_x * lax.axis_size("ty"), tile_y * lax.axis_size("tx"))
    from_odd, from_even = rim_swap(odd, even)
    raw_rim = ((depth + 3, OMAX, 128), F32)
    raw_odd, raw_even = call(raw_rims_body, [raw_rim, raw_rim], [raw, sides, taps], name="raw_rims")
    raw_from = rim_swap(raw_odd, raw_even)
    columns = [pltpu.VMEM((half, 32, 256), BF16), pltpu.VMEM((half, 32, 256), BF16), turned]
    seen = None

    for iteration in range(ITERS):
        inner = call(
            inner_body, [tile_half, tile_half], [cur, ext, mats], columns, flops=BUSY, name="inner"
        )
        mine, theirs = call(
            outer_body,
            [tile_half, tile_half],
            [from_odd, from_even, mats, *inner],
            columns,
            flops=BUSY,
            name="outer",
        )
        theirs = swap(theirs, "view", 1, (4,))
        if seen is None:
            whole = ((depth, tile_x, tile_y), F32)
            (blurred,) = call(
                planes_body,
                [whole],
                [mine, theirs, kz],
                [pltpu.VMEM((depth, tile_x, tile_y), F32)],
                flops=BUSY,
                name="planes",
            )
            (moved,) = call(
                register_columns_body,
                [whole],
                [late_offsets, raw, sides, mine],
                [turned],
                flops=BUSY,
                name="register_columns",
            )
            (seen,) = call(
                register_body,
                [whole],
                [late_offsets, moved, *raw_from, blurred],
                [pltpu.VMEM((depth, tile_x + 2 * OMAX, 128), F32), turned],
                flops=BUSY,
                name="register",
            )
        first = iteration == 0
        keep, send = call(
            divide_body if first else ratio_body,
            [tile_half, tile_half],
            [blurred, seen, kz] if first else [mine, theirs, seen, kz],
            [pltpu.VMEM((depth, tile_x, tile_y), F32)],
            flops=3 * 2 * 2 * 384 * 384 * 512,
            name="ratio",
        )
        send = swap(send, "view", 1, (4,))
        along_y = ((2, 768, 256), BF16)
        odd, even, y_h, y_l = call(
            mirror_rims_body,
            [rim, rim, along_y, along_y],
            [keep, send, mats],
            [pltpu.VMEM((half, 32, 128), F32), turned],
            name="mirror_rims",
        )
        mid, mid_ext = call(
            mirror_body,
            [tile_half, pack],
            [y_h, y_l, mats],
            [pltpu.VMEM((half, 32, 128), F32), turned],
            flops=BUSY,
            name="mirror",
        )
        if iteration == 0:
            norm, norm_ext = call(
                functools.partial(norm_body, extents), [tile_half, pack], [flat_psf, late_offsets, y_h], name="norm"
            )
        from_odd, from_even = rim_swap(odd, even)
        last = iteration == ITERS - 1
        sides, low, high = call(
            gather_body,
            [pack if last else ((12, EDGE, 128), F32), tile_quarter, tile_quarter],
            [mid, mid_ext, from_odd, from_even, norm],
            [turned],
            name="gather",
        )
        theirs = swap(sides, "view", 2, (4,))
        p_low = swap(low, "view", 2, (4,))
        p_high = swap(high, "view", 2, (4,))
        (joined,) = call(join_body, [(sides.shape, F32)], [sides, theirs], flops=BUSY, name="join")
        side = swap(joined, ("view", "tx"), 5, (4, 2))
        if last:
            (cur,) = call(new_estimate, [tile_half], [side, low, high, p_low, p_high, cur, norm], [turned], name="last")
            break
        cur, ext, odd, even = call(
            update_body,
            [tile_half, pack, rim, rim],
            [side, low, high, p_low, p_high, cur, norm, joined, ext, norm_ext],
            [turned],
            name="update",
        )
        from_odd, from_even = rim_swap(odd, even)
    far = swap(cur, "view", 1, (4,))
    outs, sem = [((depth, tile_x, tile_y), F32)], [pltpu.SemaphoreType.DMA]
    (near,) = call(near_half_body, outs, [cur], sem, flops=BUSY, name="near_half", out_place=pl.ANY)
    (out,) = call(far_half_body, outs, [far, near], sem, name="far_half", hbm=(1,), aliases={1: 0}, out_place=pl.ANY)
    return out


def solution(mesh):
    placed = (P("view", None, "ty", "tx"), P(), P(), P(None, "ty", "tx"))
    return jax.shard_map(
        shards, mesh=mesh, in_specs=placed, out_specs=P(None, "ty", "tx"), check_vma=False
    )
```

```python
import functools

import jax
import jax.numpy as jnp
import numpy as np
from jax import lax
from jax.experimental import pallas as pl
from jax.experimental.pallas import tpu as pltpu
from jax.sharding import PartitionSpec as P

OMAX = 8
ITERS = 2
TAPS = 31
HALF = 15
EDGE = 16
F32 = jnp.float32
BUSY = 6000000000
BF16 = jnp.bfloat16
highest = lax.Precision.HIGHEST

NN = (((1,), (0,)), ((), ()))


def split(value):
    high = value.astype(BF16)
    low = (value - high.astype(F32)).astype(BF16)
    return high, low


def dot(a, b, dims):
    return lax.dot_general(a, b, dims, preferred_element_type=F32)


def rows3(a, b):
    n = a.shape[0] // 2
    both = dot(a, b[0], NN)
    return both[:n] + (dot(a[:n], b[1], NN) + both[n:])


def call(body, outs, args, scratch=(), flops=0, name=None, hbm=(), limit=8, aliases=None, out_place=pltpu.VMEM):
    def place(i, a):
        if i in hbm:
            return pltpu.HBM
        return pltpu.SMEM if a.ndim == 1 or a.dtype == jnp.int32 else pltpu.VMEM

    specs = [pl.BlockSpec(memory_space=place(i, a)) for i, a in enumerate(args)]
    outs = [jax.ShapeDtypeStruct(*o) for o in outs]
    moved = sum(int(np.prod(a.shape)) * a.dtype.itemsize for a in list(args) + outs)
    return pl.pallas_call(
        body,
        out_shape=outs,
        in_specs=specs,
        out_specs=[pl.BlockSpec(memory_space=out_place)] * len(outs),
        scratch_shapes=list(scratch),
        input_output_aliases=aliases or {},
        compiler_params=pltpu.CompilerParams(vmem_limit_bytes=limit << 20),
        cost_estimate=pl.CostEstimate(flops=flops, bytes_accessed=moved, transcendentals=0),
        name=name,
    )(*args)


def toeplitz(row, rows, width, shift):
    wide = jnp.broadcast_to(row[:, :width], (rows, width))
    return pltpu.roll(wide, shift % width, 1, stride=1, stride_axis=0)


MATS = 10
YF, IN, OUT, BT, YT = 0, 2, 4, 6, 8


def bands_body(taps, place, psf, offsets, kz, mats, placed):
    view = lax.axis_index("view")
    views = (view, view + 1 - 2 * (view % 2))
    total = jnp.sum(taps[...], axis=1, keepdims=True)
    rest = taps[...] / jnp.where(total > 0, total, 1.0)
    placed[...] = jnp.zeros_like(placed)
    for _ in range(3):
        part = rest.astype(BF16)
        placed[...] += dot(part, place[...], NN)
        rest = rest - part.astype(F32)

    def row(v, dim, kind):
        return placed[pl.ds(3 * views[v] + dim, 1), 512 * kind : 512 * kind + 512]

    for m in range(2):
        high, low = split(toeplitz(row(0, 0, m), 384, 512, 0)[:, :384])
        for third in range(3):
            rows = slice(128 * third, 128 * third + 128)
            kz[m, 256 * third : 256 * third + 128] = high[rows]
            kz[m, 256 * third + 128 : 256 * third + 256] = low[rows]
    lane = lax.broadcasted_iota(jnp.int32, (64, 256), 1)

    def between(band, first, count, rest):
        at = lane[: band.shape[0]]
        return jnp.where((at >= first) & (at < first + count), band, rest)

    for v in range(2):
        taps_x = row(v, 1, 2)
        for p in range(4):
            at = 32 * p
            none = jnp.zeros((32, 256), F32)
            inner = between(toeplitz(taps_x, 32, 256, at - HALF), at, 32, none)
            outer = between(toeplitz(taps_x, 32, 256, at + 1), at, 16, none)
            outer = between(toeplitz(taps_x, 32, 256, at - 2 * HALF - 1), at + 16, 16, outer)
            for m, band in ((IN + v, inner), (OUT + v, outer)):
                mats[m, at : at + 32], mats[m, 128 + at : 160 + at] = split(band)
        rows = slice(128 * v, 128 * v + 128)
        mats[0, rows], mats[1, rows] = split(toeplitz(row(v, 2, 2), 128, 256, -HALF))
        mats[YT, :, rows], mats[YT + 1, :, rows] = split(toeplitz(row(v, 2, 3), 256, 256, -HALF)[:, :128])
    for p in range(4):
        both = jnp.zeros((64, 256), F32)
        for v in range(2):
            at = 128 * v + 32 * p
            both = between(toeplitz(row(v, 1, 3), 64, 256, at - 2 * HALF - 1), at, 32, both)
        rims, at = jnp.concatenate([both[0:16], both[48:64]]), 32 * p
        mats[BT, at : at + 32], mats[BT, 128 + at : 160 + at] = split(rims)
        mats[BT + 1, at : at + 32], mats[BT + 1, 128 + at : 160 + at] = split(both[16:48])


def placing():
    place = np.zeros((TAPS + 1, 4, 512), np.float32)
    for k in range(TAPS):
        for kind, at in enumerate((8 * (k - HALF), 8 * (HALF - k), k, TAPS - 1 - k)):
            place[k, kind, at % 512] = 1
    return jnp.asarray(place.reshape(TAPS + 1, 2048), BF16)


def bands(taps, planes, psf, offsets):
    nz = 8 * planes
    return call(
        bands_body,
        [((2, 2 * nz, nz), BF16), ((MATS, 256, 256), BF16)],
        [taps, placing(), psf, offsets],
        [pltpu.VMEM((16, 2048), F32)],
        flops=BUSY,
        name="bands",
    )


def pack_columns(value, at, width, scratch):
    flat = value.reshape(value.shape[0] * value.shape[1], 128)
    scratch[...] = flat.T
    return scratch[pl.ds(pl.multiple_of(at, 8), width), :]


def spread_columns(pack, at, width, scratch):
    for t, part in enumerate(pack):
        scratch[pl.ds(pl.multiple_of(at, 8), width), 128 * t : 128 * t + 128] = part
    return scratch[...].T


def norm_body(shape, psf, offsets, after, norm, norm_ext):
    nx, ny = shape
    views = offsets.shape[0]
    core = lax.axis_index("view") % 2
    x_first = 32 * lax.axis_index("ty")
    tx = lax.axis_index("tx")

    def iota(shape, dim):
        return lax.broadcasted_iota(jnp.int32, shape, dim)

    lane = iota((8, 128), 1)
    tile = jnp.minimum(iota((8, 128), 0), 2)
    places = (
        (0, 24 * core + iota((24, 128), 0)),
        (0, 24 * core + (128 * tile + lane) // EDGE),
        (1, x_first + iota((32, 128), 0)),
        (1, x_first + EDGE * (iota((8, 128), 0) % 2) + lane % EDGE),
        (2, 128 * tx + lane),
        (2, 128 - EDGE * tx + iota((EDGE, 128), 0)),
    )
    extents = (48, nx, ny)
    norm[...] = jnp.zeros_like(norm)
    norm_ext[...] = jnp.zeros_like(norm_ext)

    def one_view(v, _):
        shifts = (0, offsets[v, 0], offsets[v, 1])

        def one_tap(i, carry):
            totals, weights = carry
            taps = [psf[(v * 3 + dim) * TAPS + TAPS - 1 - i] for dim in range(3)]
            new = []
            for (dim, place), total in zip(places, totals):
                at = place + (i - HALF)
                moved = at + shifts[dim]
                inside = (at >= 0) & (at < extents[dim]) & (moved >= 0) & (moved < extents[dim])
                new.append(total + jnp.where(inside, taps[dim], 0.0))
            return tuple(new), tuple(w + t for w, t in zip(weights, taps))

        none = tuple(jnp.zeros(place.shape, F32) for _, place in places)
        totals, weights = lax.fori_loop(0, TAPS, one_tap, (none, (0.0, 0.0, 0.0)))
        in_z, z_row, in_x, x_row, in_y, in_e = (t / weights[dim] for t, (dim, _) in zip(totals, places))
        xy = in_x * in_y[0:1]
        for z in range(24):
            norm[z] += in_z[z : z + 1] * xy
        for k in range(6):
            norm_ext[k] += in_e * (z_row[k % 3 : k % 3 + 1] * x_row[k // 3 : k // 3 + 1])
        return 0

    lax.fori_loop(0, offsets.shape[0], one_view, 0)


def mesh_core():
    return lax.axis_index("view") % 2


def parity():
    return lax.axis_index("ty") % 2 == 1


def put_packs(value, at, width, turned, out, first):
    cols = pack_columns(value, at, width, turned)
    for t in range(3):
        out[first + t] = cols[:, 128 * t : 128 * t + 128]


def begin_body(est, raw, pack_out, raw_pack, cur, raw_here, turned, sems):
    tx = lax.axis_index("tx")
    first = 24 * mesh_core()
    copies = []
    for i in range(2):
        z = slice(12 * i, 12 * i + 12)
        copies.append(pltpu.make_async_copy(est.at[pl.ds(first + 12 * i, 12)], cur.at[z], sems.at[i]))
    for i in range(4):
        z = slice(12 * i, 12 * i + 12)
        copies.append(pltpu.make_async_copy(raw.at[z], raw_here.at[z], sems.at[2 + i]))
    for copy in copies:
        copy.start()
    for copy in copies[:2]:
        copy.wait()
    for xh in range(2):
        put_packs(cur[:, 16 * xh : 16 * xh + 16, :], 112 * (1 - tx), 16, turned, pack_out, 3 * xh)
    for copy in copies[2:]:
        copy.wait()
    for xb in range(4):
        put_packs(raw_here[:, 8 * xb : 8 * xb + 8, :], 120 * (1 - tx), 8, turned, raw_pack, 3 * xb)


def put_rims(top, bottom, even_out, odd_out, planes):
    odd = parity()
    even_out[planes] = jnp.where(odd, top, bottom)
    odd_out[planes] = jnp.where(odd, bottom, top)


def rims_body(est, cur_out, odd_out, even_out):
    cur_out[...] = est[pl.ds(24 * mesh_core(), 24)]
    put_rims(cur_out[:, 0:16, :], cur_out[:, 16:32, :], even_out, odd_out, slice(0, 24))
    odd_out[24:27] = jnp.zeros((3, 16, 128), F32)
    even_out[24:27] = jnp.zeros((3, 16, 128), F32)


def corners_body(pack, odd_in, even_in, odd_out, even_out):
    put_rims(pack[0:3], pack[3:6], even_out, odd_out, slice(24, 27))


def raw_rims_body(raw, pack, after, odd_out, even_out):
    put_rims(raw[:, 0:8, :], raw[:, 24:32, :], even_out, odd_out, slice(0, 48))
    for t in range(3):
        put_rims(pack[t][None], pack[9 + t][None], even_out, odd_out, slice(48 + t, 49 + t))


def shift_columns(tile, side, sy):
    lane = lax.broadcasted_iota(jnp.int32, tile.shape, 2)
    inside = (lane >= sy) & (lane < 128 + sy)
    return pltpu.roll(jnp.where(inside, tile, side), lax.rem(128 - sy, 128), 2)


def register_columns_body(offsets, raw, pack, after, out, turned):
    view, tx = lax.axis_index("view"), lax.axis_index("tx")
    sy = offsets[view, 1]
    turned[...] = jnp.zeros_like(turned)
    for b in range(4):
        parts = [pack[3 * b + t] for t in range(3)]
        side = spread_columns(parts, 120 * tx, 8, turned).reshape(48, 8, 128)
        rows = slice(8 * b, 8 * b + 8)
        out[:, rows, :] = shift_columns(raw[:, rows, :], side, sy)


def register_body(offsets, moved, from_odd, from_even, after, out, wide, turned):
    view, tx = lax.axis_index("view"), lax.axis_index("tx")
    sx, sy = offsets[view, 0], offsets[view, 1]
    odd = parity()
    above = jnp.where(odd, from_even[...], from_odd[...])
    below = jnp.where(odd, from_odd[...], from_even[...])
    turned[...] = jnp.zeros_like(turned)
    wide[:, 8:40, :] = moved[...]
    for rim, rows in ((above, slice(0, 8)), (below, slice(40, 48))):
        side = spread_columns([rim[48 + t] for t in range(3)], 120 * tx, 8, turned).reshape(48, 8, 128)
        wide[:, rows, :] = shift_columns(rim[0:48], side, sy)
    out[...] = wide[:, pl.ds(8 + sx, 32), :]


def put_columns(rows, main, rim, tx, x_h, x_l, turned):
    x_h[:, rows, 0:128], x_l[:, rows, 0:128] = split(main)
    side = spread_columns(rim, 112 * tx, 16, turned).reshape(24, 16, 128)
    x_h[:, rows, 128:256], x_l[:, rows, 128:256] = split(side)


def blur_rows(x_h, x_l, yf, bx, g):
    z = slice(4 * g, 4 * g + 4)
    high, low = x_h[z].reshape(128, 256), x_l[z].reshape(128, 256)
    along_y = split(dot(high, yf[0], NN) + (dot(high, yf[1], NN) + dot(low, yf[0], NN)))
    for v in range(2):
        cols = slice(128 * v, 128 * v + 128)
        yield v, z, rows3(bx[v][:, 0:128], (along_y[0][:, cols], along_y[1][:, cols])).reshape(4, 32, 128)


def inner_body(cur, ext, mats, own, other, x_h, x_l, turned):
    tx = lax.axis_index("tx")
    turned[...] = jnp.zeros_like(turned)
    for xh in range(2):
        rows = slice(16 * xh, 16 * xh + 16)
        put_columns(rows, cur[:, rows, :], [ext[3 * xh + t] for t in range(3)], tx, x_h, x_l, turned)
    for g in range(6):
        for v, z, part in blur_rows(x_h, x_l, (mats[YT], mats[YT + 1]), (mats[IN], mats[IN + 1]), g):
            (own, other)[v][z] = part


def fill_outer(from_odd, from_even, x_h, x_l, turned):
    tx = lax.axis_index("tx")
    odd = parity()
    above = jnp.where(odd, from_even[...], from_odd[...])
    below = jnp.where(odd, from_odd[...], from_even[...])
    turned[...] = jnp.zeros_like(turned)
    for xh, rim in ((0, above), (1, below)):
        rows = slice(16 * xh, 16 * xh + 16)
        put_columns(rows, rim[0:24], [rim[24 + t] for t in range(3)], tx, x_h, x_l, turned)


def outer_body(from_odd, from_even, mats, in_own, in_other, own, other, x_h, x_l, turned):
    fill_outer(from_odd, from_even, x_h, x_l, turned)
    for g in range(6):
        for v, z, part in blur_rows(x_h, x_l, (mats[YT], mats[YT + 1]), (mats[OUT], mats[OUT + 1]), g):
            (own, other)[v][z] = (in_own, in_other)[v][z] + part


def along_z(kz, m, high, low):
    parts = []
    for third, reach in ((0, slice(0, 256)), (1, slice(0, 384)), (2, slice(128, 384))):
        parts.append(rows3(kz[m, 256 * third : 256 * third + 256, reach], (high[reach], low[reach])))
    return jnp.concatenate(parts)


def plane_pair(ref, xp):
    return jnp.concatenate(
        [ref[:, 16 * xp + 8 * i : 16 * xp + 8 * i + 8, :].reshape(384, 128) for i in range(2)], axis=1
    )


def put_pair(ref, xp, value):
    for i in range(2):
        at = slice(16 * xp + 8 * i, 16 * xp + 8 * i + 8)
        ref[:, at, :] = value[:, 128 * i : 128 * i + 128].reshape(48, 8, 128)


def join_planes(mine, theirs, full):
    core = mesh_core()
    full[pl.ds(24 * core, 24)] = mine[...]
    full[pl.ds(24 * (1 - core), 24)] = theirs[...]


def part_planes(keep, send, full):
    core = mesh_core()
    keep[...] = full[pl.ds(24 * core, 24)]
    send[...] = full[pl.ds(24 * (1 - core), 24)]


def ratio_body(mine, theirs, seen, kz, keep, send, full):
    join_planes(mine, theirs, full)
    for xp in range(2):
        blurred = along_z(kz, 0, *split(plane_pair(full, xp)))
        ratio = plane_pair(seen, xp) / blurred
        put_pair(full, xp, along_z(kz, 1, *split(ratio)))
    part_planes(keep, send, full)


def planes_body(mine, theirs, kz, out, full):
    join_planes(mine, theirs, full)
    for xp in range(2):
        put_pair(out, xp, along_z(kz, 0, *split(plane_pair(full, xp))))


def divide_body(blurred, seen, kz, keep, send, full):
    for xp in range(2):
        ratio = plane_pair(seen, xp) / plane_pair(blurred, xp)
        put_pair(full, xp, along_z(kz, 1, *split(ratio)))
    part_planes(keep, send, full)


def put_sides(sides, tx, turned, put):
    for xh in range(2):
        cols = pack_columns(sides[:, 16 * xh : 16 * xh + 16, :], 112 * tx, 16, turned)
        for t in range(3):
            put(xh, t, cols[:, 128 * t : 128 * t + 128])


def spread_rows(band, y_h, y_l, g):
    rows = slice(128 * g, 128 * g + 128)
    both = tuple(jnp.concatenate([y[0, rows], y[1, rows]], axis=0) for y in (y_h, y_l))
    return rows3(band, both).reshape(4, 32, 256)


def mirror_rims_body(own, other, mats, odd_out, even_out, y_h, y_l, sides, turned):
    tx = lax.axis_index("tx")
    for v, ref in ((0, own), (1, other)):
        high, low = split(ref[...].reshape(768, 128))
        rows = slice(128 * v, 128 * v + 128)
        band = mats[YF, rows]
        y_h[v], y_l[v] = split(
            dot(jnp.concatenate([high, low], axis=1), jnp.concatenate([band, band]), NN)
            + dot(high, mats[YF + 1, rows], NN)
        )
    for g in range(6):
        z = slice(4 * g, 4 * g + 4)
        wide = spread_rows(mats[BT], y_h, y_l, g)
        put_rims(wide[:, 0:16, 0:128], wide[:, 16:32, 0:128], even_out, odd_out, z)
        sides[z] = wide[:, :, 128:256]
    parts = {}
    put_sides(sides, tx, turned, lambda xh, t, cols: parts.update({(xh, t): cols}))
    for t in range(3):
        put_rims(parts[0, t][None], parts[1, t][None], even_out, odd_out, slice(24 + t, 25 + t))


def mirror_body(y_h, y_l, mats, mid, mid_ext, sides, turned):
    for g in range(6):
        z = slice(4 * g, 4 * g + 4)
        wide = spread_rows(mats[BT + 1], y_h, y_l, g)
        mid[z] = wide[:, :, 0:128]
        sides[z] = wide[:, :, 128:256]

    def put(xh, t, cols):
        mid_ext[3 * xh + t] = cols

    put_sides(sides, lax.axis_index("tx"), turned, put)


def gather_body(mid, mid_ext, from_odd, from_even, after, sides_out, low_out, high_out, turned):
    tx = lax.axis_index("tx")
    odd = parity()
    above = jnp.where(odd, from_even[...], from_odd[...])
    below = jnp.where(odd, from_odd[...], from_even[...])
    for out, z in ((low_out, slice(0, 12)), (high_out, slice(12, 24))):
        out[:, 0:16, :] = mid[z, 0:16, :] + above[z]
        out[:, 16:32, :] = mid[z, 16:32, :] + below[z]
    sides_out[0:3] = mid_ext[0:3] + above[24:27]
    sides_out[3:6] = mid_ext[3:6] + below[24:27]
    if sides_out.shape[0] == 12:
        for xh in range(2):
            at = slice(16 * xh, 16 * xh + 16)
            both = jnp.concatenate([low_out[:, at, :], high_out[:, at, :]])
            put_packs(both, 112 * (1 - tx), 16, turned, sides_out, 6 + 3 * xh)


def join_body(mine, theirs, out):
    out[...] = mine[...] + theirs[...]


def new_estimate(side, low, high, p_low, p_high, cur, norm, cur_out, turned):
    tx = lax.axis_index("tx")
    turned[...] = jnp.zeros_like(turned)
    for xh in range(2):
        at = slice(16 * xh, 16 * xh + 16)
        parts = [side[3 * xh + t] for t in range(3)]
        edge = spread_columns(parts, 112 * (1 - tx), 16, turned).reshape(24, 16, 128)
        for mine, theirs, z in ((low, p_low, slice(0, 12)), (high, p_high, slice(12, 24))):
            total = mine[:, at, :] + theirs[:, at, :] + edge[z]
            cur_out[z, at, :] = cur[z, at, :] * total / norm[z, at, :]


def update_body(
    side, low, high, p_low, p_high, cur, norm, joined, ext, norm_ext, cur_out, ext_out, odd_out, even_out, turned
):
    new_estimate(side, low, high, p_low, p_high, cur, norm, cur_out, turned)
    ext_out[...] = ext[0:6] * (side[6:12] + joined[0:6]) / norm_ext[...]
    put_rims(cur_out[:, 0:16, :], cur_out[:, 16:32, :], even_out, odd_out, slice(0, 24))
    put_rims(ext_out[0:3], ext_out[3:6], even_out, odd_out, slice(24, 27))


def near_half_body(mine, out, sem):
    copy = pltpu.make_async_copy(mine, out.at[pl.ds(24 * mesh_core(), 24)], sem)
    copy.start()
    copy.wait()


def far_half_body(theirs, near, out, sem):
    copy = pltpu.make_async_copy(theirs, out.at[pl.ds(24 * (1 - mesh_core()), 24)], sem)
    copy.start()
    copy.wait()


def swap(value, axis, by, sizes):
    count = int(np.prod(sizes))
    return lax.ppermute(value, axis, [(i, i ^ by) for i in range(count)])


def rim_swap(odd, even):
    rows = lax.axis_size("ty")
    odd_pairs = [(i, i + 1) for i in range(1, rows - 1, 2)]
    odd_pairs += [(b, a) for a, b in odd_pairs]
    from_odd = lax.ppermute(odd, "ty", odd_pairs)
    from_even = lax.ppermute(even, "ty", [(i, i ^ 1) for i in range(rows)])
    return from_odd, from_even


def shards(raw_views, psf_taps, offsets, estimate):
    depth, tile_x, tile_y = estimate.shape
    half = depth // 2
    raw = raw_views[0]

    tile_half = ((half, tile_x, tile_y), F32)
    tile_quarter = ((half // 2, tile_x, tile_y), F32)
    pack = ((6, EDGE, 128), F32)
    rim = ((half + 3, EDGE, 128), F32)
    turned = pltpu.VMEM((128, 384), F32)
    two_sems = pltpu.SemaphoreType.DMA((2,))

    ext, sides = call(
        begin_body,
        [pack, ((12, OMAX, 128), F32)],
        [estimate, raw],
        [pltpu.VMEM((half, tile_x, tile_y), F32), pltpu.VMEM(raw.shape, F32), turned, pltpu.SemaphoreType.DMA((6,))],
        name="begin",
        hbm=(0, 1),
        limit=62,
    )
    ext = swap(ext, ("view", "tx"), 5, (4, 2))
    sides = swap(sides, "tx", 1, (2,))
    cur, odd, even = call(rims_body, [tile_half, rim, rim], [estimate], name="rims")

    odd, even = call(corners_body, [rim, rim], [ext, odd, even], name="corners", aliases={1: 0, 2: 1})
    late_taps, late_offsets, _ = lax.optimization_barrier((psf_taps, offsets, odd))
    taps = jnp.pad(late_taps.reshape(-1, TAPS), ((0, 4), (0, 1)))
    flat_psf = late_taps.reshape(-1)
    kz, mats = bands(taps, depth, flat_psf, late_offsets)
    extents = (tile_x * lax.axis_size("ty"), tile_y * lax.axis_size("tx"))
    from_odd, from_even = rim_swap(odd, even)
    raw_rim = ((depth + 3, OMAX, 128), F32)
    raw_odd, raw_even = call(raw_rims_body, [raw_rim, raw_rim], [raw, sides, taps], name="raw_rims")
    raw_from = rim_swap(raw_odd, raw_even)
    columns = [pltpu.VMEM((half, 32, 256), BF16), pltpu.VMEM((half, 32, 256), BF16), turned]
    seen = None

    for iteration in range(ITERS):
        inner = call(
            inner_body, [tile_half, tile_half], [cur, ext, mats], columns, flops=BUSY, name="inner"
        )
        mine, theirs = call(
            outer_body,
            [tile_half, tile_half],
            [from_odd, from_even, mats, *inner],
            columns,
            flops=BUSY,
            name="outer",
        )
        theirs = swap(theirs, "view", 1, (4,))
        if seen is None:
            whole = ((depth, tile_x, tile_y), F32)
            (blurred,) = call(
                planes_body,
                [whole],
                [mine, theirs, kz],
                [pltpu.VMEM((depth, tile_x, tile_y), F32)],
                flops=BUSY,
                name="planes",
            )
            (moved,) = call(
                register_columns_body,
                [whole],
                [late_offsets, raw, sides, mine],
                [turned],
                flops=BUSY,
                name="register_columns",
            )
            (seen,) = call(
                register_body,
                [whole],
                [late_offsets, moved, *raw_from, blurred],
                [pltpu.VMEM((depth, tile_x + 2 * OMAX, 128), F32), turned],
                flops=BUSY,
                name="register",
            )
        first = iteration == 0
        keep, send = call(
            divide_body if first else ratio_body,
            [tile_half, tile_half],
            [blurred, seen, kz] if first else [mine, theirs, seen, kz],
            [pltpu.VMEM((depth, tile_x, tile_y), F32)],
            flops=3 * 2 * 2 * 384 * 384 * 512,
            name="ratio",
        )
        send = swap(send, "view", 1, (4,))
        along_y = ((2, 768, 256), BF16)
        odd, even, y_h, y_l = call(
            mirror_rims_body,
            [rim, rim, along_y, along_y],
            [keep, send, mats],
            [pltpu.VMEM((half, 32, 128), F32), turned],
            name="mirror_rims",
        )
        mid, mid_ext = call(
            mirror_body,
            [tile_half, pack],
            [y_h, y_l, mats],
            [pltpu.VMEM((half, 32, 128), F32), turned],
            flops=BUSY,
            name="mirror",
        )
        if iteration == 0:
            norm, norm_ext = call(
                functools.partial(norm_body, extents), [tile_half, pack], [flat_psf, late_offsets, y_h], name="norm"
            )
        from_odd, from_even = rim_swap(odd, even)
        last = iteration == ITERS - 1
        sides, low, high = call(
            gather_body,
            [pack if last else ((12, EDGE, 128), F32), tile_quarter, tile_quarter],
            [mid, mid_ext, from_odd, from_even, norm],
            [turned],
            name="gather",
        )
        theirs = swap(sides, "view", 2, (4,))
        p_low = swap(low, "view", 2, (4,))
        p_high = swap(high, "view", 2, (4,))
        (joined,) = call(join_body, [(sides.shape, F32)], [sides, theirs], flops=BUSY, name="join")
        side = swap(joined, ("view", "tx"), 5, (4, 2))
        if last:
            (cur,) = call(new_estimate, [tile_half], [side, low, high, p_low, p_high, cur, norm], [turned], name="last")
            break
        cur, ext, odd, even = call(
            update_body,
            [tile_half, pack, rim, rim],
            [side, low, high, p_low, p_high, cur, norm, joined, ext, norm_ext],
            [turned],
            name="update",
        )
        from_odd, from_even = rim_swap(odd, even)
    far = swap(cur, "view", 1, (4,))
    outs, sem = [((depth, tile_x, tile_y), F32)], [pltpu.SemaphoreType.DMA]
    (near,) = call(near_half_body, outs, [cur], sem, flops=BUSY, name="near_half", out_place=pl.ANY)
    (out,) = call(far_half_body, outs, [far, near], sem, name="far_half", hbm=(1,), aliases={1: 0}, out_place=pl.ANY)
    return out


def solution(mesh):
    placed = (P("view", None, "ty", "tx"), P(), P(), P(None, "ty", "tx"))
    return jax.shard_map(
        shards, mesh=mesh, in_specs=placed, out_specs=P(None, "ty", "tx"), check_vma=False
    )
```

```python
import functools

import jax
import jax.numpy as jnp
import numpy as np
from jax import lax
from jax.experimental import pallas as pl
from jax.experimental.pallas import tpu as pltpu
from jax.sharding import PartitionSpec as P

OMAX = 8
ITERS = 2
TAPS = 31
HALF = 15
EDGE = 16
F32 = jnp.float32
BUSY = 6000000000
BF16 = jnp.bfloat16
highest = lax.Precision.HIGHEST

NN = (((1,), (0,)), ((), ()))


def split(value):
    high = value.astype(BF16)
    low = (value - high.astype(F32)).astype(BF16)
    return high, low


def dot(a, b, dims):
    return lax.dot_general(a, b, dims, preferred_element_type=F32)


def rows3(a, b):
    n = a.shape[0] // 2
    both = dot(a, b[0], NN)
    return both[:n] + (dot(a[:n], b[1], NN) + both[n:])


def call(body, outs, args, scratch=(), flops=0, name=None, hbm=(), limit=8, aliases=None, out_place=pltpu.VMEM):
    def place(i, a):
        if i in hbm:
            return pltpu.HBM
        return pltpu.SMEM if a.ndim == 1 or a.dtype == jnp.int32 else pltpu.VMEM

    specs = [pl.BlockSpec(memory_space=place(i, a)) for i, a in enumerate(args)]
    outs = [jax.ShapeDtypeStruct(*o) for o in outs]
    moved = sum(int(np.prod(a.shape)) * a.dtype.itemsize for a in list(args) + outs)
    return pl.pallas_call(
        body,
        out_shape=outs,
        in_specs=specs,
        out_specs=[pl.BlockSpec(memory_space=out_place)] * len(outs),
        scratch_shapes=list(scratch),
        input_output_aliases=aliases or {},
        compiler_params=pltpu.CompilerParams(vmem_limit_bytes=limit << 20),
        cost_estimate=pl.CostEstimate(flops=flops, bytes_accessed=moved, transcendentals=0),
        name=name,
    )(*args)


def toeplitz(row, rows, width, shift):
    wide = jnp.broadcast_to(row[:, :width], (rows, width))
    return pltpu.roll(wide, shift % width, 1, stride=1, stride_axis=0)


MATS = 10
YF, IN, OUT, BT, YT = 0, 2, 4, 6, 8


def bands_body(taps, place, psf, offsets, kz, mats, placed):
    view = lax.axis_index("view")
    views = (view, view + 1 - 2 * (view % 2))
    total = jnp.sum(taps[...], axis=1, keepdims=True)
    rest = taps[...] / jnp.where(total > 0, total, 1.0)
    placed[...] = jnp.zeros_like(placed)
    for _ in range(3):
        part = rest.astype(BF16)
        placed[...] += dot(part, place[...], NN)
        rest = rest - part.astype(F32)

    def row(v, dim, kind):
        return placed[pl.ds(3 * views[v] + dim, 1), 512 * kind : 512 * kind + 512]

    for m in range(2):
        high, low = split(toeplitz(row(0, 0, m), 384, 512, 0)[:, :384])
        for third in range(3):
            rows = slice(128 * third, 128 * third + 128)
            kz[m, 256 * third : 256 * third + 128] = high[rows]
            kz[m, 256 * third + 128 : 256 * third + 256] = low[rows]
    lane = lax.broadcasted_iota(jnp.int32, (64, 256), 1)

    def between(band, first, count, rest):
        at = lane[: band.shape[0]]
        return jnp.where((at >= first) & (at < first + count), band, rest)

    for v in range(2):
        taps_x = row(v, 1, 2)
        for p in range(4):
            at = 32 * p
            none = jnp.zeros((32, 256), F32)
            inner = between(toeplitz(taps_x, 32, 256, at - HALF), at, 32, none)
            outer = between(toeplitz(taps_x, 32, 256, at + 1), at, 16, none)
            outer = between(toeplitz(taps_x, 32, 256, at - 2 * HALF - 1), at + 16, 16, outer)
            for m, band in ((IN + v, inner), (OUT + v, outer)):
                mats[m, at : at + 32], mats[m, 128 + at : 160 + at] = split(band)
        rows = slice(128 * v, 128 * v + 128)
        mats[0, rows], mats[1, rows] = split(toeplitz(row(v, 2, 2), 128, 256, -HALF))
        mats[YT, :, rows], mats[YT + 1, :, rows] = split(toeplitz(row(v, 2, 3), 256, 256, -HALF)[:, :128])
    for p in range(4):
        both = jnp.zeros((64, 256), F32)
        for v in range(2):
            at = 128 * v + 32 * p
            both = between(toeplitz(row(v, 1, 3), 64, 256, at - 2 * HALF - 1), at, 32, both)
        rims, at = jnp.concatenate([both[0:16], both[48:64]]), 32 * p
        mats[BT, at : at + 32], mats[BT, 128 + at : 160 + at] = split(rims)
        mats[BT + 1, at : at + 32], mats[BT + 1, 128 + at : 160 + at] = split(both[16:48])


def placing():
    place = np.zeros((TAPS + 1, 4, 512), np.float32)
    for k in range(TAPS):
        for kind, at in enumerate((8 * (k - HALF), 8 * (HALF - k), k, TAPS - 1 - k)):
            place[k, kind, at % 512] = 1
    return jnp.asarray(place.reshape(TAPS + 1, 2048), BF16)


def bands(taps, planes, psf, offsets):
    nz = 8 * planes
    return call(
        bands_body,
        [((2, 2 * nz, nz), BF16), ((MATS, 256, 256), BF16)],
        [taps, placing(), psf, offsets],
        [pltpu.VMEM((16, 2048), F32)],
        flops=BUSY,
        name="bands",
    )


def pack_columns(value, at, width, scratch):
    flat = value.reshape(value.shape[0] * value.shape[1], 128)
    scratch[...] = flat.T
    return scratch[pl.ds(pl.multiple_of(at, 8), width), :]


def spread_columns(pack, at, width, scratch):
    for t, part in enumerate(pack):
        scratch[pl.ds(pl.multiple_of(at, 8), width), 128 * t : 128 * t + 128] = part
    return scratch[...].T


def norm_body(shape, psf, offsets, after, norm, norm_ext):
    nx, ny = shape
    views = offsets.shape[0]
    core = lax.axis_index("view") % 2
    x_first = 32 * lax.axis_index("ty")
    tx = lax.axis_index("tx")

    def iota(shape, dim):
        return lax.broadcasted_iota(jnp.int32, shape, dim)

    lane = iota((8, 128), 1)
    tile = jnp.minimum(iota((8, 128), 0), 2)
    places = (
        (0, 24 * core + iota((24, 128), 0)),
        (0, 24 * core + (128 * tile + lane) // EDGE),
        (1, x_first + iota((32, 128), 0)),
        (1, x_first + EDGE * (iota((8, 128), 0) % 2) + lane % EDGE),
        (2, 128 * tx + lane),
        (2, 128 - EDGE * tx + iota((EDGE, 128), 0)),
    )
    extents = (48, nx, ny)
    norm[...] = jnp.zeros_like(norm)
    norm_ext[...] = jnp.zeros_like(norm_ext)

    def one_view(v, _):
        shifts = (0, offsets[v, 0], offsets[v, 1])

        def one_tap(i, carry):
            totals, weights = carry
            taps = [psf[(v * 3 + dim) * TAPS + TAPS - 1 - i] for dim in range(3)]
            new = []
            for (dim, place), total in zip(places, totals):
                at = place + (i - HALF)
                moved = at + shifts[dim]
                inside = (at >= 0) & (at < extents[dim]) & (moved >= 0) & (moved < extents[dim])
                new.append(total + jnp.where(inside, taps[dim], 0.0))
            return tuple(new), tuple(w + t for w, t in zip(weights, taps))

        none = tuple(jnp.zeros(place.shape, F32) for _, place in places)
        totals, weights = lax.fori_loop(0, TAPS, one_tap, (none, (0.0, 0.0, 0.0)))
        in_z, z_row, in_x, x_row, in_y, in_e = (t / weights[dim] for t, (dim, _) in zip(totals, places))
        xy = in_x * in_y[0:1]
        for z in range(24):
            norm[z] += in_z[z : z + 1] * xy
        for k in range(6):
            norm_ext[k] += in_e * (z_row[k % 3 : k % 3 + 1] * x_row[k // 3 : k // 3 + 1])
        return 0

    lax.fori_loop(0, offsets.shape[0], one_view, 0)


def mesh_core():
    return lax.axis_index("view") % 2


def parity():
    return lax.axis_index("ty") % 2 == 1


def put_packs(value, at, width, turned, out, first):
    cols = pack_columns(value, at, width, turned)
    for t in range(3):
        out[first + t] = cols[:, 128 * t : 128 * t + 128]


def begin_body(est, pack_out, turned):
    tx = lax.axis_index("tx")
    half = pl.ds(24 * mesh_core(), 24)
    for xh in range(2):
        put_packs(est[half, 16 * xh : 16 * xh + 16, :], 112 * (1 - tx), 16, turned, pack_out, 3 * xh)


def raw_sides_body(raw, pack_out, turned):
    tx = lax.axis_index("tx")
    for xb in range(4):
        put_packs(raw[:, 8 * xb : 8 * xb + 8, :], 120 * (1 - tx), 8, turned, pack_out, 3 * xb)


def put_rims(top, bottom, even_out, odd_out, planes):
    odd = parity()
    even_out[planes] = jnp.where(odd, top, bottom)
    odd_out[planes] = jnp.where(odd, bottom, top)


def rims_body(est, cur_out, odd_out, even_out):
    cur_out[...] = est[pl.ds(24 * mesh_core(), 24)]
    put_rims(cur_out[:, 0:16, :], cur_out[:, 16:32, :], even_out, odd_out, slice(0, 24))
    odd_out[24:27] = jnp.zeros((3, 16, 128), F32)
    even_out[24:27] = jnp.zeros((3, 16, 128), F32)


def corners_body(pack, odd_in, even_in, odd_out, even_out):
    put_rims(pack[0:3], pack[3:6], even_out, odd_out, slice(24, 27))


def raw_rims_body(raw, pack, after, odd_out, even_out):
    put_rims(raw[:, 0:8, :], raw[:, 24:32, :], even_out, odd_out, slice(0, 48))
    for t in range(3):
        put_rims(pack[t][None], pack[9 + t][None], even_out, odd_out, slice(48 + t, 49 + t))


def shift_columns(tile, side, sy):
    lane = lax.broadcasted_iota(jnp.int32, tile.shape, 2)
    inside = (lane >= sy) & (lane < 128 + sy)
    return pltpu.roll(jnp.where(inside, tile, side), lax.rem(128 - sy, 128), 2)


def register_columns_body(offsets, raw, pack, after, out, turned):
    view, tx = lax.axis_index("view"), lax.axis_index("tx")
    sy = offsets[view, 1]
    turned[...] = jnp.zeros_like(turned)
    for b in range(4):
        parts = [pack[3 * b + t] for t in range(3)]
        side = spread_columns(parts, 120 * tx, 8, turned).reshape(48, 8, 128)
        rows = slice(8 * b, 8 * b + 8)
        out[:, rows, :] = shift_columns(raw[:, rows, :], side, sy)


def register_body(offsets, moved, from_odd, from_even, after, out, wide, turned):
    view, tx = lax.axis_index("view"), lax.axis_index("tx")
    sx, sy = offsets[view, 0], offsets[view, 1]
    odd = parity()
    above = jnp.where(odd, from_even[...], from_odd[...])
    below = jnp.where(odd, from_odd[...], from_even[...])
    turned[...] = jnp.zeros_like(turned)
    wide[:, 8:40, :] = moved[...]
    for rim, rows in ((above, slice(0, 8)), (below, slice(40, 48))):
        side = spread_columns([rim[48 + t] for t in range(3)], 120 * tx, 8, turned).reshape(48, 8, 128)
        wide[:, rows, :] = shift_columns(rim[0:48], side, sy)
    out[...] = wide[:, pl.ds(8 + sx, 32), :]


def put_columns(rows, main, rim, tx, x_h, x_l, turned):
    x_h[:, rows, 0:128], x_l[:, rows, 0:128] = split(main)
    side = spread_columns(rim, 112 * tx, 16, turned).reshape(24, 16, 128)
    x_h[:, rows, 128:256], x_l[:, rows, 128:256] = split(side)


def blur_rows(x_h, x_l, yf, bx, g):
    z = slice(4 * g, 4 * g + 4)
    high, low = x_h[z].reshape(128, 256), x_l[z].reshape(128, 256)
    along_y = split(dot(high, yf[0], NN) + (dot(high, yf[1], NN) + dot(low, yf[0], NN)))
    for v in range(2):
        cols = slice(128 * v, 128 * v + 128)
        yield v, z, rows3(bx[v][:, 0:128], (along_y[0][:, cols], along_y[1][:, cols])).reshape(4, 32, 128)


def inner_body(cur, ext, mats, own, other, x_h, x_l, turned):
    tx = lax.axis_index("tx")
    turned[...] = jnp.zeros_like(turned)
    for xh in range(2):
        rows = slice(16 * xh, 16 * xh + 16)
        put_columns(rows, cur[:, rows, :], [ext[3 * xh + t] for t in range(3)], tx, x_h, x_l, turned)
    for g in range(6):
        for v, z, part in blur_rows(x_h, x_l, (mats[YT], mats[YT + 1]), (mats[IN], mats[IN + 1]), g):
            (own, other)[v][z] = part


def fill_outer(from_odd, from_even, x_h, x_l, turned):
    tx = lax.axis_index("tx")
    odd = parity()
    above = jnp.where(odd, from_even[...], from_odd[...])
    below = jnp.where(odd, from_odd[...], from_even[...])
    turned[...] = jnp.zeros_like(turned)
    for xh, rim in ((0, above), (1, below)):
        rows = slice(16 * xh, 16 * xh + 16)
        put_columns(rows, rim[0:24], [rim[24 + t] for t in range(3)], tx, x_h, x_l, turned)


def outer_body(from_odd, from_even, mats, in_own, in_other, own, other, x_h, x_l, turned):
    fill_outer(from_odd, from_even, x_h, x_l, turned)
    for g in range(6):
        for v, z, part in blur_rows(x_h, x_l, (mats[YT], mats[YT + 1]), (mats[OUT], mats[OUT + 1]), g):
            (own, other)[v][z] = (in_own, in_other)[v][z] + part


def along_z(kz, m, high, low):
    parts = []
    for third, reach in ((0, slice(0, 256)), (1, slice(0, 384)), (2, slice(128, 384))):
        parts.append(rows3(kz[m, 256 * third : 256 * third + 256, reach], (high[reach], low[reach])))
    return jnp.concatenate(parts)


def plane_pair(ref, xp):
    return jnp.concatenate(
        [ref[:, 16 * xp + 8 * i : 16 * xp + 8 * i + 8, :].reshape(384, 128) for i in range(2)], axis=1
    )


def put_pair(ref, xp, value):
    for i in range(2):
        at = slice(16 * xp + 8 * i, 16 * xp + 8 * i + 8)
        ref[:, at, :] = value[:, 128 * i : 128 * i + 128].reshape(48, 8, 128)


def join_planes(mine, theirs, full):
    core = mesh_core()
    full[pl.ds(24 * core, 24)] = mine[...]
    full[pl.ds(24 * (1 - core), 24)] = theirs[...]


def part_planes(keep, send, full):
    core = mesh_core()
    keep[...] = full[pl.ds(24 * core, 24)]
    send[...] = full[pl.ds(24 * (1 - core), 24)]


def ratio_body(mine, theirs, seen, kz, keep, send, full):
    join_planes(mine, theirs, full)
    for xp in range(2):
        blurred = along_z(kz, 0, *split(plane_pair(full, xp)))
        ratio = plane_pair(seen, xp) / blurred
        put_pair(full, xp, along_z(kz, 1, *split(ratio)))
    part_planes(keep, send, full)


def planes_body(mine, theirs, kz, out, full):
    join_planes(mine, theirs, full)
    for xp in range(2):
        put_pair(out, xp, along_z(kz, 0, *split(plane_pair(full, xp))))


def divide_body(blurred, seen, kz, keep, send, full):
    for xp in range(2):
        ratio = plane_pair(seen, xp) / plane_pair(blurred, xp)
        put_pair(full, xp, along_z(kz, 1, *split(ratio)))
    part_planes(keep, send, full)


def put_sides(sides, tx, turned, put):
    for xh in range(2):
        cols = pack_columns(sides[:, 16 * xh : 16 * xh + 16, :], 112 * tx, 16, turned)
        for t in range(3):
            put(xh, t, cols[:, 128 * t : 128 * t + 128])


def spread_rows(band, y_h, y_l, g):
    rows = slice(128 * g, 128 * g + 128)
    both = tuple(jnp.concatenate([y[0, rows], y[1, rows]], axis=0) for y in (y_h, y_l))
    return rows3(band, both).reshape(4, 32, 256)


def mirror_rims_body(own, other, mats, odd_out, even_out, y_h, y_l, sides, turned):
    tx = lax.axis_index("tx")
    for v, ref in ((0, own), (1, other)):
        high, low = split(ref[...].reshape(768, 128))
        rows = slice(128 * v, 128 * v + 128)
        band = mats[YF, rows]
        y_h[v], y_l[v] = split(
            dot(jnp.concatenate([high, low], axis=1), jnp.concatenate([band, band]), NN)
            + dot(high, mats[YF + 1, rows], NN)
        )
    for g in range(6):
        z = slice(4 * g, 4 * g + 4)
        wide = spread_rows(mats[BT], y_h, y_l, g)
        put_rims(wide[:, 0:16, 0:128], wide[:, 16:32, 0:128], even_out, odd_out, z)
        sides[z] = wide[:, :, 128:256]
    parts = {}
    put_sides(sides, tx, turned, lambda xh, t, cols: parts.update({(xh, t): cols}))
    for t in range(3):
        put_rims(parts[0, t][None], parts[1, t][None], even_out, odd_out, slice(24 + t, 25 + t))


def mirror_body(y_h, y_l, mats, mid, mid_ext, sides, turned):
    for g in range(6):
        z = slice(4 * g, 4 * g + 4)
        wide = spread_rows(mats[BT + 1], y_h, y_l, g)
        mid[z] = wide[:, :, 0:128]
        sides[z] = wide[:, :, 128:256]

    def put(xh, t, cols):
        mid_ext[3 * xh + t] = cols

    put_sides(sides, lax.axis_index("tx"), turned, put)


def gather_body(mid, mid_ext, from_odd, from_even, after, sides_out, out, turned):
    tx = lax.axis_index("tx")
    odd = parity()
    above = jnp.where(odd, from_even[...], from_odd[...])
    below = jnp.where(odd, from_odd[...], from_even[...])
    out[:, 0:16, :] = mid[:, 0:16, :] + above[0:24]
    out[:, 16:32, :] = mid[:, 16:32, :] + below[0:24]
    sides_out[0:3] = mid_ext[0:3] + above[24:27]
    sides_out[3:6] = mid_ext[3:6] + below[24:27]
    if sides_out.shape[0] == 12:
        for xh in range(2):
            at = slice(16 * xh, 16 * xh + 16)
            put_packs(out[:, at, :], 112 * (1 - tx), 16, turned, sides_out, 6 + 3 * xh)


def join_body(mine, theirs, out):
    out[...] = mine[...] + theirs[...]


def new_estimate(side, mine, theirs, cur, norm, cur_out, turned):
    tx = lax.axis_index("tx")
    turned[...] = jnp.zeros_like(turned)
    for xh in range(2):
        at = slice(16 * xh, 16 * xh + 16)
        parts = [side[3 * xh + t] for t in range(3)]
        edge = spread_columns(parts, 112 * (1 - tx), 16, turned).reshape(24, 16, 128)
        total = mine[:, at, :] + theirs[:, at, :] + edge
        cur_out[:, at, :] = cur[:, at, :] * total / norm[:, at, :]


def update_body(
    side, mine, theirs, cur, norm, joined, ext, norm_ext, cur_out, ext_out, odd_out, even_out, turned
):
    new_estimate(side, mine, theirs, cur, norm, cur_out, turned)
    ext_out[...] = ext[0:6] * (side[6:12] + joined[0:6]) / norm_ext[...]
    put_rims(cur_out[:, 0:16, :], cur_out[:, 16:32, :], even_out, odd_out, slice(0, 24))
    put_rims(ext_out[0:3], ext_out[3:6], even_out, odd_out, slice(24, 27))


def near_half_body(mine, out, sem):
    copy = pltpu.make_async_copy(mine, out.at[pl.ds(24 * mesh_core(), 24)], sem)
    copy.start()
    copy.wait()


def far_half_body(theirs, near, out, sem):
    copy = pltpu.make_async_copy(theirs, out.at[pl.ds(24 * (1 - mesh_core()), 24)], sem)
    copy.start()
    copy.wait()


def swap(value, axis, by, sizes):
    count = int(np.prod(sizes))
    return lax.ppermute(value, axis, [(i, i ^ by) for i in range(count)])


def rim_swap(odd, even):
    rows = lax.axis_size("ty")
    odd_pairs = [(i, i + 1) for i in range(1, rows - 1, 2)]
    odd_pairs += [(b, a) for a, b in odd_pairs]
    from_odd = lax.ppermute(odd, "ty", odd_pairs)
    from_even = lax.ppermute(even, "ty", [(i, i ^ 1) for i in range(rows)])
    return from_odd, from_even


def shards(raw_views, psf_taps, offsets, estimate):
    depth, tile_x, tile_y = estimate.shape
    half = depth // 2
    raw = raw_views[0]

    tile_half = ((half, tile_x, tile_y), F32)
    pack = ((6, EDGE, 128), F32)
    rim = ((half + 3, EDGE, 128), F32)
    turned = pltpu.VMEM((128, 384), F32)
    two_sems = pltpu.SemaphoreType.DMA((2,))

    (ext,) = call(begin_body, [pack], [estimate], [turned], name="begin")
    ext = swap(ext, ("view", "tx"), 5, (4, 2))
    (sides,) = call(raw_sides_body, [((12, OMAX, 128), F32)], [raw], [turned], flops=BUSY, name="raw_sides")
    sides = swap(sides, "tx", 1, (2,))
    cur, odd, even = call(rims_body, [tile_half, rim, rim], [estimate], name="rims")

    odd, even = call(corners_body, [rim, rim], [ext, odd, even], name="corners", aliases={1: 0, 2: 1})
    late_taps, late_offsets, _ = lax.optimization_barrier((psf_taps, offsets, odd))
    taps = jnp.pad(late_taps.reshape(-1, TAPS), ((0, 4), (0, 1)))
    flat_psf = late_taps.reshape(-1)
    kz, mats = bands(taps, depth, flat_psf, late_offsets)
    extents = (tile_x * lax.axis_size("ty"), tile_y * lax.axis_size("tx"))
    from_odd, from_even = rim_swap(odd, even)
    raw_rim = ((depth + 3, OMAX, 128), F32)
    raw_odd, raw_even = call(raw_rims_body, [raw_rim, raw_rim], [raw, sides, taps], name="raw_rims")
    raw_from = rim_swap(raw_odd, raw_even)
    columns = [pltpu.VMEM((half, 32, 256), BF16), pltpu.VMEM((half, 32, 256), BF16), turned]
    seen = None

    for iteration in range(ITERS):
        inner = call(
            inner_body, [tile_half, tile_half], [cur, ext, mats], columns, flops=BUSY, name="inner"
        )
        mine, theirs = call(
            outer_body,
            [tile_half, tile_half],
            [from_odd, from_even, mats, *inner],
            columns,
            flops=BUSY,
            name="outer",
        )
        theirs = swap(theirs, "view", 1, (4,))
        if seen is None:
            whole = ((depth, tile_x, tile_y), F32)
            (blurred,) = call(
                planes_body,
                [whole],
                [mine, theirs, kz],
                [pltpu.VMEM((depth, tile_x, tile_y), F32)],
                flops=BUSY,
                name="planes",
            )
            (moved,) = call(
                register_columns_body,
                [whole],
                [late_offsets, raw, sides, mine],
                [turned],
                flops=BUSY,
                name="register_columns",
            )
            (seen,) = call(
                register_body,
                [whole],
                [late_offsets, moved, *raw_from, blurred],
                [pltpu.VMEM((depth, tile_x + 2 * OMAX, 128), F32), turned],
                flops=BUSY,
                name="register",
            )
        first = iteration == 0
        keep, send = call(
            divide_body if first else ratio_body,
            [tile_half, tile_half],
            [blurred, seen, kz] if first else [mine, theirs, seen, kz],
            [pltpu.VMEM((depth, tile_x, tile_y), F32)],
            flops=3 * 2 * 2 * 384 * 384 * 512,
            name="ratio",
        )
        send = swap(send, "view", 1, (4,))
        along_y = ((2, 768, 256), BF16)
        odd, even, y_h, y_l = call(
            mirror_rims_body,
            [rim, rim, along_y, along_y],
            [keep, send, mats],
            [pltpu.VMEM((half, 32, 128), F32), turned],
            name="mirror_rims",
        )
        mid, mid_ext = call(
            mirror_body,
            [tile_half, pack],
            [y_h, y_l, mats],
            [pltpu.VMEM((half, 32, 128), F32), turned],
            flops=BUSY,
            name="mirror",
        )
        if iteration == 0:
            norm, norm_ext = call(
                functools.partial(norm_body, extents), [tile_half, pack], [flat_psf, late_offsets, y_h], name="norm"
            )
        from_odd, from_even = rim_swap(odd, even)
        last = iteration == ITERS - 1
        sides, summed = call(
            gather_body,
            [pack if last else ((12, EDGE, 128), F32), tile_half],
            [mid, mid_ext, from_odd, from_even, norm],
            [turned],
            name="gather",
        )
        theirs = swap(sides, "view", 2, (4,))
        partner = swap(summed, "view", 2, (4,))
        (joined,) = call(join_body, [(sides.shape, F32)], [sides, theirs], flops=BUSY, name="join")
        side = swap(joined, ("view", "tx"), 5, (4, 2))
        if last:
            (cur,) = call(new_estimate, [tile_half], [side, summed, partner, cur, norm], [turned], name="last")
            break
        cur, ext, odd, even = call(
            update_body,
            [tile_half, pack, rim, rim],
            [side, summed, partner, cur, norm, joined, ext, norm_ext],
            [turned],
            name="update",
        )
        from_odd, from_even = rim_swap(odd, even)
    far = swap(cur, "view", 1, (4,))
    outs, sem = [((depth, tile_x, tile_y), F32)], [pltpu.SemaphoreType.DMA]
    (near,) = call(near_half_body, outs, [cur], sem, flops=BUSY, name="near_half", out_place=pl.ANY)
    (out,) = call(far_half_body, outs, [far, near], sem, name="far_half", hbm=(1,), aliases={1: 0}, out_place=pl.ANY)
    return out


def solution(mesh):
    placed = (P("view", None, "ty", "tx"), P(), P(), P(None, "ty", "tx"))
    return jax.shard_map(
        shards, mesh=mesh, in_specs=placed, out_specs=P(None, "ty", "tx"), check_vma=False
    )
```
